32 devices in a mesh: fsdp: 4 (over z), ctx: 4 (over y, x), tp: 2 (over core).
Axes of the slice: x: 2, y: 2, z: 4, core: 2. Of those that a mesh axis runs over, the one named last changes fastest.
Arguments:
- hidden_in: bfloat16 [4, 2048, 2048], P('fsdp', 'ctx'), may hold values from -6 to 6
- out_grad: bfloat16 [4, 2048, 2048], P('fsdp', 'ctx'), may hold values from -8 to 8
- ln_gain: bfloat16 [2048], replicated, may hold values from 0.5 to 1.5
- ln_bias: bfloat16 [2048], replicated, may hold values from -1.25 to 1.25
- w_qkv: bfloat16 [2048, 6144], P('fsdp', 'tp'), may hold values from -0.125 to 0.125
- b_qkv: bfloat16 [6144], P('tp'), may hold values from -1.75 to 1.75
- w_dense: bfloat16 [2048, 2048], P('fsdp', 'tp'), may hold values from -0.5 to 0.5
- b_dense: bfloat16 [2048], replicated, may hold values from -1.25 to 1.25
- w_fc1: bfloat16 [2048, 8192], P('fsdp', 'tp'), may hold values from -0.125 to 0.125
- b_fc1: bfloat16 [8192], P('tp'), may hold values from -1.75 to 1.75
- w_fc2: bfloat16 [2048, 8192], P('fsdp', 'tp'), may hold values from -0.125 to 0.125
- b_fc2: bfloat16 [2048], replicated, may hold values from -1.25 to 1.25
- lengths: int32 [4, 4], P('fsdp'), may hold values from 1 to 1024, 2048 in all within a row
- assignment: int32 [4, 2048], P('fsdp'), may hold values from 0 to 2047, each once within a row
Outputs:
- hidden_out: bfloat16 [4, 2048, 2048], P('fsdp', 'ctx')
- input_grad: float32 [4, 2048, 2048], P('fsdp', 'ctx')
- ln_gain_grad: float32 [2048], replicated
- ln_bias_grad: float32 [2048], replicated
- qkv_weight_grad: float32 [2048, 6144], P(('fsdp', 'ctx'), 'tp')
- qkv_bias_grad: float32 [6144], P('tp')
- dense_weight_grad: float32 [2048, 2048], P(('fsdp', 'ctx'), 'tp')
- dense_bias_grad: float32 [2048], replicated
- fc1_weight_grad: float32 [2048, 8192], P(('fsdp', 'ctx'), 'tp')
- fc1_bias_grad: float32 [8192], P('tp')
- fc2_weight_grad: float32 [2048, 8192], P(('fsdp', 'ctx'), 'tp')
- fc2_bias_grad: float32 [2048], replicated
The draws below stay inside these ranges and needn't reach their ends.
Inputs may be any that keep to these rules, and one draw needn't show every extreme that they name: `lengths`: each row sums to 2048 and its largest entry is 1024. `assignment`: each row holds every number from 0 to 2047 once.
All inputs are finite; a program needn't handle non-finite values.
Results may differ from the reference program's by a relative error of at most 0.0074.
Values may be sent and summed in bfloat16 or wider, within the bound.
No kernel may reach another device: no remote copies, remote signals or barrier semaphores. Data moves between devices by JAX's collectives and lax.ppermute only.
A program may use at most 384 MiB of HBM per device.

```python
import math
import jax
import jax.numpy as jnp
import numpy as np
from jax import lax

D = 2048
HEADS = 32
HEAD = 64
ROT = 32
FF = 8192
GROUPS = 4
GROUP_TOK = 2048
MAXLEN = 1024
NSEQ = 4


def with_spikes(array, rng, source, target, parts, factor):
    owner, partner = [(jnp.arange(array.shape[dim]) // (array.shape[dim] // parts)).reshape([-1 if axis == dim else 1 for axis in range(array.ndim)]) for dim in (source, target)]
    chosen = jax.random.permutation(rng, parts)[partner]
    strong = (owner == chosen) | (owner == (partner + parts // 2) % parts)
    return jnp.where(strong, factor * array, array)


def level_of(key, shape, split, least, largest):
    factor_of = 1.0
    for axis_at, blocks in split:
        draws = jax.random.uniform(jax.random.fold_in(jax.random.fold_in(key, 6), axis_at), (blocks,), jnp.float32, least / len(split), largest / len(split))
        factor_of = factor_of * jnp.repeat(jnp.exp(draws), shape[axis_at] // blocks).reshape((-1,) + (1,) * (len(shape) - 1 - axis_at))
    return factor_of


def profile(amount, total, limit, lean):
    weights = [(1 << 20) // math.isqrt(grade ** lean) + 1 for grade in range(2, amount + 1)]
    surplus, holding = total - limit - (amount - 1), [1] * (amount - 1)
    while surplus > 0:
        free = [i for i in range(amount - 1) if holding[i] < limit]
        mass, left = sum([weights[i] for i in free]), surplus
        for i in free:
            addition = min(limit - holding[i], max(1, left * weights[i] // mass), surplus)
            holding[i] = holding[i] + addition
            surplus = surplus - addition
    return np.array([limit] + holding)


def uneven_parts(own_key, number_of, total, reach, skew):
    if number_of == 2:
        one = jax.random.randint(own_key, (), max(1, total - reach), min(reach, total - 1) + 1)
        return jnp.stack([one, total - one])
    tallies = jnp.asarray(profile(number_of, total, reach, skew), jnp.int32)
    pairs = (number_of - 1) // 2
    giver, sink = tallies[1:1 + 2 * pairs:2], tallies[2:2 + 2 * pairs:2]
    slack = jnp.minimum(giver - 1, reach - sink)
    moved = jax.random.randint(jax.random.fold_in(own_key, 1), (pairs,), 0, 1 << 20) % (slack + 1)
    tallies = tallies.at[1:1 + 2 * pairs:2].set(giver - moved).at[2:2 + 2 * pairs:2].set(sink + moved)
    return tallies[jax.random.permutation(jax.random.fold_in(own_key, 2), number_of)]


def noise(rng, extent, width, limit, split=(), kind=jnp.bfloat16):
    drawn = jax.random.normal(rng, extent, jnp.float32) * width
    if len(split) > 0:
        drawn = level_of(rng, extent, split, -0.22, 0.18) * drawn
    return jnp.clip(drawn, min=-limit, max=limit).astype(kind)


def bell_draw_with(rng, shape, scale, limit, split, heavy, held_as=jnp.bfloat16):
    values = scale * jax.random.normal(rng, shape, jnp.float32)
    if split:
        values = values * level_of(rng, shape, split, -0.22, 0.18)
    return jnp.clip(with_spikes(values, jax.random.fold_in(rng, 3), *heavy), -limit, limit).astype(held_as)


def setup_inputs(seed: int = 0) -> dict:
    keys = jax.random.split(jax.random.key(seed), 15)
    hidden_in = noise(keys[0], (GROUPS, GROUP_TOK, D), 1.0, 6.0, ((0, 4), (1, 4)))
    out_grad = bell_draw_with(keys[1], (GROUPS, GROUP_TOK, D), 1.0, 8.0, ((0, 4), (1, 4)), (1, 2, 4, 2.0))
    ln_gain = jnp.clip(1.0 + 0.1 * jax.random.normal(keys[2], (D,), jnp.float32), 0.5, 1.5).astype(jnp.bfloat16)
    ln_bias = noise(keys[3], (D,), 0.2, 1.25)
    w_qkv = noise(keys[4], (D, 3 * D), D ** -0.5, 0.125, ((0, 4), (1, 2)))
    b_qkv = noise(keys[5], (3 * D,), 0.3, 1.75, ((0, 2),))
    w_dense = noise(keys[6], (D, D), (D // 16) ** -0.5, 0.5, ((0, 4), (1, 2)))
    b_dense = noise(keys[7], (D,), 0.2, 1.25)
    w_fc1 = noise(keys[8], (D, FF), D ** -0.5, 0.125, ((0, 4), (1, 2)))
    b_fc1 = noise(keys[9], (FF,), 0.3, 1.75, ((0, 2),))
    w_fc2 = noise(keys[10], (D, FF), (FF // 4) ** -0.5, 0.125, ((0, 4), (1, 2)))
    b_fc2 = noise(keys[11], (D,), 0.2, 1.25)
    lengths = jax.vmap(lambda own: uneven_parts(own, NSEQ, GROUP_TOK, MAXLEN, 2))(jax.random.split(keys[12], GROUPS)).reshape((GROUPS, NSEQ)).astype(jnp.int32)
    assignment = jax.vmap(lambda own: jax.random.permutation(own, GROUP_TOK))(jax.random.split(keys[13], GROUPS)).reshape((GROUPS, GROUP_TOK)).astype(jnp.int32)
    return {"hidden_in": hidden_in, "out_grad": out_grad, "ln_gain": ln_gain, "ln_bias": ln_bias, "w_qkv": w_qkv, "b_qkv": b_qkv, "w_dense": w_dense, "b_dense": b_dense, "w_fc1": w_fc1, "b_fc1": b_fc1, "w_fc2": w_fc2, "b_fc2": b_fc2, "lengths": lengths, "assignment": assignment}


MASKED = -1e+30
EPSILON = 1e-05
HIGHEST = lax.Precision.HIGHEST

@jax.custom_vjp
def low(v):
    return lax.optimization_barrier(v.astype(jnp.bfloat16)).astype(jnp.float32)

@jax.custom_vjp
def low_back(v):
    return v

def low_keep(v):
    return (low(v), None)

def low_pass(kept, grad):
    return (grad,)

def back_keep(v):
    return (v, None)

def back_low(kept, grad):
    return (low(grad),)
low.defvjp(low_keep, low_pass)
low_back.defvjp(back_keep, back_low)

def layer_norm(source, gain_vec, shift_vec):
    centred = source - lax.optimization_barrier(jnp.mean(source, axis=-1, keepdims=True))
    spread = lax.optimization_barrier(jnp.mean(centred * centred, axis=-1, keepdims=True))
    return centred * lax.rsqrt(spread + EPSILON) * gain_vec + shift_vec

def rotate(values, places):
    half_dim = ROT // 2
    frequency = jnp.power(10000.0, -(jnp.arange(half_dim, dtype=jnp.float32) * 2.0 / ROT))
    angles = places.astype(jnp.float32)[:, None] * frequency[None, :]
    cosine = jnp.cos(angles)[:, None, :]
    sine_part = jnp.sin(angles)[:, None, :]
    leading = values[..., :half_dim]
    trailing = values[..., half_dim:ROT]
    return jnp.concatenate([leading * cosine - trailing * sine_part, trailing * cosine + leading * sine_part, values[..., ROT:]], axis=-1)

def positions(packed, lengths):
    seq_ends = jnp.cumsum(lengths).astype(jnp.int32)
    starts = seq_ends - lengths
    segment = lax.optimization_barrier(jnp.sum((packed[:, None] >= seq_ends[None, :]).astype(jnp.int32), axis=1))
    owner_mask = segment[:, None] == jnp.arange(lengths.shape[0], dtype=jnp.int32)[None, :]
    return (segment, packed - lax.optimization_barrier(jnp.sum(jnp.where(owner_mask, starts[None, :], 0), axis=1)))

def gelu_tanh(values):
    return jax.nn.gelu(values, approximate=True)

def reference(hidden_in, out_grad, ln_gain, ln_bias, w_qkv, b_qkv, w_dense, b_dense, w_fc1, b_fc1, w_fc2, b_fc2, lengths, assignment):
    segment, place = jax.vmap(positions)(assignment, lengths)
    scaling = 1.0 / math.sqrt(HEAD)

    def head_attend(keep_mask, queries, keys_in, values_in):
        scores = low_back(jnp.dot(queries, keys_in.T, precision=HIGHEST) * scaling)
        scores = jnp.where(keep_mask, scores, MASKED)
        row_max = lax.optimization_barrier(jnp.max(scores, axis=-1, keepdims=True))
        raised = jnp.exp(scores - row_max)
        probs = raised / lax.optimization_barrier(jnp.sum(raised, axis=-1, keepdims=True))
        return jnp.dot(low(probs), values_in, precision=HIGHEST)
    head_step = jax.checkpoint(head_attend)

    def group_attend(inputs):
        queries, keys_in, values_in, seg_ids, packed = inputs
        keep_mask = (seg_ids[:, None] == seg_ids[None, :]) & (packed[None, :] <= packed[:, None])
        outputs = lax.map(lambda triple: head_step(keep_mask, triple[0], triple[1], triple[2]), (jnp.moveaxis(queries, 1, 0), jnp.moveaxis(keys_in, 1, 0), jnp.moveaxis(values_in, 1, 0)))
        return jnp.moveaxis(outputs, 0, 1).reshape(GROUP_TOK, D)

    def forward(source, gain_vec, shift_vec, weight_qkv, bias_qkv, weight_dense, bias_dense, weight_up, bias_up, weight_down, bias_down):
        normed_low = low(layer_norm(source, gain_vec, shift_vec))
        qkv = low_back(jnp.einsum('gtd,de->gte', normed_low, weight_qkv, precision=HIGHEST)) + bias_qkv
        qkv = qkv.reshape(GROUPS * GROUP_TOK, HEADS, 3, HEAD)
        flat_place = place.reshape(-1)
        queries = low_back(low(rotate(qkv[:, :, 0], flat_place))).reshape(GROUPS, GROUP_TOK, HEADS, HEAD)
        keys_rot = low_back(low(rotate(qkv[:, :, 1], flat_place))).reshape(GROUPS, GROUP_TOK, HEADS, HEAD)
        values_low = low_back(low(qkv[:, :, 2])).reshape(GROUPS, GROUP_TOK, HEADS, HEAD)
        mixed = lax.map(group_attend, (queries, keys_rot, values_low, segment, assignment))
        mixed = low_back(low(mixed))
        attn_branch = jnp.einsum('gti,oi->gto', mixed, weight_dense, precision=HIGHEST) + bias_dense
        up_value = low_back(jnp.einsum('gtd,df->gtf', normed_low, weight_up, precision=HIGHEST)) + bias_up
        act_low = low(gelu_tanh(up_value))
        mlp_branch = jnp.einsum('gtf,of->gto', act_low, weight_down, precision=HIGHEST) + bias_down
        return source + attn_branch + mlp_branch
    floats = [a.astype(jnp.float32) for a in (hidden_in, ln_gain, ln_bias, w_qkv, b_qkv, w_dense, b_dense, w_fc1, b_fc1, w_fc2, b_fc2)]
    result, pullback = jax.vjp(forward, floats[0], floats[1], floats[2], floats[3], floats[4], floats[5], floats[6], floats[7], floats[8], floats[9], floats[10])
    grads = pullback(out_grad.astype(jnp.float32))
    return (result.astype(jnp.bfloat16), grads[0], grads[1], grads[2], grads[3], grads[4], grads[5], grads[6], grads[7], grads[8], grads[9], grads[10])
```

```python
import math

import jax
import jax.numpy as jnp
from jax import lax
from jax.sharding import PartitionSpec as P

HEAD = 64
ROT = 32
MASKED = -1e30
EPSILON = 1e-05
f32 = jnp.float32
bf16 = jnp.bfloat16


def positions(packed, lengths):
    seq_ends = jnp.cumsum(lengths)
    starts = seq_ends - lengths
    segment = jnp.sum((packed[:, None] >= seq_ends[None, :]).astype(jnp.int32), axis=1)
    owner_mask = segment[:, None] == jnp.arange(lengths.shape[0], dtype=jnp.int32)[None, :]
    return (segment, packed - jnp.sum(jnp.where(owner_mask, starts[None, :], 0), axis=1))


def gelu_tanh(values):
    return jax.nn.gelu(values, approximate=True)


def swap(x, axis, bit):
    size = lax.axis_size(axis)
    return lax.ppermute(x, axis, [(i, i ^ bit) for i in range(size)])


def line_gather(own):
    n = lax.axis_size("fsdp")
    z = lax.axis_index("fsdp")
    up = down = own
    ups, downs = [None], [None]
    for s in range(1, n):
        up = lax.ppermute(up, "fsdp", [(i, i + 1) for i in range(s - 1, n - 1)])
        down = lax.ppermute(down, "fsdp", [(i, i - 1) for i in range(1, n - s + 1)])
        ups.append(up)
        downs.append(down)
    return [own] + [jnp.where(s <= z, ups[s], downs[n - s]) for s in range(1, n)]


def line_scatter(parts):
    n = lax.axis_size("fsdp")
    up = down = None
    for s in range(1, n):
        send_up, send_down = parts[s], parts[n - s]
        if s > 1:
            send_up, send_down = add(send_up, up), add(send_down, down)
        up = lax.ppermute(send_up, "fsdp", [(i, i + 1) for i in range(0, min(s, n - 1))])
        down = lax.ppermute(send_down, "fsdp", [(i, i - 1) for i in range(max(n - s, 1), n)])
    return parts[0].astype(f32) + up.astype(f32) + down.astype(f32)


def add(a, b):
    return (a.astype(f32) + b.astype(f32)).astype(bf16)


def gather_rows(rows):
    m = lax.axis_size("ctx")
    half = rows.shape[0] // 2
    mine = rows[:half]
    if m == 4:
        quarter = half // 2
        first = swap(mine, "ctx", 1)
        second = swap(mine, "ctx", 2)
        third_a = swap(first[:quarter], "ctx", 2)
        third_b = swap(second[quarter:], "ctx", 1)
        got = [[first], [second], [third_a, third_b]]
    else:
        slots = [mine]
        bit = 1
        while bit < m:
            slots = slots + [swap(piece, "ctx", bit) for piece in slots]
            bit *= 2
        got = [[piece] for piece in slots[1:]]
    blocks = [rows]
    for pieces in got:
        blocks = blocks + pieces + [swap(piece, "tp", 1) for piece in pieces]
    return jnp.concatenate(blocks, axis=0)


def scatter_rows(part):
    m = lax.axis_size("ctx")
    half = part.shape[0] // (2 * m)
    blocks = part.reshape(m, 2, half, part.shape[1])
    slots = add(blocks[:, 0], swap(blocks[:, 1], "tp", 1))
    if m == 4:
        quarter = half // 2
        to_second = swap(slots[3, :quarter], "ctx", 2)
        to_first = swap(slots[3, quarter:], "ctx", 1)
        first = jnp.concatenate([add(slots[1, :quarter], to_second), slots[1, quarter:]], axis=0)
        second = jnp.concatenate([slots[2, :quarter], add(slots[2, quarter:], to_first)], axis=0)
        return (
            slots[0].astype(f32)
            + swap(first, "ctx", 1).astype(f32)
            + swap(second, "ctx", 2).astype(f32)
        )
    bit = m // 2
    while bit >= 1:
        slots = add(slots[:bit], swap(slots[bit : 2 * bit], "ctx", bit))
        bit //= 2
    return slots[0].astype(f32)


def spread_columns(block):
    m = lax.axis_size("ctx")
    c = lax.axis_index("ctx")
    rows, cols = block.shape[0] // m, block.shape[1]
    pieces = []
    for j in range(m):
        piece = lax.dynamic_slice_in_dim(block, (c ^ j) * rows, rows, axis=0)
        pieces.append(piece if j == 0 else swap(piece, "ctx", j))
    stacked = jnp.stack(pieces)
    ordered = [
        lax.dynamic_index_in_dim(stacked, c ^ k, axis=0, keepdims=False) for k in range(m)
    ]
    return jnp.concatenate(ordered, axis=1).astype(f32)


def column_order(heads):
    order = []
    for part in range(2):
        for start, width in ((0, ROT // 2), (ROT // 2, ROT // 2), (ROT, HEAD - ROT)):
            for head in range(heads):
                base = (head * 3 + part) * HEAD + start
                order += list(range(base, base + width))
    for head in range(heads):
        base = (head * 3 + 2) * HEAD
        order += list(range(base, base + HEAD))
    return order


def shards(
    hidden_in,
    out_grad,
    ln_gain,
    ln_bias,
    w_qkv,
    b_qkv,
    w_dense,
    b_dense,
    w_fc1,
    b_fc1,
    w_fc2,
    b_fc2,
    lengths,
    assignment,
):
    n = lax.axis_size("fsdp")
    m = lax.axis_size("ctx")
    z = lax.axis_index("fsdp")
    c = lax.axis_index("ctx")
    t = lax.axis_index("tp")
    rows, width = hidden_in.shape[1], hidden_in.shape[2]
    half = rows // 2
    group_rows = rows * m
    feat = width // n
    heads = w_qkv.shape[1] // (3 * HEAD) // m
    wide = heads * HEAD
    by_columns = (((1,), (1,)), ((), ()))
    by_rows = (((0,), (0,)), ((), ()))
    scaling = 1.0 / math.sqrt(HEAD)

    def turn(x):
        return jnp.concatenate(
            [lax.dynamic_slice_in_dim(x, lax.rem(z - s + n, n) * feat, feat, axis=1) for s in range(n)],
            axis=1,
        )

    def halves(x):
        return jnp.where(t == 0, x, jnp.concatenate([x[half:], x[:half]], axis=0))

    def mine(weight):
        share = weight.shape[-1] // m
        return lax.dynamic_slice_in_dim(weight, c * share, share, axis=weight.ndim - 1)

    order = jnp.array(column_order(heads), jnp.int32)
    place_of = (jnp.arange(3 * wide, dtype=jnp.int32)[:, None] == order[None, :]).astype(bf16)
    qkv_own = jnp.dot(mine(w_qkv), place_of, preferred_element_type=f32).astype(bf16)
    qkv_bias = jnp.dot(mine(b_qkv)[None], place_of, preferred_element_type=f32)
    up_bias = mine(b_fc1).astype(f32)

    up_slots = line_gather(mine(w_fc1))
    qkv_slots = line_gather(qkv_own)
    dense_slots = line_gather(mine(w_dense))
    down_slots = line_gather(mine(w_fc2))
    w_up = jnp.concatenate(up_slots, axis=0)
    w_in = jnp.concatenate(qkv_slots, axis=0)
    w_out = jnp.concatenate(dense_slots, axis=0)
    w_down = jnp.concatenate(down_slots, axis=0)

    source = halves(hidden_in[0]).astype(f32)
    gain_vec = ln_gain.astype(f32)
    shift_vec = ln_bias.astype(f32)
    centred = source - jnp.mean(source, axis=-1, keepdims=True)
    rstd = lax.rsqrt(jnp.mean(centred * centred, axis=-1, keepdims=True) + EPSILON)
    xhat = centred * rstd
    normed = gather_rows(turn((xhat * gain_vec + shift_vec).astype(bf16)))
    grad_own = halves(out_grad[0])
    grads = gather_rows(turn(grad_own))

    block_of = [((c ^ j) * 2 + (t ^ h)) * half for j in range(m) for h in range(2)]
    packed = jnp.concatenate(
        [lax.dynamic_slice_in_dim(assignment[0], at, half) for at in block_of]
    )
    segment, place = positions(packed, lengths[0])
    frequency = jnp.power(
        10000.0, -(jnp.arange(ROT // 2, dtype=f32) * 2.0 / ROT)
    )
    angles = place.astype(f32)[:, None] * jnp.tile(frequency, 2 * heads)[None, :]
    cosine = jnp.cos(angles)
    sine = jnp.sin(angles) * jnp.where(jnp.arange(ROT * heads) < ROT // 2 * heads, -1.0, 1.0)[None, :]
    split = ROT // 2 * heads

    def rotate(x, sign):
        front = x[:, : 2 * split]
        partner = jnp.concatenate([front[:, split:], front[:, :split]], axis=1)
        return jnp.concatenate([front * cosine + sign * sine * partner, x[:, 2 * split :]], axis=1)

    up = jnp.dot(normed, w_up, preferred_element_type=f32) + up_bias
    act = gelu_tanh(up).astype(bf16)
    qkv = jnp.dot(normed, w_in, preferred_element_type=f32) + qkv_bias
    query = rotate(qkv[:, :wide], 1.0).astype(bf16)
    key = rotate(qkv[:, wide : 2 * wide], 1.0).astype(bf16)
    value = qkv[:, 2 * wide :].astype(bf16)
    lane = jnp.arange(wide)
    lane_head = jnp.where(lane < 2 * split, (lane % split) // (ROT // 2), (lane - 2 * split) // (HEAD - ROT))
    head_qk = (lane_head[None] == jnp.arange(heads)[:, None]).astype(bf16)
    head_v = ((lane // HEAD)[None] == jnp.arange(heads)[:, None]).astype(bf16)
    block_rows = min(512, group_rows)
    block_ids = jnp.arange(group_rows // block_rows, dtype=jnp.int32)

    def block_scores(start):
        q = lax.dynamic_slice_in_dim(query, start, block_rows)
        seg = lax.dynamic_slice_in_dim(segment, start, block_rows)
        pos = lax.dynamic_slice_in_dim(packed, start, block_rows)
        keep = (seg[:, None] == segment[None, :]) & (packed[None, :] <= pos[:, None])
        scores = jnp.einsum("hqe,ke->hqk", q[None] * head_qk[:, None, :], key, preferred_element_type=f32)
        return q, jnp.where(keep[None], scores * scaling, MASKED)

    def attend(index):
        _, scores = block_scores(index * block_rows)
        top = jnp.max(scores, axis=-1, keepdims=True)
        raised = jnp.exp(scores - top)
        total = jnp.sum(raised, axis=-1, keepdims=True)
        weights = (raised / total).astype(bf16)
        mixed = jnp.einsum("hqk,hke->qe", weights, value[None] * head_v[:, None, :], preferred_element_type=f32)
        return mixed.astype(bf16), (top + jnp.log(total))[..., 0]

    mixed, lse = lax.map(attend, block_ids)
    mixed = mixed.reshape(group_rows, wide)

    branch = lax.dot_general(mixed, w_out, by_columns, preferred_element_type=f32)
    branch = branch + lax.dot_general(act, w_down, by_columns, preferred_element_type=f32)
    branch = turn(scatter_rows(branch.astype(bf16)))
    biases = b_dense.astype(f32) + b_fc2.astype(f32)
    result = (source[:half] + branch + biases).astype(bf16)
    result_other = swap(result, "tp", 1)
    result = halves(jnp.concatenate([result, result_other], axis=0))

    mixed_grad = jnp.dot(grads, w_out, preferred_element_type=f32).astype(bf16)
    act_grad = jnp.dot(grads, w_down, preferred_element_type=f32)
    up_grad = jax.vjp(gelu_tanh, up)[1](act_grad)[0]
    up_grad_low = up_grad.astype(bf16)

    def attend_back(carried, inputs):
        key_grad, value_grad = carried
        index, lse_blk = inputs
        start = index * block_rows
        q, scores = block_scores(start)
        probs = jnp.exp(scores - lse_blk[:, :, None])
        grad = lax.dynamic_slice_in_dim(mixed_grad, start, block_rows)
        grad_h = grad[None] * head_v[:, None, :]
        prob_grad = jnp.einsum("hqe,ke->hqk", grad_h, value, preferred_element_type=f32)
        inner = jnp.sum(probs * prob_grad, axis=-1, keepdims=True)
        score_grad = (probs * (prob_grad - inner)).astype(bf16)
        query_grad = scaling * jnp.einsum(
            "hqk,hke->qe", score_grad, key[None] * head_qk[:, None, :], preferred_element_type=f32
        )
        key_grad = key_grad + scaling * jnp.einsum(
            "hqk,hqe->ke", score_grad, q[None] * head_qk[:, None, :], preferred_element_type=f32
        )
        value_grad = value_grad + jnp.einsum(
            "hqk,hqe->ke", probs.astype(bf16), grad_h, preferred_element_type=f32
        )
        return (key_grad, value_grad), query_grad

    zeros = jnp.zeros((group_rows, wide), f32)
    (key_grad, value_grad), query_grad = lax.scan(attend_back, (zeros, zeros), (block_ids, lse))
    query_grad = query_grad.reshape(group_rows, wide)
    qkv_grad = jnp.concatenate(
        [rotate(query_grad, -1.0), rotate(key_grad, -1.0), value_grad], axis=1
    )
    qkv_grad_low = qkv_grad.astype(bf16)

    normed_grad = lax.dot_general(qkv_grad_low, w_in, by_columns, preferred_element_type=f32)
    normed_grad = normed_grad + lax.dot_general(up_grad_low, w_up, by_columns, preferred_element_type=f32)
    normed_grad = turn(scatter_rows(normed_grad.astype(bf16)))
    d = normed_grad * gain_vec
    xhat_half = xhat[:half]
    input_grad = (
        rstd[:half]
        * (
            d
            - jnp.mean(d, axis=-1, keepdims=True)
            - xhat_half * jnp.mean(d * xhat_half, axis=-1, keepdims=True)
        )
        + grad_own[:half].astype(f32)
    )
    input_grad = halves(jnp.concatenate([input_grad, swap(input_grad, "tp", 1)], axis=0))

    def summed(left, right):
        full = lax.dot_general(left, right, by_rows, preferred_element_type=f32).astype(bf16)
        return line_scatter([full[s * feat : (s + 1) * feat] for s in range(n)]).astype(bf16)

    down_part = spread_columns(summed(grads, act))
    dense_part = spread_columns(summed(grads, mixed))
    qkv_sum = summed(normed, qkv_grad_low)
    qkv_sum = lax.dot_general(qkv_sum, place_of, by_columns, preferred_element_type=f32).astype(bf16)
    qkv_part = spread_columns(qkv_sum)
    up_part = spread_columns(summed(normed, up_grad_low))

    def placed(vector):
        full = jnp.zeros((vector.shape[0] * m,), f32)
        return lax.dynamic_update_slice_in_dim(full, vector, c * vector.shape[0], axis=0)

    qkv_bias_grad = lax.dot_general(
        jnp.sum(qkv_grad, axis=0)[None], place_of.astype(f32), by_columns,
        precision=lax.Precision.HIGHEST, preferred_element_type=f32,
    )[0]
    qkv_bias_grad, up_bias_grad, out_bias_grad = lax.psum(
        (placed(qkv_bias_grad), placed(jnp.sum(up_grad, axis=0)), jnp.sum(grad_own.astype(f32), axis=0)),
        ("fsdp", "ctx"),
    )
    gain_grad, shift_grad = lax.psum(
        (jnp.sum(normed_grad * xhat_half, axis=0), jnp.sum(normed_grad, axis=0)),
        ("fsdp", "ctx", "tp"),
    )
    return (
        result[None],
        input_grad[None],
        gain_grad,
        shift_grad,
        qkv_part,
        qkv_bias_grad,
        dense_part,
        out_bias_grad,
        up_part,
        up_bias_grad,
        down_part,
        out_bias_grad,
    )


def solution(mesh):
    in_specs = (
        P("fsdp", "ctx", None),
        P("fsdp", "ctx", None),
        P(),
        P(),
        P("fsdp", "tp"),
        P("tp"),
        P("fsdp", "tp"),
        P(),
        P("fsdp", "tp"),
        P("tp"),
        P("fsdp", "tp"),
        P(),
        P("fsdp", None),
        P("fsdp", None),
    )
    out_specs = (
        P("fsdp", "ctx", None),
        P("fsdp", "ctx", None),
        P(),
        P(),
        P(("fsdp", "ctx"), "tp"),
        P("tp"),
        P(("fsdp", "ctx"), "tp"),
        P(),
        P(("fsdp", "ctx"), "tp"),
        P("tp"),
        P(("fsdp", "ctx"), "tp"),
        P(),
    )
    return jax.shard_map(shards, mesh=mesh, in_specs=in_specs, out_specs=out_specs, check_vma=False)
```

```python
import functools
import math

import jax
import jax.numpy as jnp
from jax import lax
from jax.experimental import pallas as pl
from jax.experimental.pallas import tpu as pltpu
from jax.sharding import PartitionSpec as P

HEAD = 64
ROT = 32
MASKED = -1e30
EPSILON = 1e-05
f32 = jnp.float32
bf16 = jnp.bfloat16


def positions(packed, lengths):
    seq_ends = jnp.cumsum(lengths)
    starts = seq_ends - lengths
    segment = jnp.sum((packed[:, None] >= seq_ends[None, :]).astype(jnp.int32), axis=1)
    owner_mask = segment[:, None] == jnp.arange(lengths.shape[0], dtype=jnp.int32)[None, :]
    return (segment, packed - jnp.sum(jnp.where(owner_mask, starts[None, :], 0), axis=1))


def gelu_tanh(values):
    return jax.nn.gelu(values, approximate=True)


def swap(x, axis, bit):
    size = lax.axis_size(axis)
    return lax.ppermute(x, axis, [(i, i ^ bit) for i in range(size)])


def everywhere(x, *axes):
    for axis in axes:
        bit = 1
        while bit < lax.axis_size(axis):
            x = x + swap(x, axis, bit)
            bit *= 2
    return x


def line_gather(own):
    n = lax.axis_size("fsdp")
    z = lax.axis_index("fsdp")
    up = down = own
    ups, downs = [None], [None]
    for s in range(1, n):
        up = lax.ppermute(up, "fsdp", [(i, i + 1) for i in range(s - 1, n - 1)])
        down = lax.ppermute(down, "fsdp", [(i, i - 1) for i in range(1, n - s + 1)])
        ups.append(up)
        downs.append(down)
    return [own] + [jnp.where(s <= z, ups[s], downs[n - s]) for s in range(1, n)]


def line_scatter(parts):
    n = lax.axis_size("fsdp")
    up = down = None
    for s in range(1, n):
        send_up, send_down = parts[s], parts[n - s]
        if s > 1:
            send_up, send_down = add(send_up, up), add(send_down, down)
        up = lax.ppermute(send_up, "fsdp", [(i, i + 1) for i in range(0, min(s, n - 1))])
        down = lax.ppermute(send_down, "fsdp", [(i, i - 1) for i in range(max(n - s, 1), n)])
    return parts[0].astype(f32) + up.astype(f32) + down.astype(f32)


def add(a, b):
    return (a.astype(f32) + b.astype(f32)).astype(bf16)


def gather_rows(rows):
    m = lax.axis_size("ctx")
    half = rows.shape[0] // 2
    mine = rows[:half]
    if m == 4:
        quarter = half // 2
        first = swap(mine, "ctx", 1)
        second = swap(mine, "ctx", 2)
        third_a = swap(first[:quarter], "ctx", 2)
        third_b = swap(second[quarter:], "ctx", 1)
        got = [[first], [second], [third_a, third_b]]
    else:
        slots = [mine]
        bit = 1
        while bit < m:
            slots = slots + [swap(piece, "ctx", bit) for piece in slots]
            bit *= 2
        got = [[piece] for piece in slots[1:]]
    blocks = [rows]
    for pieces in got:
        blocks = blocks + pieces + [swap(piece, "tp", 1) for piece in pieces]
    return jnp.concatenate(blocks, axis=0)


def scatter_rows(part):
    m = lax.axis_size("ctx")
    half = part.shape[0] // (2 * m)
    blocks = part.reshape(m, 2, half, part.shape[1])
    slots = add(blocks[:, 0], swap(blocks[:, 1], "tp", 1))
    if m == 4:
        quarter = half // 2
        to_second = swap(slots[3, :quarter], "ctx", 2)
        to_first = swap(slots[3, quarter:], "ctx", 1)
        first = jnp.concatenate([add(slots[1, :quarter], to_second), slots[1, quarter:]], axis=0)
        second = jnp.concatenate([slots[2, :quarter], add(slots[2, quarter:], to_first)], axis=0)
        return (
            slots[0].astype(f32)
            + swap(first, "ctx", 1).astype(f32)
            + swap(second, "ctx", 2).astype(f32)
        )
    bit = m // 2
    while bit >= 1:
        slots = add(slots[:bit], swap(slots[bit : 2 * bit], "ctx", bit))
        bit //= 2
    return slots[0].astype(f32)


def spread_columns(block):
    m = lax.axis_size("ctx")
    c = lax.axis_index("ctx")
    rows, cols = block.shape[0] // m, block.shape[1]
    pieces = []
    for j in range(m):
        piece = lax.dynamic_slice_in_dim(block, (c ^ j) * rows, rows, axis=0)
        pieces.append(piece if j == 0 else swap(piece, "ctx", j))
    stacked = jnp.stack(pieces)
    ordered = [
        lax.dynamic_index_in_dim(stacked, c ^ k, axis=0, keepdims=False) for k in range(m)
    ]
    return jnp.concatenate(ordered, axis=1).astype(f32)


def column_order(heads):
    order = []
    for part in range(2):
        for start, width in ((0, ROT // 2), (ROT // 2, ROT // 2), (ROT, HEAD - ROT)):
            for head in range(heads):
                base = (head * 3 + part) * HEAD + start
                order += list(range(base, base + width))
    for head in range(heads):
        base = (head * 3 + 2) * HEAD
        order += list(range(base, base + HEAD))
    return order


BLOCK = 256
NT = (((1,), (1,)), ((), ()))


def mm(a, b, dims=(((1,), (0,)), ((), ()))):
    return lax.dot_general(a, b, dims, preferred_element_type=f32)


def turned(x, cosine, sine, split):
    slab = cosine.shape[1]
    front = x[:, :slab]
    if slab == 2 * split:
        partner = pltpu.roll(front, split, 1)
    else:
        lane = lax.broadcasted_iota(jnp.int32, front.shape, 1)
        partner = jnp.where(
            lane < split, pltpu.roll(front, slab - split, 1), pltpu.roll(front, split, 1)
        )
    front = front * cosine + partner * sine
    if slab == x.shape[1]:
        return front
    return jnp.concatenate([front, x[:, slab:]], axis=1)


def to_packed(prow_ref, block, data):
    shape = (BLOCK, prow_ref.shape[1])
    at = lax.broadcasted_iota(jnp.int32, shape, 0) + block * BLOCK
    return mm((at == prow_ref[...]).astype(f32).astype(bf16), data)


def to_arrival(pcol_ref, block, data):
    rows = pl.ds(pl.multiple_of(block * BLOCK, BLOCK), BLOCK)
    shape = (BLOCK, data.shape[0])
    at = lax.broadcasted_iota(jnp.int32, shape, 1)
    return mm((at == pcol_ref[rows, :]).astype(f32).astype(bf16), data)


def kept(i, j, start):
    keys = lax.broadcasted_iota(jnp.int32, (BLOCK, BLOCK), 0) + j * BLOCK
    queries = lax.broadcasted_iota(jnp.int32, (BLOCK, BLOCK), 1) + i * BLOCK
    return (keys >= start) & (keys <= queries)


def forward_kernel(
    heads, low_ref, qkv_ref, bias_ref, cos_ref, sin_ref, prow_ref, pcol_ref, start_ref, qmask_ref,
    packed_ref, outt_ref, lse_ref, mixed_ref, x_ref, vt_ref, mp_ref,
):
    rows_all, wide = mixed_ref.shape
    blocks = rows_all // BLOCK
    split = ROT // 2 * heads

    @pl.loop(0, blocks)
    def _(r):
        rows = pl.ds(pl.multiple_of(r * BLOCK, BLOCK), BLOCK)
        cosine, sine = cos_ref[rows, :], sin_ref[rows, :]
        x = qkv_ref[rows, :] + bias_ref[0:1, :]
        q = turned(x[:, :wide], cosine, sine, split) * (1.0 / math.sqrt(HEAD))
        k = turned(x[:, wide : 2 * wide], cosine, sine, split)
        x_ref[rows, :] = jnp.concatenate([q, k, x[:, 2 * wide :]], axis=1).astype(bf16)

    @pl.loop(0, blocks)
    def _(p):
        rows = pl.ds(pl.multiple_of(p * BLOCK, BLOCK), BLOCK)
        y = to_packed(prow_ref, p, x_ref[...])
        packed_ref[rows, :] = y.astype(bf16)
        vt_ref[:, rows] = y[:, 2 * wide :].T.astype(bf16)

    @pl.loop(0, blocks)
    def _(i):
        rows = pl.ds(pl.multiple_of(i * BLOCK, BLOCK), BLOCK)
        start = start_ref[0:1, rows]
        q = packed_ref[rows, :wide]
        qs = [q * qmask_ref[h] for h in range(heads)]

        def step(j, carried):
            keys = pl.ds(pl.multiple_of(j * BLOCK, BLOCK), BLOCK)
            k = packed_ref[keys, wide : 2 * wide]
            keep = kept(i, j, start)
            after = []
            for h in range(heads):
                top, total, acc = carried[h]
                s = jnp.where(keep, mm(k, qs[h], NT), MASKED)
                new_top = jnp.maximum(top, jnp.max(s, axis=0, keepdims=True))
                p = jnp.exp(s - new_top)
                alpha = jnp.exp(top - new_top)
                total = total * alpha + jnp.sum(p, axis=0, keepdims=True)
                acc = acc * alpha + mm(vt_ref[h * HEAD : (h + 1) * HEAD, keys], p.astype(bf16))
                after.append((new_top, total, acc))
            return tuple(after)

        begin = tuple(
            (
                jnp.full((1, BLOCK), MASKED, f32),
                jnp.zeros((1, BLOCK), f32),
                jnp.zeros((HEAD, BLOCK), f32),
            )
            for _ in range(heads)
        )
        state = lax.fori_loop(low_ref[i], i + 1, step, begin)
        out = jnp.concatenate([acc / total for _, total, acc in state], axis=0)
        outt_ref[:, rows] = out
        mp_ref[rows, :] = out.T.astype(bf16)
        lse = [top + jnp.log(total) for top, total, _ in state]
        lse_ref[:, rows] = jnp.concatenate(lse + [jnp.zeros((8 - heads, BLOCK), f32)], axis=0)

    @pl.loop(0, blocks)
    def _(r):
        rows = pl.ds(pl.multiple_of(r * BLOCK, BLOCK), BLOCK)
        mixed_ref[rows, :] = to_arrival(pcol_ref, r, mp_ref[...]).astype(bf16)


def backward_kernel(
    heads, low_ref, packed_ref, outt_ref, lse_ref, grad_ref, cos_ref, sin_ref, prow_ref, pcol_ref, start_ref,
    qmask_ref, vmask_ref, ktmask_ref,
    qkv_grad_ref, bias_grad_ref, kt_ref, dk_ref, dv_ref, dq_ref, gp_ref,
):
    rows_all, wide = grad_ref.shape
    blocks = rows_all // BLOCK
    split = ROT // 2 * heads

    @pl.loop(0, blocks)
    def _(p):
        rows = pl.ds(pl.multiple_of(p * BLOCK, BLOCK), BLOCK)
        gp_ref[rows, :wide] = to_packed(prow_ref, p, grad_ref[...]).astype(bf16)
        kt_ref[:, rows] = packed_ref[rows, wide : 2 * wide].astype(f32).T.astype(bf16)
        dk_ref[rows, :] = jnp.zeros((BLOCK, wide), f32)
        dv_ref[rows, :] = jnp.zeros((BLOCK, wide), f32)

    @pl.loop(0, blocks)
    def _(i):
        rows = pl.ds(pl.multiple_of(i * BLOCK, BLOCK), BLOCK)
        start = start_ref[0:1, rows]
        q = packed_ref[rows, :wide]
        g = gp_ref[rows, :wide]
        qs = [q * qmask_ref[h] for h in range(heads)]
        gs = [g * vmask_ref[h] for h in range(heads)]
        product = g.astype(f32).T * outt_ref[:, rows]
        inner = [
            jnp.sum(product[h * HEAD : (h + 1) * HEAD], axis=0, keepdims=True) for h in range(heads)
        ]
        lse = [lse_ref[h : h + 1, rows] for h in range(heads)]

        def step(j, dqt):
            keys = pl.ds(pl.multiple_of(j * BLOCK, BLOCK), BLOCK)
            k = packed_ref[keys, wide : 2 * wide]
            v = packed_ref[keys, 2 * wide :]
            kt = kt_ref[:, keys]
            keep = kept(i, j, start)
            dk = dk_ref[keys, :]
            dv = dv_ref[keys, :]
            for h in range(heads):
                s = jnp.where(keep, mm(k, qs[h], NT), MASKED)
                p = jnp.exp(s - lse[h])
                dp = mm(v, gs[h], NT)
                ds = (p * (dp - inner[h])).astype(bf16)
                dv = dv + mm(p.astype(bf16), gs[h])
                dk = dk + mm(ds, qs[h])
                dqt = dqt + mm(kt * ktmask_ref[h], ds)
            dk_ref[keys, :] = dk
            dv_ref[keys, :] = dv
            return dqt

        dqt = lax.fori_loop(low_ref[i], i + 1, step, jnp.zeros((wide, BLOCK), f32))
        dq_ref[rows, :] = dqt.T * (1.0 / math.sqrt(HEAD))

    bias_grad_ref[...] = jnp.zeros(bias_grad_ref.shape, f32)

    @pl.loop(0, blocks)
    def _(p):
        rows = pl.ds(pl.multiple_of(p * BLOCK, BLOCK), BLOCK)
        cosine, sine = cos_ref[rows, :], -sin_ref[rows, :]
        dq = turned(dq_ref[rows, :], cosine, sine, split)
        dk = turned(dk_ref[rows, :], cosine, sine, split)
        full = jnp.concatenate([dq, dk, dv_ref[rows, :]], axis=1)
        bias_grad_ref[0:1, :] = bias_grad_ref[0:1, :] + jnp.sum(full, axis=0, keepdims=True)
        gp_ref[rows, :] = full.astype(bf16)

    @pl.loop(0, blocks)
    def _(r):
        rows = pl.ds(pl.multiple_of(r * BLOCK, BLOCK), BLOCK)
        qkv_grad_ref[rows, :] = to_arrival(pcol_ref, r, gp_ref[...]).astype(bf16)


def whole(count):
    return [pl.BlockSpec(memory_space=pltpu.VMEM)] * count


def attend(heads, low, qkv, bias, cosine, sine, prow, pcol, start, qmask):
    rows, wide = qkv.shape[0], heads * HEAD
    pairs = (rows // BLOCK) * 4 * heads * BLOCK * BLOCK
    return pl.pallas_call(
        functools.partial(forward_kernel, heads),
        grid_spec=pltpu.PrefetchScalarGridSpec(
            num_scalar_prefetch=1,
            grid=(),
            in_specs=whole(8),
            out_specs=whole(4),
            scratch_shapes=[
                pltpu.VMEM((rows, 3 * wide), bf16),
                pltpu.VMEM((wide, rows), bf16),
                pltpu.VMEM((rows, wide), bf16),
            ],
        ),
        out_shape=[
            jax.ShapeDtypeStruct((rows, 3 * wide), bf16),
            jax.ShapeDtypeStruct((wide, rows), f32),
            jax.ShapeDtypeStruct((8, rows), f32),
            jax.ShapeDtypeStruct((rows, wide), bf16),
        ],
        compiler_params=pltpu.CompilerParams(vmem_limit_bytes=40 * 2**20),
        cost_estimate=pl.CostEstimate(
            flops=8 * rows * rows * wide + pairs * 4 * wide, bytes_accessed=20 * rows * wide, transcendentals=pairs
        ),
        name="attend_forward",
    )(low, qkv, bias, cosine, sine, prow, pcol, start, qmask)


def attend_back(heads, low, packed, outt, lse, grad, cosine, sine, prow, pcol, start, qmask, vmask, ktmask):
    rows, wide = grad.shape
    pairs = (rows // BLOCK) * 4 * heads * BLOCK * BLOCK
    return pl.pallas_call(
        functools.partial(backward_kernel, heads),
        grid_spec=pltpu.PrefetchScalarGridSpec(
            num_scalar_prefetch=1,
            grid=(),
            in_specs=whole(12),
            out_specs=whole(2),
            scratch_shapes=[
                pltpu.VMEM((wide, rows), bf16),
                pltpu.VMEM((rows, wide), f32),
                pltpu.VMEM((rows, wide), f32),
                pltpu.VMEM((rows, wide), f32),
                pltpu.VMEM((rows, 3 * wide), bf16),
            ],
        ),
        out_shape=[
            jax.ShapeDtypeStruct((rows, 3 * wide), bf16),
            jax.ShapeDtypeStruct((8, 3 * wide), f32),
        ],
        compiler_params=pltpu.CompilerParams(vmem_limit_bytes=40 * 2**20),
        cost_estimate=pl.CostEstimate(
            flops=8 * rows * rows * wide + pairs * 10 * wide, bytes_accessed=20 * rows * wide, transcendentals=pairs
        ),
        name="attend_backward",
    )(low, packed, outt, lse, grad, cosine, sine, prow, pcol, start, qmask, vmask, ktmask)


def shards(
    hidden_in,
    out_grad,
    ln_gain,
    ln_bias,
    w_qkv,
    b_qkv,
    w_dense,
    b_dense,
    w_fc1,
    b_fc1,
    w_fc2,
    b_fc2,
    lengths,
    assignment,
):
    n = lax.axis_size("fsdp")
    m = lax.axis_size("ctx")
    z = lax.axis_index("fsdp")
    c = lax.axis_index("ctx")
    t = lax.axis_index("tp")
    rows, width = hidden_in.shape[1], hidden_in.shape[2]
    half = rows // 2
    group_rows = rows * m
    feat = width // n
    heads = w_qkv.shape[1] // (3 * HEAD) // m
    wide = heads * HEAD
    by_columns = (((1,), (1,)), ((), ()))
    by_rows = (((0,), (0,)), ((), ()))

    def turn(x):
        return jnp.concatenate(
            [lax.dynamic_slice_in_dim(x, lax.rem(z - s + n, n) * feat, feat, axis=1) for s in range(n)],
            axis=1,
        )

    def halves(x):
        return jnp.where(t == 0, x, jnp.concatenate([x[half:], x[:half]], axis=0))

    def mine(weight):
        share = weight.shape[-1] // m
        return lax.dynamic_slice_in_dim(weight, c * share, share, axis=weight.ndim - 1)

    order = jnp.array(column_order(heads), jnp.int32)
    place_of = (jnp.arange(3 * wide, dtype=jnp.int32)[:, None] == order[None, :]).astype(bf16)
    qkv_own = jnp.dot(mine(w_qkv), place_of, preferred_element_type=f32).astype(bf16)
    qkv_bias = jnp.dot(mine(b_qkv)[None], place_of, preferred_element_type=f32)
    up_bias = mine(b_fc1).astype(f32)

    up_slots = line_gather(mine(w_fc1))
    qkv_slots = line_gather(qkv_own)
    dense_slots = line_gather(mine(w_dense))
    down_slots = line_gather(mine(w_fc2))
    w_up = jnp.concatenate(up_slots, axis=0)
    w_in = jnp.concatenate(qkv_slots, axis=0)
    w_out = jnp.concatenate(dense_slots, axis=0)
    w_down = jnp.concatenate(down_slots, axis=0)

    source = halves(hidden_in[0]).astype(f32)
    gain_vec = ln_gain.astype(f32)
    shift_vec = ln_bias.astype(f32)
    centred = source - jnp.mean(source, axis=-1, keepdims=True)
    rstd = lax.rsqrt(jnp.mean(centred * centred, axis=-1, keepdims=True) + EPSILON)
    xhat = centred * rstd
    normed = gather_rows(turn((xhat * gain_vec + shift_vec).astype(bf16)))
    grad_own = halves(out_grad[0])
    grads = gather_rows(turn(grad_own))

    block_of = [((c ^ j) * 2 + (t ^ h)) * half for j in range(m) for h in range(2)]
    packed = jnp.concatenate(
        [lax.dynamic_slice_in_dim(assignment[0], at, half) for at in block_of]
    )
    split = ROT // 2 * heads
    slab = 2 * split if 2 * split % 128 == 0 else wide
    lane = jnp.arange(wide)
    lane_head = jnp.where(lane < 2 * split, (lane % split) // (ROT // 2), (lane - 2 * split) // (HEAD - ROT))
    exponent = (lane[:slab] % (ROT // 2)).astype(f32) * 2.0 / ROT
    frequency = jnp.where(lane[:slab] < 2 * split, jnp.power(10000.0, -exponent), 0.0)
    sign = jnp.where(lane[:slab] < split, -1.0, 1.0)

    def tables(place):
        angles = place.astype(f32)[:, None] * frequency[None, :]
        return jnp.cos(angles), jnp.sin(angles) * sign[None, :]

    ordered = jnp.arange(group_rows, dtype=jnp.int32)
    place_packed = positions(ordered, lengths[0])[1]
    start = ordered - place_packed
    low = start[::BLOCK] // BLOCK
    start = start[None]
    cos_arrival, sin_arrival = tables(positions(packed, lengths[0])[1])
    cos_packed, sin_packed = tables(place_packed)
    prow, pcol = packed[None], packed[:, None]
    head_qk = (lane_head[None] == jnp.arange(heads)[:, None]).astype(bf16)
    head_v = ((lane // HEAD)[None] == jnp.arange(heads)[:, None]).astype(bf16)
    qmask = jnp.broadcast_to(head_qk[:, None, :], (heads, BLOCK, wide))
    vmask = jnp.broadcast_to(head_v[:, None, :], (heads, BLOCK, wide))
    ktmask = jnp.broadcast_to(head_qk[:, :, None], (heads, wide, BLOCK))

    up = jnp.dot(normed, w_up, preferred_element_type=f32) + up_bias
    act = gelu_tanh(up).astype(bf16)
    qkv = jnp.dot(normed, w_in, preferred_element_type=f32)
    qkv_bias = jnp.broadcast_to(qkv_bias, (8, 3 * wide))
    qkv_packed, outt, lse, mixed = attend(
        heads, low, qkv, qkv_bias, cos_arrival, sin_arrival, prow, pcol, start, qmask
    )

    branch = lax.dot_general(mixed, w_out, by_columns, preferred_element_type=f32)
    branch = branch + lax.dot_general(act, w_down, by_columns, preferred_element_type=f32)
    branch = turn(scatter_rows(branch.astype(bf16)))
    biases = b_dense.astype(f32) + b_fc2.astype(f32)
    result = (source[:half] + branch + biases).astype(bf16)
    result_other = swap(result, "tp", 1)
    result = halves(jnp.concatenate([result, result_other], axis=0))

    mixed_grad = jnp.dot(grads, w_out, preferred_element_type=f32).astype(bf16)
    act_grad = jnp.dot(grads, w_down, preferred_element_type=f32)
    up_grad = jax.vjp(gelu_tanh, up)[1](act_grad)[0]
    up_grad_low = up_grad.astype(bf16)

    qkv_grad_low, qkv_bias_sum = attend_back(
        heads, low, qkv_packed, outt, lse, mixed_grad, cos_packed, sin_packed, prow, pcol, start,
        qmask, vmask, ktmask,
    )

    normed_grad = lax.dot_general(qkv_grad_low, w_in, by_columns, preferred_element_type=f32)
    normed_grad = normed_grad + lax.dot_general(up_grad_low, w_up, by_columns, preferred_element_type=f32)
    normed_grad = turn(scatter_rows(normed_grad.astype(bf16)))
    d = normed_grad * gain_vec
    xhat_half = xhat[:half]
    input_grad = (
        rstd[:half]
        * (
            d
            - jnp.mean(d, axis=-1, keepdims=True)
            - xhat_half * jnp.mean(d * xhat_half, axis=-1, keepdims=True)
        )
        + grad_own[:half].astype(f32)
    )
    input_grad = halves(jnp.concatenate([input_grad, swap(input_grad, "tp", 1)], axis=0))

    def summed(left, right):
        full = lax.dot_general(left, right, by_rows, preferred_element_type=f32).astype(bf16)
        return line_scatter([full[s * feat : (s + 1) * feat] for s in range(n)]).astype(bf16)

    down_part = spread_columns(summed(grads, act))
    dense_part = spread_columns(summed(grads, mixed))
    qkv_sum = summed(normed, qkv_grad_low)
    qkv_sum = lax.dot_general(qkv_sum, place_of, by_columns, preferred_element_type=f32).astype(bf16)
    qkv_part = spread_columns(qkv_sum)
    up_part = spread_columns(summed(normed, up_grad_low))

    def placed(vector):
        full = jnp.zeros((vector.shape[0] * m,), f32)
        return lax.dynamic_update_slice_in_dim(full, vector, c * vector.shape[0], axis=0)

    qkv_bias_grad = lax.dot_general(
        qkv_bias_sum[:1], place_of.astype(f32), by_columns,
        precision=lax.Precision.HIGHEST, preferred_element_type=f32,
    )[0]
    bias_sums = everywhere(
        jnp.concatenate([placed(qkv_bias_grad), placed(jnp.sum(up_grad, axis=0))]), "ctx", "fsdp"
    )
    qkv_bias_grad, up_bias_grad = bias_sums[: 3 * wide * m], bias_sums[3 * wide * m :]
    out_bias_grad = everywhere(jnp.sum(out_grad[0].astype(f32), axis=0), "ctx", "fsdp")
    norm_sums = everywhere(
        jnp.stack([jnp.sum(normed_grad * xhat_half, axis=0), jnp.sum(normed_grad, axis=0)]),
        "tp", "ctx", "fsdp",
    )
    gain_grad, shift_grad = norm_sums[0], norm_sums[1]
    return (
        result[None],
        input_grad[None],
        gain_grad,
        shift_grad,
        qkv_part,
        qkv_bias_grad,
        dense_part,
        out_bias_grad,
        up_part,
        up_bias_grad,
        down_part,
        out_bias_grad,
    )


def solution(mesh):
    in_specs = (
        P("fsdp", "ctx", None),
        P("fsdp", "ctx", None),
        P(),
        P(),
        P("fsdp", "tp"),
        P("tp"),
        P("fsdp", "tp"),
        P(),
        P("fsdp", "tp"),
        P("tp"),
        P("fsdp", "tp"),
        P(),
        P("fsdp", None),
        P("fsdp", None),
    )
    out_specs = (
        P("fsdp", "ctx", None),
        P("fsdp", "ctx", None),
        P(),
        P(),
        P(("fsdp", "ctx"), "tp"),
        P("tp"),
        P(("fsdp", "ctx"), "tp"),
        P(),
        P(("fsdp", "ctx"), "tp"),
        P("tp"),
        P(("fsdp", "ctx"), "tp"),
        P(),
    )
    return jax.shard_map(shards, mesh=mesh, in_specs=in_specs, out_specs=out_specs, check_vma=False)
```

```python
import functools
import math

import jax
import jax.numpy as jnp
from jax import lax
from jax.experimental import pallas as pl
from jax.experimental.pallas import tpu as pltpu
from jax.sharding import PartitionSpec as P

HEAD = 64
ROT = 32
MASKED = -1e30
EPSILON = 1e-05
f32 = jnp.float32
bf16 = jnp.bfloat16


def positions(packed, lengths):
    seq_ends = jnp.cumsum(lengths)
    starts = seq_ends - lengths
    segment = jnp.sum((packed[:, None] >= seq_ends[None, :]).astype(jnp.int32), axis=1)
    owner_mask = segment[:, None] == jnp.arange(lengths.shape[0], dtype=jnp.int32)[None, :]
    return (segment, packed - jnp.sum(jnp.where(owner_mask, starts[None, :], 0), axis=1))


def gelu_tanh(values):
    return jax.nn.gelu(values, approximate=True)


def swap(x, axis, bit):
    size = lax.axis_size(axis)
    return lax.ppermute(x, axis, [(i, i ^ bit) for i in range(size)])


def everywhere(x, *axes):
    for axis in axes:
        bit = 1
        while bit < lax.axis_size(axis):
            x = x + swap(x, axis, bit)
            bit *= 2
    return x


def after(x, *before):
    before = [item for item in before if item is not None]
    return lax.optimization_barrier((x, *before))[0] if before else x


class Order:
    def __init__(self):
        self.last = ()

    def then(self, x):
        return after(x, *self.last)

    def did(self, *values):
        self.last = values

    def arrive(self, values):
        values = after(values, *self.last)
        self.last = self.last + tuple(jax.tree.leaves(values))
        return values


def line_up(x, first, last):
    return lax.ppermute(x, "fsdp", [(i, i + 1) for i in range(first, last)])


def line_down(x, first, last):
    return lax.ppermute(x, "fsdp", [(i, i - 1) for i in range(first, last)])


class Gather:
    def __init__(self, own):
        self.ups, self.downs = [own], [own]

    def start(self):
        n, s = lax.axis_size("fsdp"), len(self.ups)
        if s < n:
            self.ups.append(line_up(self.ups[-1], s - 1, n - 1))
            self.downs.append(line_down(self.downs[-1], 1, n - s + 1))

    def arrive(self, order):
        self.ups[-1], self.downs[-1] = order.arrive((self.ups[-1], self.downs[-1]))

    def rest(self, order):
        for _ in range(len(self.ups), lax.axis_size("fsdp")):
            self.start()
            self.arrive(order)

    def sources(self):
        return self.ups + self.downs[1:]


class Scatter:
    def __init__(self, parts):
        self.parts, self.sums, self.step = parts, None, 1

    def start(self):
        n, s = lax.axis_size("fsdp"), self.step
        if s < n:
            up, down = self.parts[s], self.parts[n - s]
            if self.sums is not None:
                up, down = add(up, self.sums[0]), add(down, self.sums[1])
            self.sums = line_up(up, 0, min(s, n - 1)), line_down(down, max(n - s, 1), n)
            self.step += 1

    def arrive(self, order):
        self.sums = order.arrive(self.sums)

    def rest(self, order):
        for _ in range(self.step, lax.axis_size("fsdp")):
            self.start()
            self.arrive(order)

    def total(self):
        up, down = self.sums
        return (self.parts[0].astype(f32) + up.astype(f32) + down.astype(f32)).astype(bf16)


class Rows:
    def __init__(self, own):
        self.own = own
        self.half = own.shape[0] // 2

    def start(self):
        mine = self.own[: self.half]
        self.got = [swap(mine, "ctx", 1 << k) for k in range(lax.axis_size("ctx").bit_length() - 1)]

    def arrive(self, order):
        self.got = order.arrive(self.got)

    def start_far(self):
        m, quarter = lax.axis_size("ctx"), self.half // 2
        if m == 4:
            first, second = self.got
            self.far = [swap(first[:quarter], "ctx", 2), swap(second[quarter:], "ctx", 1)]
            self.near = [first, second]
        else:
            mine = self.own[: self.half]
            self.near = self.got
            self.far = [swap(mine, "ctx", j) for j in range(1, m) if j & (j - 1)]
        self.near_other = [swap(piece, "tp", 1) for piece in self.near]

    def arrive_far(self, order):
        self.far, self.near_other = order.arrive((self.far, self.near_other))

    def start_last(self):
        self.far_other = [swap(piece, "tp", 1) for piece in self.far]

    def arrive_last(self, order):
        self.far_other = order.arrive(self.far_other)

    def blocks(self):
        m = lax.axis_size("ctx")
        near = list(zip(self.near, self.near_other))
        far = list(zip(self.far, self.far_other))
        blocks = [self.own]
        for j in range(1, m):
            if j & (j - 1) == 0:
                blocks += near.pop(0)
            elif m == 4:
                blocks += [far[0][0], far[1][0], far[0][1], far[1][1]]
            else:
                blocks += far.pop(0)
        return blocks


class RowSums:
    def __init__(self, slots):
        self.slots = [slots[j] for j in range(slots.shape[0])]

    def start(self):
        m, slots = len(self.slots), self.slots
        quarter = slots[0].shape[0] // 2
        if m == 4:
            self.got = [swap(slots[3][:quarter], "ctx", 2), swap(slots[3][quarter:], "ctx", 1)]
        else:
            self.got = [swap(slots[j], "ctx", j) for j in range(1, m) if j & (j - 1)]

    def arrive(self, order):
        self.got = order.arrive(self.got)

    def start_last(self):
        m, slots = len(self.slots), self.slots
        quarter = slots[0].shape[0] // 2
        if m == 4:
            first = jnp.concatenate([add(slots[1][:quarter], self.got[0]), slots[1][quarter:]], axis=0)
            second = jnp.concatenate([slots[2][:quarter], add(slots[2][quarter:], self.got[1])], axis=0)
            self.last, self.got = [swap(first, "ctx", 1), swap(second, "ctx", 2)], []
        else:
            self.last = [swap(slots[j], "ctx", j) for j in range(1, m) if j & (j - 1) == 0]

    def arrive_last(self, order):
        self.last, self.slots[0] = order.arrive((self.last, self.slots[0]))

    def total(self):
        return sum((x.astype(f32) for x in self.got + self.last), self.slots[0].astype(f32))


def add(a, b):
    return (a.astype(f32) + b.astype(f32)).astype(bf16)


def spread_start(block):
    m = lax.axis_size("ctx")
    c = lax.axis_index("ctx")
    rows = block.shape[0] // m
    pieces = []
    for j in range(m):
        piece = lax.dynamic_slice_in_dim(block, (c ^ j) * rows, rows, axis=0)
        pieces.append(piece if j == 0 else swap(piece, "ctx", j))
    return pieces


def side_by_side(pieces):
    m = lax.axis_size("ctx")
    c = lax.axis_index("ctx")
    stacked = jnp.stack(pieces)
    ordered = [lax.dynamic_index_in_dim(stacked, c ^ k, axis=0, keepdims=False) for k in range(m)]
    return jnp.concatenate(ordered, axis=1).astype(f32)


def column_order(heads):
    order = []
    for part in range(2):
        for start, width in ((0, ROT // 2), (ROT // 2, ROT // 2), (ROT, HEAD - ROT)):
            for head in range(heads):
                base = (head * 3 + part) * HEAD + start
                order += list(range(base, base + width))
    for head in range(heads):
        base = (head * 3 + 2) * HEAD
        order += list(range(base, base + HEAD))
    return order


BLOCK = 256
NT = (((1,), (1,)), ((), ()))


def mm(a, b, dims=(((1,), (0,)), ((), ()))):
    return lax.dot_general(a, b, dims, preferred_element_type=f32)


def turned(x, cosine, sine, split):
    slab = cosine.shape[1]
    front = x[:, :slab]
    if slab == 2 * split:
        partner = pltpu.roll(front, split, 1)
    else:
        lane = lax.broadcasted_iota(jnp.int32, front.shape, 1)
        partner = jnp.where(
            lane < split, pltpu.roll(front, slab - split, 1), pltpu.roll(front, split, 1)
        )
    front = front * cosine + partner * sine
    if slab == x.shape[1]:
        return front
    return jnp.concatenate([front, x[:, slab:]], axis=1)


def to_packed(prow_ref, block, data):
    shape = (BLOCK, prow_ref.shape[1])
    at = lax.broadcasted_iota(jnp.int32, shape, 0) + block * BLOCK
    return mm((at == prow_ref[...]).astype(f32).astype(bf16), data)


def to_arrival(pcol_ref, block, data):
    rows = pl.ds(pl.multiple_of(block * BLOCK, BLOCK), BLOCK)
    shape = (BLOCK, data.shape[0])
    at = lax.broadcasted_iota(jnp.int32, shape, 1)
    return mm((at == pcol_ref[rows, :]).astype(f32).astype(bf16), data)


def kept(i, j, start):
    keys = lax.broadcasted_iota(jnp.int32, (BLOCK, BLOCK), 0) + j * BLOCK
    queries = lax.broadcasted_iota(jnp.int32, (BLOCK, BLOCK), 1) + i * BLOCK
    return (keys >= start) & (keys <= queries)


def fetch(z_ref, sources, weight_ref, sems, first):
    n = (len(sources) + 1) // 2
    feat, cols = weight_ref.shape[0] // n, weight_ref.shape[1]

    def copy(source, s):
        rows = pl.ds(s * feat, feat)
        return pltpu.make_async_copy(
            source.at[:, pl.ds(first, cols)], weight_ref.at[rows, :], sems.at[s]
        )

    def each(do):
        do(copy(sources[0], 0))
        for s in range(1, n):

            @pl.when(z_ref[0] >= s)
            def _():
                do(copy(sources[s], s))

            @pl.when(z_ref[0] < s)
            def _():
                do(copy(sources[2 * n - 1 - s], s))

    each(lambda c: c.start())
    each(lambda c: c.wait())


def pack_kernel(heads, count, z_ref, x_in_ref, bias_ref, cos_ref, sin_ref, prow_ref, *rest):
    sources, (packed_ref, vt_ref, x_ref, weight_ref, sems) = rest[:count], rest[count:]
    wide = vt_ref.shape[0]
    blocks = x_ref.shape[0] // BLOCK
    split = ROT // 2 * heads
    r = pl.program_id(0)

    @pl.when(r == 0)
    def _():
        fetch(z_ref, sources, weight_ref, sems, 0)

    rows = pl.ds(pl.multiple_of(r * BLOCK, BLOCK), BLOCK)
    cosine, sine = cos_ref[rows, :], sin_ref[rows, :]
    x_in = x_in_ref[...]
    for part in range(3):
        at = slice(part * wide, (part + 1) * wide)
        x = mm(x_in, weight_ref[:, at]) + bias_ref[0:1, at]
        if part < 2:
            x = turned(x, cosine, sine, split)
        if part == 0:
            x = x * (1.0 / math.sqrt(HEAD))
        x_ref[rows, at] = x.astype(bf16)

    @pl.when(r == blocks - 1)
    def _():
        @pl.loop(0, blocks)
        def _(p):
            rows = pl.ds(pl.multiple_of(p * BLOCK, BLOCK), BLOCK)
            y = to_packed(prow_ref, p, x_ref[...])
            packed_ref[rows, :] = y.astype(bf16)
            vt_ref[:, rows] = y[:, 2 * wide :].T.astype(bf16)


def curve(u):
    square = u * u
    return jnp.tanh(math.sqrt(2.0 / math.pi) * (u + 0.044715 * (square * u))), square


def up_kernel(count, z_ref, x_ref, bias_ref, *rest):
    sources, (up_ref, act_ref, weight_ref, sems) = rest[:count], rest[count:]

    @pl.when(pl.program_id(0) == 0)
    def _():
        fetch(z_ref, sources, weight_ref, sems, 0)

    x = x_ref[...]
    step = min(256, up_ref.shape[1])
    for at in range(0, up_ref.shape[1], step):
        at = slice(at, at + step)
        u = mm(x, weight_ref[:, at]) + bias_ref[0:1, at]
        up_ref[:, at] = u
        act_ref[:, at] = (0.5 * u * (1.0 + curve(u)[0])).astype(bf16)


def up_back_kernel(count, z_ref, x_ref, up_ref, *rest):
    sources, (grad_ref, sum_ref, weight_ref, sems) = rest[:count], rest[count:]

    @pl.when(pl.program_id(0) == 0)
    def _():
        fetch(z_ref, sources, weight_ref, sems, 0)
        sum_ref[...] = jnp.zeros(sum_ref.shape, f32)

    x = x_ref[...]
    step = min(256, grad_ref.shape[1])
    for at in range(0, grad_ref.shape[1], step):
        at = slice(at, at + step)
        u = up_ref[:, at]
        bend, square = curve(u)
        slope = 0.5 * (1.0 + bend) + (0.5 * math.sqrt(2.0 / math.pi)) * u * (
            (1.0 - bend * bend) * (1.0 + (3.0 * 0.044715) * square)
        )
        grad = mm(x, weight_ref[:, at]) * slope
        grad_ref[:, at] = grad.astype(bf16)
        sum_ref[0:1, at] = sum_ref[0:1, at] + jnp.sum(grad, axis=0, keepdims=True)


def plain_kernel(count, first, z_ref, x_ref, *rest):
    sources, (out_ref, weight_ref, sems) = rest[:count], rest[count:]

    @pl.when(pl.program_id(0) == 0)
    def _():
        fetch(z_ref, sources, weight_ref, sems, first)

    out_ref[...] = mm(x_ref[...], weight_ref[...]).astype(bf16)


def spread_kernel(count, first, z_ref, a_ref, b_ref, *rest):
    a_sources, b_sources = rest[:count], rest[count : 2 * count]
    keep_ref, send_ref, a_weight_ref, b_weight_ref, sems = rest[2 * count :]

    @pl.when(pl.program_id(0) == 0)
    def _():
        fetch(z_ref, a_sources, a_weight_ref, sems, first)
        fetch(z_ref, b_sources, b_weight_ref, sems, 0)

    half = keep_ref.shape[1]
    for h, out_ref in ((0, keep_ref), (1, send_ref)):
        rows = slice(h * half, (h + 1) * half)
        a, b = a_ref[rows, :], b_ref[rows, :]
        for at in range(0, out_ref.shape[2], 256):
            at = slice(at, at + 256)
            out = mm(a, a_weight_ref[at, :], NT) + mm(b, b_weight_ref[at, :], NT)
            out_ref[0, :, at] = out.astype(bf16)


def forward_kernel(
    heads, low_ref, packed_ref, vt_ref, pcol_ref, start_ref, qmask_ref,
    outt_ref, lse_ref, mixed_ref, mp_ref,
):
    rows_all, wide = mixed_ref.shape
    blocks = rows_all // BLOCK

    @pl.loop(0, blocks)
    def _(i):
        rows = pl.ds(pl.multiple_of(i * BLOCK, BLOCK), BLOCK)
        start = start_ref[0:1, rows]
        q = packed_ref[rows, :wide]
        qs = [q * qmask_ref[h] for h in range(heads)]

        def step(j, carried):
            keys = pl.ds(pl.multiple_of(j * BLOCK, BLOCK), BLOCK)
            k = packed_ref[keys, wide : 2 * wide]
            keep = kept(i, j, start)
            after = []
            for h in range(heads):
                top, total, acc = carried[h]
                s = jnp.where(keep, mm(k, qs[h], NT), MASKED)
                new_top = jnp.maximum(top, jnp.max(s, axis=0, keepdims=True))
                p = jnp.exp(s - new_top)
                alpha = jnp.exp(top - new_top)
                total = total * alpha + jnp.sum(p, axis=0, keepdims=True)
                acc = acc * alpha + mm(vt_ref[h * HEAD : (h + 1) * HEAD, keys], p.astype(bf16))
                after.append((new_top, total, acc))
            return tuple(after)

        begin = tuple(
            (
                jnp.full((1, BLOCK), MASKED, f32),
                jnp.zeros((1, BLOCK), f32),
                jnp.zeros((HEAD, BLOCK), f32),
            )
            for _ in range(heads)
        )
        state = lax.fori_loop(low_ref[i], i + 1, step, begin)
        out = jnp.concatenate([acc / total for _, total, acc in state], axis=0)
        outt_ref[:, rows] = out
        mp_ref[rows, :] = out.T.astype(bf16)
        lse = [top + jnp.log(total) for top, total, _ in state]
        lse_ref[:, rows] = jnp.concatenate(lse + [jnp.zeros((8 - heads, BLOCK), f32)], axis=0)

    @pl.loop(0, blocks)
    def _(r):
        rows = pl.ds(pl.multiple_of(r * BLOCK, BLOCK), BLOCK)
        mixed_ref[rows, :] = to_arrival(pcol_ref, r, mp_ref[...]).astype(bf16)


def backward_kernel(
    heads, low_ref, packed_ref, outt_ref, lse_ref, grad_ref, cos_ref, sin_ref, prow_ref, pcol_ref, start_ref,
    qmask_ref, vmask_ref, ktmask_ref,
    qkv_grad_ref, bias_grad_ref, kt_ref, dk_ref, dv_ref, dq_ref, gp_ref,
):
    rows_all, wide = grad_ref.shape
    blocks = rows_all // BLOCK
    split = ROT // 2 * heads

    @pl.loop(0, blocks)
    def _(p):
        rows = pl.ds(pl.multiple_of(p * BLOCK, BLOCK), BLOCK)
        gp_ref[rows, :wide] = to_packed(prow_ref, p, grad_ref[...]).astype(bf16)
        kt_ref[:, rows] = packed_ref[rows, wide : 2 * wide].astype(f32).T.astype(bf16)
        dk_ref[rows, :] = jnp.zeros((BLOCK, wide), f32)
        dv_ref[rows, :] = jnp.zeros((BLOCK, wide), f32)

    @pl.loop(0, blocks)
    def _(i):
        rows = pl.ds(pl.multiple_of(i * BLOCK, BLOCK), BLOCK)
        start = start_ref[0:1, rows]
        q = packed_ref[rows, :wide]
        g = gp_ref[rows, :wide]
        qs = [q * qmask_ref[h] for h in range(heads)]
        gs = [g * vmask_ref[h] for h in range(heads)]
        product = g.astype(f32).T * outt_ref[:, rows]
        inner = [
            jnp.sum(product[h * HEAD : (h + 1) * HEAD], axis=0, keepdims=True) for h in range(heads)
        ]
        lse = [lse_ref[h : h + 1, rows] for h in range(heads)]

        def step(j, dqt):
            keys = pl.ds(pl.multiple_of(j * BLOCK, BLOCK), BLOCK)
            k = packed_ref[keys, wide : 2 * wide]
            v = packed_ref[keys, 2 * wide :]
            kt = kt_ref[:, keys]
            keep = kept(i, j, start)
            dk = dk_ref[keys, :]
            dv = dv_ref[keys, :]
            for h in range(heads):
                s = jnp.where(keep, mm(k, qs[h], NT), MASKED)
                p = jnp.exp(s - lse[h])
                dp = mm(v, gs[h], NT)
                ds = (p * (dp - inner[h])).astype(bf16)
                dv = dv + mm(p.astype(bf16), gs[h])
                dk = dk + mm(ds, qs[h])
                dqt = dqt + mm(kt * ktmask_ref[h], ds)
            dk_ref[keys, :] = dk
            dv_ref[keys, :] = dv
            return dqt

        dqt = lax.fori_loop(low_ref[i], i + 1, step, jnp.zeros((wide, BLOCK), f32))
        dq_ref[rows, :] = dqt.T * (1.0 / math.sqrt(HEAD))

    bias_grad_ref[...] = jnp.zeros(bias_grad_ref.shape, f32)

    @pl.loop(0, blocks)
    def _(p):
        rows = pl.ds(pl.multiple_of(p * BLOCK, BLOCK), BLOCK)
        cosine, sine = cos_ref[rows, :], -sin_ref[rows, :]
        dq = turned(dq_ref[rows, :], cosine, sine, split)
        dk = turned(dk_ref[rows, :], cosine, sine, split)
        full = jnp.concatenate([dq, dk, dv_ref[rows, :]], axis=1)
        bias_grad_ref[0:1, :] = bias_grad_ref[0:1, :] + jnp.sum(full, axis=0, keepdims=True)
        gp_ref[rows, :] = full.astype(bf16)

    @pl.loop(0, blocks)
    def _(r):
        rows = pl.ds(pl.multiple_of(r * BLOCK, BLOCK), BLOCK)
        qkv_grad_ref[rows, :] = to_arrival(pcol_ref, r, gp_ref[...]).astype(bf16)


def whole(count):
    return [pl.BlockSpec(memory_space=pltpu.VMEM)] * count


COST = 0.05


def blocks_call(kernel, name, z, ins, in_specs, sources, outs, out_specs, scratch, steps, flops, weight_shapes):
    sems = len(sources[0]) // 2 + 1
    return pl.pallas_call(
        kernel,
        grid_spec=pltpu.PrefetchScalarGridSpec(
            num_scalar_prefetch=1,
            grid=(steps,),
            in_specs=in_specs + [pl.BlockSpec(memory_space=pl.ANY)] * sum(map(len, sources)),
            out_specs=out_specs,
            scratch_shapes=scratch
            + [pltpu.VMEM(shape, bf16) for shape in weight_shapes]
            + [pltpu.SemaphoreType.DMA((sems,))],
        ),
        out_shape=outs,
        compiler_params=pltpu.CompilerParams(vmem_limit_bytes=48 * 2**20),
        cost_estimate=pl.CostEstimate(flops=int(COST * flops), bytes_accessed=2**20, transcendentals=0),
        name=name,
    )(z, *ins, *[x for group in sources for x in group])


def fixed(shape):
    return pl.BlockSpec(shape, lambda *_: (0,) * len(shape))


def by_row(rows, cols):
    return pl.BlockSpec((rows, cols), lambda i, *_: (i, 0))


def prepare_kernel(norm, slots, at_ref, x_ref, gain_ref, shift_ref, out_ref, *rest):
    rows, width = x_ref.shape
    half, step = rows // 2, 64
    feat = width // slots
    if not norm:
        rest[0][...] = jnp.zeros(rest[0].shape, f32)

    @pl.loop(0, rows // step)
    def _(b):
        source = pl.ds(pl.multiple_of(b * step, step), step)
        first = b * step
        second = (first >= half).astype(jnp.int32)
        place = (second ^ at_ref[1]) * half + first - second * half
        target = pl.ds(pl.multiple_of(place, step), step)
        x = x_ref[source, :].astype(f32)
        if norm:
            mean = jnp.mean(x, axis=-1, keepdims=True)
            centred = x - mean
            rstd = lax.rsqrt(jnp.mean(centred * centred, axis=-1, keepdims=True) + EPSILON)
        else:
            rest[0][0:1, :] = rest[0][0:1, :] + jnp.sum(x, axis=0, keepdims=True)
        for s in range(slots):
            block = lax.rem(at_ref[0] - s + slots, slots)
            columns = pl.ds(pl.multiple_of(block * feat, feat), feat)
            y = x_ref[source, columns]
            if norm:
                y = (y.astype(f32) - mean) * rstd * gain_ref[0:1, columns] + shift_ref[0:1, columns]
            out_ref[target, s * feat : (s + 1) * feat] = y.astype(bf16)


def prepare(norm, at, x, gain, shift, n):
    rows, width = x.shape
    out = [jax.ShapeDtypeStruct((rows, width), bf16)]
    if not norm:
        out.append(jax.ShapeDtypeStruct((8, width), f32))
    return pl.pallas_call(
        functools.partial(prepare_kernel, norm, n),
        grid_spec=pltpu.PrefetchScalarGridSpec(
            num_scalar_prefetch=1, grid=(), in_specs=whole(3), out_specs=whole(len(out))
        ),
        out_shape=out,
        compiler_params=pltpu.CompilerParams(vmem_limit_bytes=40 * 2**20),
        cost_estimate=pl.CostEstimate(flops=2**20, bytes_accessed=2**20, transcendentals=0),
        name="prepare",
    )(at, x, gain, shift)


def assemble_kernel(*refs):
    *pieces, out_ref, sems = refs

    def each(do):
        first = 0
        for k, piece in enumerate(pieces):
            count = piece.shape[0]
            do(pltpu.make_async_copy(piece, out_ref.at[pl.ds(first, count), :], sems.at[k]))
            first += count

    each(lambda copy: copy.start())
    each(lambda copy: copy.wait())


def assemble(pieces):
    rows = sum(piece.shape[0] for piece in pieces)
    return pl.pallas_call(
        assemble_kernel,
        in_specs=whole(len(pieces)),
        out_specs=pl.BlockSpec(memory_space=pl.ANY),
        scratch_shapes=[pltpu.SemaphoreType.DMA((len(pieces),))],
        out_shape=jax.ShapeDtypeStruct((rows, pieces[0].shape[1]), bf16),
        compiler_params=pltpu.CompilerParams(vmem_limit_bytes=40 * 2**20),
        cost_estimate=pl.CostEstimate(flops=2**20, bytes_accessed=2**20, transcendentals=0),
        name="assemble",
    )(*pieces)


def pack(heads, z, normed, bias, cosine, sine, prow, sources):
    rows, width = normed.shape
    wide = heads * HEAD
    slab = cosine.shape[1]
    return blocks_call(
        functools.partial(pack_kernel, heads, len(sources)), "pack", z,
        [normed, bias, cosine, sine, prow],
        [by_row(BLOCK, width), fixed(bias.shape), fixed((rows, slab)), fixed((rows, slab)), fixed(prow.shape)],
        [sources],
        [jax.ShapeDtypeStruct((rows, 3 * wide), bf16), jax.ShapeDtypeStruct((wide, rows), bf16)],
        [fixed((rows, 3 * wide)), fixed((wide, rows))],
        [pltpu.VMEM((rows, 3 * wide), bf16)],
        rows // BLOCK, 12 * rows * rows * wide, [(width, 3 * wide)],
    )


def up_forward(z, normed, bias, sources):
    rows, width = normed.shape
    cols = bias.shape[1]
    return blocks_call(
        functools.partial(up_kernel, len(sources)), "up", z,
        [normed, bias], [by_row(512, width), fixed(bias.shape)], [sources],
        [jax.ShapeDtypeStruct((rows, cols), f32), jax.ShapeDtypeStruct((rows, cols), bf16)],
        [by_row(512, cols), by_row(512, cols)], [],
        rows // 512, 2 * rows * width * cols, [(width, cols)],
    )


def up_backward(z, grads, up, sources):
    rows, width = grads.shape
    cols = up.shape[1]
    return blocks_call(
        functools.partial(up_back_kernel, len(sources)), "up_back", z,
        [grads, up], [by_row(512, width), by_row(512, cols)], [sources],
        [jax.ShapeDtypeStruct((rows, cols), bf16), jax.ShapeDtypeStruct((8, cols), f32)],
        [by_row(512, cols), fixed((8, cols))], [],
        rows // 512, 2 * rows * width * cols, [(width, cols)],
    )


def times(z, x, sources, first, cols):
    rows, width = x.shape
    return blocks_call(
        functools.partial(plain_kernel, len(sources), first), "times", z,
        [x], [by_row(512, width)], [sources],
        [jax.ShapeDtypeStruct((rows, cols), bf16)], [by_row(512, cols)], [],
        rows // 512, 2 * rows * width * cols, [(width, cols)],
    )[0]


def to_features(z, a, a_sources, first, b, b_sources, half, width):
    rows = a.shape[0]
    slots = rows // (2 * half)
    a_cols, b_cols = a.shape[1], b.shape[1]
    out = jax.ShapeDtypeStruct((slots, half, width), bf16)
    spec = pl.BlockSpec((1, half, width), lambda i, *_: (i, 0, 0))
    return blocks_call(
        functools.partial(spread_kernel, len(a_sources), first), "to_features", z,
        [a, b], [by_row(2 * half, a_cols), by_row(2 * half, b_cols)], [a_sources, b_sources],
        [out, out], [spec, spec], [],
        slots, 2 * rows * width * (a_cols + b_cols), [(width, a_cols), (width, b_cols)],
    )


def attend(heads, low, packed, vt, pcol, start, qmask):
    rows, wide = packed.shape[0], heads * HEAD
    pairs = (rows // BLOCK) * 4 * heads * BLOCK * BLOCK
    return pl.pallas_call(
        functools.partial(forward_kernel, heads),
        grid_spec=pltpu.PrefetchScalarGridSpec(
            num_scalar_prefetch=1,
            grid=(),
            in_specs=whole(5),
            out_specs=whole(3),
            scratch_shapes=[pltpu.VMEM((rows, wide), bf16)],
        ),
        out_shape=[
            jax.ShapeDtypeStruct((wide, rows), f32),
            jax.ShapeDtypeStruct((8, rows), f32),
            jax.ShapeDtypeStruct((rows, wide), bf16),
        ],
        compiler_params=pltpu.CompilerParams(vmem_limit_bytes=40 * 2**20),
        cost_estimate=pl.CostEstimate(
            flops=2 * rows * rows * wide + pairs * 4 * wide, bytes_accessed=20 * rows * wide, transcendentals=pairs
        ),
        name="attend_forward",
    )(low, packed, vt, pcol, start, qmask)


def attend_back(heads, low, packed, outt, lse, grad, cosine, sine, prow, pcol, start, qmask, vmask, ktmask):
    rows, wide = grad.shape
    pairs = (rows // BLOCK) * 4 * heads * BLOCK * BLOCK
    return pl.pallas_call(
        functools.partial(backward_kernel, heads),
        grid_spec=pltpu.PrefetchScalarGridSpec(
            num_scalar_prefetch=1,
            grid=(),
            in_specs=whole(12),
            out_specs=whole(2),
            scratch_shapes=[
                pltpu.VMEM((wide, rows), bf16),
                pltpu.VMEM((rows, wide), f32),
                pltpu.VMEM((rows, wide), f32),
                pltpu.VMEM((rows, wide), f32),
                pltpu.VMEM((rows, 3 * wide), bf16),
            ],
        ),
        out_shape=[
            jax.ShapeDtypeStruct((rows, 3 * wide), bf16),
            jax.ShapeDtypeStruct((8, 3 * wide), f32),
        ],
        compiler_params=pltpu.CompilerParams(vmem_limit_bytes=40 * 2**20),
        cost_estimate=pl.CostEstimate(
            flops=8 * rows * rows * wide + pairs * 10 * wide, bytes_accessed=20 * rows * wide, transcendentals=pairs
        ),
        name="attend_backward",
    )(low, packed, outt, lse, grad, cosine, sine, prow, pcol, start, qmask, vmask, ktmask)


def shards(
    hidden_in,
    out_grad,
    ln_gain,
    ln_bias,
    w_qkv,
    b_qkv,
    w_dense,
    b_dense,
    w_fc1,
    b_fc1,
    w_fc2,
    b_fc2,
    lengths,
    assignment,
):
    n = lax.axis_size("fsdp")
    m = lax.axis_size("ctx")
    z = lax.axis_index("fsdp")
    c = lax.axis_index("ctx")
    t = lax.axis_index("tp")
    rows, width = hidden_in.shape[1], hidden_in.shape[2]
    half = rows // 2
    group_rows = rows * m
    feat = width // n
    heads = w_qkv.shape[1] // (3 * HEAD) // m
    wide = heads * HEAD
    by_columns = (((1,), (1,)), ((), ()))
    by_rows = (((0,), (0,)), ((), ()))

    def turn(x):
        return jnp.concatenate(
            [lax.dynamic_slice_in_dim(x, lax.rem(z - s + n, n) * feat, feat, axis=1) for s in range(n)],
            axis=1,
        )

    def mine(weight):
        share = weight.shape[-1] // m
        return lax.dynamic_slice_in_dim(weight, c * share, share, axis=weight.ndim - 1)

    listed = jnp.array(column_order(heads), jnp.int32)
    place_of = (jnp.arange(3 * wide, dtype=jnp.int32)[:, None] == listed[None, :]).astype(bf16)
    qkv_own = jnp.dot(mine(w_qkv), place_of, preferred_element_type=f32).astype(bf16)
    qkv_bias = jnp.dot(mine(b_qkv)[None], place_of, preferred_element_type=f32)
    up_bias = mine(b_fc1).astype(f32)

    order = Order()
    z_ref = jnp.full((1,), z, jnp.int32)
    first = Gather(jnp.concatenate([qkv_own, mine(w_dense)], axis=1))
    first.start()

    at = jnp.stack([z, t]).astype(jnp.int32)
    gain_vec = ln_gain.astype(f32)
    shift_vec = ln_bias.astype(f32)
    gain_row = jnp.broadcast_to(gain_vec[None], (8, width))
    shift_row = jnp.broadcast_to(shift_vec[None], (8, width))
    normed_own = prepare(True, at, after(hidden_in[0], first.ups[0]), gain_row, shift_row, n)[0]
    order.did(normed_own)
    rows_in = Rows(normed_own)
    rows_in.start()
    first.arrive(order)
    first.start()
    grads_own, out_sum = prepare(False, at, order.then(out_grad[0]), gain_row, shift_row, n)
    order.did(grads_own)
    assignment, lengths, w_fc1, w_fc2 = order.then((assignment, lengths, w_fc1, w_fc2))
    second = Gather(mine(w_fc1))
    third = Gather(mine(w_fc2))

    block_of = [((c ^ j) * 2 + (t ^ h)) * half for j in range(m) for h in range(2)]
    packed = jnp.concatenate(
        [lax.dynamic_slice_in_dim(assignment[0], at, half) for at in block_of]
    )
    split = ROT // 2 * heads
    slab = 2 * split if 2 * split % 128 == 0 else wide
    lane = jnp.arange(wide)
    lane_head = jnp.where(lane < 2 * split, (lane % split) // (ROT // 2), (lane - 2 * split) // (HEAD - ROT))
    exponent = (lane[:slab] % (ROT // 2)).astype(f32) * 2.0 / ROT
    frequency = jnp.where(lane[:slab] < 2 * split, jnp.power(10000.0, -exponent), 0.0)
    sign = jnp.where(lane[:slab] < split, -1.0, 1.0)

    def tables(place):
        angles = place.astype(f32)[:, None] * frequency[None, :]
        return jnp.cos(angles), jnp.sin(angles) * sign[None, :]

    ordered = jnp.arange(group_rows, dtype=jnp.int32)
    place_packed = positions(ordered, lengths[0])[1]
    start = ordered - place_packed
    low = start[::BLOCK] // BLOCK
    start = start[None]
    cos_arrival, sin_arrival = tables(positions(packed, lengths[0])[1])
    cos_packed, sin_packed = tables(place_packed)
    prow, pcol = packed[None], packed[:, None]
    head_qk = (lane_head[None] == jnp.arange(heads)[:, None]).astype(bf16)
    head_v = ((lane // HEAD)[None] == jnp.arange(heads)[:, None]).astype(bf16)
    qmask = jnp.broadcast_to(head_qk[:, None, :], (heads, BLOCK, wide))
    vmask = jnp.broadcast_to(head_v[:, None, :], (heads, BLOCK, wide))
    ktmask = jnp.broadcast_to(head_qk[:, :, None], (heads, wide, BLOCK))

    order.did(second.ups[0], third.ups[0], cos_arrival, sin_arrival, cos_packed, sin_packed)
    first.arrive(order)
    rows_in.arrive(order)

    first.start()
    rows_in.start_far()
    first.arrive(order)
    rows_in.arrive_far(order)
    first.rest(order)

    second.start()
    rows_in.start_last()
    rows_grad = Rows(order.then(grads_own))
    rows_grad.start()
    rows_in.arrive_last(order)
    normed = assemble(order.then(rows_in.blocks()))
    order.did(normed)
    qkv_bias = jnp.broadcast_to(qkv_bias, (8, 3 * wide))
    qkv_packed, vt = pack(
        heads, z_ref, order.then(normed), qkv_bias, cos_arrival, sin_arrival, prow, first.sources()
    )
    order.did(qkv_packed)
    second.arrive(order)
    rows_grad.arrive(order)

    second.start()
    rows_grad.start_far()
    outt, lse, mixed = attend(heads, low, order.then(qkv_packed), vt, pcol, start, qmask)
    order.did(mixed)
    second.arrive(order)
    rows_grad.arrive_far(order)

    second.start()
    rows_grad.start_last()
    rows_grad.arrive_last(order)
    grads = assemble(order.then(rows_grad.blocks()))
    order.did(grads)
    mixed_grad = times(z_ref, order.then(grads), first.sources(), 3 * wide, wide)
    order.did(mixed_grad)
    dense_grad = lax.dot_general(grads, order.then(mixed), by_rows, preferred_element_type=f32).astype(bf16)
    order.did(dense_grad)
    second.arrive(order)
    second.rest(order)

    third.start()
    up_bias = jnp.broadcast_to(up_bias[None], (8, up_bias.shape[0]))
    up, act = up_forward(z_ref, order.then(normed), up_bias, second.sources())
    order.did(act)
    down_grad = lax.dot_general(grads, order.then(act), by_rows, preferred_element_type=f32).astype(bf16)
    down_sum = Scatter([down_grad[s * feat : (s + 1) * feat] for s in range(n)])
    order.did(*down_sum.parts)
    third.arrive(order)

    third.start()
    down_sum.start()
    qkv_grad_low, qkv_bias_sum = attend_back(
        heads, low, order.then(qkv_packed), outt, lse, mixed_grad, cos_packed, sin_packed, prow, pcol, start,
        qmask, vmask, ktmask,
    )
    order.did(qkv_grad_low)
    third.arrive(order)
    down_sum.arrive(order)

    third.start()
    down_sum.start()
    qkv_weight = lax.dot_general(
        normed, order.then(qkv_grad_low), by_rows, preferred_element_type=f32
    ).astype(bf16)
    first_sum = Scatter(
        [
            jnp.concatenate([x[s * feat : (s + 1) * feat] for x in (qkv_weight, dense_grad)], axis=1)
            for s in range(n)
        ]
    )
    order.did(*first_sum.parts)
    third.arrive(order)
    down_sum.arrive(order)
    third.rest(order)

    down_sum.start()
    first_sum.start()
    branch_keep, branch_send = to_features(
        z_ref, order.then(mixed), first.sources(), 3 * wide, act, third.sources(), half, width
    )
    order.did(branch_keep)
    branch_other = swap(branch_send, "tp", 1)
    up_grad_low, up_bias_sum = up_backward(z_ref, grads, order.then(up), third.sources())
    order.did(up_grad_low)
    down_sum.arrive(order)
    first_sum.arrive(order)
    branch_keep, branch_other = order.arrive((branch_keep, branch_other))
    down_sum.rest(order)

    first_sum.start()
    branch_sum = RowSums(add(branch_keep, branch_other))
    branch_sum.start()
    up_weight = lax.dot_general(
        normed, order.then(up_grad_low), by_rows, preferred_element_type=f32
    ).astype(bf16)
    up_sum = Scatter([up_weight[s * feat : (s + 1) * feat] for s in range(n)])
    order.did(*up_sum.parts)
    first_sum.arrive(order)
    branch_sum.arrive(order)

    first_sum.start()
    up_sum.start()
    branch_sum.start_last()
    keep, send = to_features(
        z_ref, order.then(qkv_grad_low), first.sources(), 0, up_grad_low, second.sources(), half, width
    )
    order.did(keep)
    other = swap(send, "tp", 1)
    up_sum.arrive(order)
    first_sum.arrive(order)
    branch_sum.arrive_last(order)
    keep, other = order.arrive((keep, other))
    first_sum.rest(order)

    up_sum.start()
    row_sum = RowSums(add(keep, other))
    row_sum.start()
    down_pieces = spread_start(order.then(down_sum.total()))
    branch = turn(branch_sum.total())
    source = lax.dynamic_slice_in_dim(hidden_in[0], t * half, half).astype(f32)
    biases = b_dense.astype(f32) + b_fc2.astype(f32)
    result = (source + branch + biases).astype(bf16)
    first_total = first_sum.total()
    qkv_sum = lax.dot_general(
        first_total[:, : 3 * wide], place_of, by_columns, preferred_element_type=f32
    ).astype(bf16)
    first_total = jnp.concatenate([qkv_sum, first_total[:, 3 * wide :]], axis=1)
    order.did(result, first_total)
    up_sum.arrive(order)
    row_sum.arrive(order)
    down_pieces = order.arrive(down_pieces)

    up_sum.start()
    row_sum.start_last()
    result_other = swap(order.then(result), "tp", 1)
    qkv_pieces = spread_start(order.then(first_total))
    down_part = side_by_side(down_pieces)
    centred = order.then(source)
    centred = centred - jnp.mean(centred, axis=-1, keepdims=True)
    rstd = lax.rsqrt(jnp.mean(centred * centred, axis=-1, keepdims=True) + EPSILON)
    xhat = centred * rstd
    order.did(down_part, xhat)
    row_sum.arrive_last(order)
    up_sum.arrive(order)
    up_sum.rest(order)
    result_other, qkv_pieces = order.arrive((result_other, qkv_pieces))

    up_pieces = spread_start(order.then(up_sum.total()))
    normed_grad = turn(row_sum.total())
    d = normed_grad * gain_vec
    input_grad = rstd * (
        d - jnp.mean(d, axis=-1, keepdims=True) - xhat * jnp.mean(d * xhat, axis=-1, keepdims=True)
    ) + lax.dynamic_slice_in_dim(out_grad[0], t * half, half).astype(f32)
    input_other = swap(input_grad, "tp", 1)
    norm_sums = jnp.concatenate([jnp.sum(normed_grad * xhat, axis=0), jnp.sum(normed_grad, axis=0)])
    order.did(input_grad, norm_sums)
    qkv_part = side_by_side([x[:, : 3 * wide] for x in qkv_pieces])
    dense_part = side_by_side([x[:, 3 * wide :] for x in qkv_pieces])
    up_part = side_by_side(up_pieces)

    def in_rows(own_half, other_half):
        return jnp.concatenate(
            [jnp.where(t == 0, own_half, other_half), jnp.where(t == 0, other_half, own_half)], axis=0
        )

    result = in_rows(result, result_other)
    input_grad = in_rows(input_grad, input_other)
    def placed(vector):
        full = jnp.zeros((vector.shape[0] * m,), f32)
        return lax.dynamic_update_slice_in_dim(full, vector, c * vector.shape[0], axis=0)

    qkv_bias_grad = lax.dot_general(
        qkv_bias_sum[:1], place_of.astype(f32), by_columns,
        precision=lax.Precision.HIGHEST, preferred_element_type=f32,
    )[0]
    norm_sums = norm_sums + swap(norm_sums, "tp", 1)
    sums = everywhere(
        jnp.concatenate([norm_sums, out_sum[0], placed(qkv_bias_grad), placed(up_bias_sum[0])]), "ctx", "fsdp"
    )
    gain_grad, shift_grad, out_bias_grad = sums[:width], sums[width : 2 * width], sums[2 * width : 3 * width]
    qkv_bias_grad = sums[3 * width : 3 * width + 3 * wide * m]
    up_bias_grad = sums[3 * width + 3 * wide * m :]
    return (
        result[None],
        input_grad[None],
        gain_grad,
        shift_grad,
        qkv_part,
        qkv_bias_grad,
        dense_part,
        out_bias_grad,
        up_part,
        up_bias_grad,
        down_part,
        out_bias_grad,
    )


def solution(mesh):
    in_specs = (
        P("fsdp", "ctx", None),
        P("fsdp", "ctx", None),
        P(),
        P(),
        P("fsdp", "tp"),
        P("tp"),
        P("fsdp", "tp"),
        P(),
        P("fsdp", "tp"),
        P("tp"),
        P("fsdp", "tp"),
        P(),
        P("fsdp", None),
        P("fsdp", None),
    )
    out_specs = (
        P("fsdp", "ctx", None),
        P("fsdp", "ctx", None),
        P(),
        P(),
        P(("fsdp", "ctx"), "tp"),
        P("tp"),
        P(("fsdp", "ctx"), "tp"),
        P(),
        P(("fsdp", "ctx"), "tp"),
        P("tp"),
        P(("fsdp", "ctx"), "tp"),
        P(),
    )
    return jax.shard_map(shards, mesh=mesh, in_specs=in_specs, out_specs=out_specs, check_vma=False)
```

```python
import functools
import math

import jax
import jax.numpy as jnp
from jax import lax
from jax.experimental import pallas as pl
from jax.experimental.pallas import tpu as pltpu
from jax.sharding import PartitionSpec as P

HEAD = 64
ROT = 32
MASKED = -1e30
EPSILON = 1e-05
f32 = jnp.float32
bf16 = jnp.bfloat16


def positions(packed, lengths):
    seq_ends = jnp.cumsum(lengths)
    starts = seq_ends - lengths
    segment = jnp.sum((packed[:, None] >= seq_ends[None, :]).astype(jnp.int32), axis=1)
    owner_mask = segment[:, None] == jnp.arange(lengths.shape[0], dtype=jnp.int32)[None, :]
    return (segment, packed - jnp.sum(jnp.where(owner_mask, starts[None, :], 0), axis=1))


def gelu_tanh(values):
    return jax.nn.gelu(values, approximate=True)


def swap(x, axis, bit):
    size = lax.axis_size(axis)
    return lax.ppermute(x, axis, [(i, i ^ bit) for i in range(size)])


def everywhere(x, *axes):
    for axis in axes:
        bit = 1
        while bit < lax.axis_size(axis):
            x = x + swap(x, axis, bit)
            bit *= 2
    return x


def after(x, *before):
    before = [item for item in before if item is not None]
    return lax.optimization_barrier((x, *before))[0] if before else x


class Order:
    def __init__(self):
        self.last = ()

    def then(self, x):
        return after(x, *self.last)

    def did(self, *values):
        self.last = values

    def arrive(self, values):
        values = after(values, *self.last)
        self.last = self.last + tuple(jax.tree.leaves(values))
        return values


def line_up(x, first, last):
    return lax.ppermute(x, "fsdp", [(i, i + 1) for i in range(first, last)])


def line_down(x, first, last):
    return lax.ppermute(x, "fsdp", [(i, i - 1) for i in range(first, last)])


class Gather:
    def __init__(self, own):
        self.ups, self.downs = [own], [own]

    def start(self, order):
        n, s = lax.axis_size("fsdp"), len(self.ups)
        if s < n:
            up, down = order.then((self.ups[-1], self.downs[-1]))
            self.ups.append(line_up(up, s - 1, n - 1))
            self.downs.append(line_down(down, 1, n - s + 1))

    def arrive(self, order):
        self.ups[-1], self.downs[-1] = order.arrive((self.ups[-1], self.downs[-1]))

    def rest(self, order):
        for _ in range(len(self.ups), lax.axis_size("fsdp")):
            self.start(order)
            self.arrive(order)

    def sources(self):
        return self.ups + self.downs[1:]


class Scatter:
    def __init__(self, parts):
        self.parts, self.sums, self.step = parts, None, 1

    def start(self, order):
        n, s = lax.axis_size("fsdp"), self.step
        if s < n:
            up, down = order.then((self.parts[s], self.parts[n - s]))
            if self.sums is not None:
                up, down = order.arrive((add(up, self.sums[0]), add(down, self.sums[1])))
            self.sums = line_up(up, 0, min(s, n - 1)), line_down(down, max(n - s, 1), n)
            self.step += 1

    def arrive(self, order):
        self.sums = order.arrive(self.sums)

    def rest(self, order):
        for _ in range(self.step, lax.axis_size("fsdp")):
            self.start(order)
            self.arrive(order)

    def total(self):
        up, down = self.sums
        return (self.parts[0].astype(f32) + up.astype(f32) + down.astype(f32)).astype(bf16)


class Rows:
    def __init__(self, mine):
        self.mine = mine

    def start(self, order):
        mine = order.then(self.mine)
        self.near = [swap(mine, "ctx", 1 << k) for k in range(lax.axis_size("ctx").bit_length() - 1)]

    def arrive(self, order):
        self.near = order.arrive(self.near)

    def start_far(self):
        m, quarter = lax.axis_size("ctx"), self.mine.shape[0] // 2
        if m == 4:
            first, second = self.near
            self.far = [swap(first[:quarter], "ctx", 2), swap(second[quarter:], "ctx", 1)]
        else:
            self.far = [swap(self.mine, "ctx", j) for j in range(1, m) if j & (j - 1)]

    def arrive_far(self, order):
        self.far = order.arrive(self.far)

    def halves(self, order):
        m = lax.axis_size("ctx")
        near, far = list(self.near), list(self.far)
        blocks = [self.mine]
        for j in range(1, m):
            if j & (j - 1) == 0:
                blocks.append(near.pop(0))
            elif m == 4:
                blocks += far
            else:
                blocks.append(far.pop(0))
        self.here = assemble(order.then(blocks))
        order.did(self.here)

    def start_last(self, order):
        self.there = swap(order.then(self.here), "tp", 1)

    def arrive_last(self, order):
        self.there = order.arrive(self.there)

    def all(self, order):
        full = assemble(order.then([self.here, self.there]))
        order.did(full)
        return full


class RowSums:
    def __init__(self, slots):
        self.slots = [slots[j] for j in range(slots.shape[0])]

    def start(self, order):
        m, slots = len(self.slots), order.then(self.slots)
        quarter = slots[0].shape[0] // 2
        if m == 4:
            self.got = [swap(slots[3][:quarter], "ctx", 2), swap(slots[3][quarter:], "ctx", 1)]
        else:
            self.got = [swap(slots[j], "ctx", j) for j in range(1, m) if j & (j - 1)]

    def arrive(self, order):
        self.got = order.arrive(self.got)

    def start_last(self, order):
        m, slots = len(self.slots), order.then(self.slots)
        quarter = slots[0].shape[0] // 2
        if m == 4:
            first = jnp.concatenate([add(slots[1][:quarter], self.got[0]), slots[1][quarter:]], axis=0)
            second = jnp.concatenate([slots[2][:quarter], add(slots[2][quarter:], self.got[1])], axis=0)
            first, second = order.arrive((first, second))
            self.last, self.got = [swap(first, "ctx", 1), swap(second, "ctx", 2)], []
        else:
            self.last = [swap(slots[j], "ctx", j) for j in range(1, m) if j & (j - 1) == 0]

    def arrive_last(self, order):
        self.last, self.slots[0] = order.arrive((self.last, self.slots[0]))

    def total(self):
        return sum((x.astype(f32) for x in self.got + self.last), self.slots[0].astype(f32))


def add(a, b):
    return (a.astype(f32) + b.astype(f32)).astype(bf16)


def spread_start(block):
    m = lax.axis_size("ctx")
    c = lax.axis_index("ctx")
    rows = block.shape[0] // m
    pieces = []
    for j in range(m):
        piece = lax.dynamic_slice_in_dim(block, (c ^ j) * rows, rows, axis=0)
        pieces.append(piece if j == 0 else swap(piece, "ctx", j))
    return pieces


def column_order(heads):
    order = []
    for part in range(2):
        for start, width in ((0, ROT // 2), (ROT // 2, ROT // 2), (ROT, HEAD - ROT)):
            for head in range(heads):
                base = (head * 3 + part) * HEAD + start
                order += list(range(base, base + width))
    for head in range(heads):
        base = (head * 3 + 2) * HEAD
        order += list(range(base, base + HEAD))
    return order


BLOCK = 256
NT = (((1,), (1,)), ((), ()))


def mm(a, b, dims=(((1,), (0,)), ((), ()))):
    return lax.dot_general(a, b, dims, preferred_element_type=f32)


def turned(x, cosine, sine, split):
    slab = cosine.shape[1]
    front = x[:, :slab]
    if slab == 2 * split:
        partner = pltpu.roll(front, split, 1)
    else:
        lane = lax.broadcasted_iota(jnp.int32, front.shape, 1)
        partner = jnp.where(
            lane < split, pltpu.roll(front, slab - split, 1), pltpu.roll(front, split, 1)
        )
    front = front * cosine + partner * sine
    if slab == x.shape[1]:
        return front
    return jnp.concatenate([front, x[:, slab:]], axis=1)


def to_packed(prow_ref, block, data):
    shape = (BLOCK, prow_ref.shape[1])
    at = lax.broadcasted_iota(jnp.int32, shape, 0) + block * BLOCK
    return mm((at == prow_ref[...]).astype(f32).astype(bf16), data)


def to_arrival(pcol_ref, block, data):
    rows = pl.ds(pl.multiple_of(block * BLOCK, BLOCK), BLOCK)
    shape = (BLOCK, data.shape[0])
    at = lax.broadcasted_iota(jnp.int32, shape, 1)
    return mm((at == pcol_ref[rows, :]).astype(f32).astype(bf16), data)


def kept(i, j, start):
    keys = lax.broadcasted_iota(jnp.int32, (BLOCK, BLOCK), 0) + j * BLOCK
    queries = lax.broadcasted_iota(jnp.int32, (BLOCK, BLOCK), 1) + i * BLOCK
    return (keys >= start) & (keys <= queries)


def fetch(z_ref, sources, weight_ref, sems, first):
    feat, cols = sources[0].shape[0], weight_ref.shape[1]
    if len(sources) == 1:
        feat = weight_ref.shape[0] // sems.shape[0]
    n = weight_ref.shape[0] // feat

    def copy(source, s):
        rows = pl.ds(s * feat, feat)
        return pltpu.make_async_copy(
            source.at[:, pl.ds(first, cols)], weight_ref.at[rows, :], sems.at[s]
        )

    def each(do):
        if len(sources) == 1:
            for s in range(n):
                block = pl.multiple_of(lax.rem(z_ref[0] - s + n, n) * feat, feat)
                do(copy(sources[0].at[pl.ds(block, feat), :], s))
            return
        do(copy(sources[0], 0))
        for s in range(1, n):

            @pl.when(z_ref[0] >= s)
            def _():
                do(copy(sources[s], s))

            @pl.when(z_ref[0] < s)
            def _():
                do(copy(sources[2 * n - 1 - s], s))

    each(lambda c: c.start())
    each(lambda c: c.wait())


def pack_kernel(heads, count, z_ref, x_in_ref, bias_ref, cos_ref, sin_ref, prow_ref, *rest):
    sources, (packed_ref, vt_ref, x_ref, weight_ref, sems) = rest[:count], rest[count:]
    wide = vt_ref.shape[0]
    blocks = x_ref.shape[0] // BLOCK
    split = ROT // 2 * heads
    r = pl.program_id(0)

    @pl.when(r == 0)
    def _():
        fetch(z_ref, sources, weight_ref, sems, 0)

    rows = pl.ds(pl.multiple_of(r * BLOCK, BLOCK), BLOCK)
    cosine, sine = cos_ref[rows, :], sin_ref[rows, :]
    x_in = x_in_ref[...]
    for part in range(3):
        at = slice(part * wide, (part + 1) * wide)
        x = mm(x_in, weight_ref[:, at]) + bias_ref[0:1, at]
        if part < 2:
            x = turned(x, cosine, sine, split)
        if part == 0:
            x = x * (1.0 / math.sqrt(HEAD))
        x_ref[rows, at] = x.astype(bf16)

    @pl.when(r == blocks - 1)
    def _():
        @pl.loop(0, blocks)
        def _(p):
            rows = pl.ds(pl.multiple_of(p * BLOCK, BLOCK), BLOCK)
            y = to_packed(prow_ref, p, x_ref[...])
            packed_ref[rows, :] = y.astype(bf16)
            vt_ref[:, rows] = y[:, 2 * wide :].T.astype(bf16)


def curve(u):
    square = u * u
    return jnp.tanh(math.sqrt(2.0 / math.pi) * (u + 0.044715 * (square * u))), square


def up_kernel(count, z_ref, x_ref, bias_ref, *rest):
    sources, (up_ref, act_ref, weight_ref, sems) = rest[:count], rest[count:]

    @pl.when(pl.program_id(0) == 0)
    def _():
        fetch(z_ref, sources, weight_ref, sems, 0)

    x = x_ref[...]
    step = min(256, up_ref.shape[1])
    for at in range(0, up_ref.shape[1], step):
        at = slice(at, at + step)
        u = mm(x, weight_ref[:, at]) + bias_ref[0:1, at]
        up_ref[:, at] = u
        act_ref[:, at] = (0.5 * u * (1.0 + curve(u)[0])).astype(bf16)


def up_back_kernel(count, z_ref, x_ref, up_ref, *rest):
    sources, (grad_ref, sum_ref, weight_ref, sems) = rest[:count], rest[count:]

    @pl.when(pl.program_id(0) == 0)
    def _():
        fetch(z_ref, sources, weight_ref, sems, 0)
        sum_ref[...] = jnp.zeros(sum_ref.shape, f32)

    x = x_ref[...]
    step = min(256, grad_ref.shape[1])
    for at in range(0, grad_ref.shape[1], step):
        at = slice(at, at + step)
        u = up_ref[:, at]
        bend, square = curve(u)
        slope = 0.5 * (1.0 + bend) + (0.5 * math.sqrt(2.0 / math.pi)) * u * (
            (1.0 - bend * bend) * (1.0 + (3.0 * 0.044715) * square)
        )
        grad = mm(x, weight_ref[:, at]) * slope
        grad_ref[:, at] = grad.astype(bf16)
        sum_ref[0:1, at] = sum_ref[0:1, at] + jnp.sum(grad, axis=0, keepdims=True)


def plain_kernel(count, first, z_ref, x_ref, *rest):
    sources, (out_ref, weight_ref, sems) = rest[:count], rest[count:]

    @pl.when(pl.program_id(0) == 0)
    def _():
        fetch(z_ref, sources, weight_ref, sems, first)

    out_ref[...] = mm(x_ref[...], weight_ref[...]).astype(bf16)


def spread_kernel(count, first, z_ref, a_ref, b_ref, *rest):
    a_sources, b_sources = rest[: count[0]], rest[count[0] : sum(count)]
    keep_ref, send_ref, a_weight_ref, b_weight_ref, sems = rest[sum(count) :]

    @pl.when(pl.program_id(0) == 0)
    def _():
        fetch(z_ref, a_sources, a_weight_ref, sems, first)
        fetch(z_ref, b_sources, b_weight_ref, sems, 0)

    slots, half, width = keep_ref.shape
    steps = pl.num_programs(0) // 2

    def write(out_ref):
        for slot in range(slots):
            rows = slice(slot * half, (slot + 1) * half)
            a, b = a_ref[rows, :], b_ref[rows, :]
            for at in range(0, width, 256):
                at = slice(at, at + 256)
                out = mm(a, a_weight_ref[at, :], NT) + mm(b, b_weight_ref[at, :], NT)
                out_ref[slot, :, at] = out.astype(bf16)

    @pl.when(pl.program_id(0) < steps)
    def _():
        write(keep_ref)

    @pl.when(pl.program_id(0) >= steps)
    def _():
        write(send_ref)


def forward_kernel(
    heads, low_ref, packed_ref, vt_ref, pcol_ref, start_ref, qmask_ref,
    outt_ref, lse_ref, mixed_ref, mp_ref,
):
    rows_all, wide = mixed_ref.shape
    blocks = rows_all // BLOCK

    @pl.loop(0, blocks)
    def _(i):
        rows = pl.ds(pl.multiple_of(i * BLOCK, BLOCK), BLOCK)
        start = start_ref[0:1, rows]
        q = packed_ref[rows, :wide]
        qs = jnp.concatenate([q * qmask_ref[h] for h in range(heads)], axis=0)

        def step(j, carried):
            keys = pl.ds(pl.multiple_of(j * BLOCK, BLOCK), BLOCK)
            k = packed_ref[keys, wide : 2 * wide]
            keep = kept(i, j, start)
            scores = mm(k, qs, NT)
            after = []
            for h in range(heads):
                top, total, acc = carried[h]
                s = jnp.where(keep, scores[:, h * BLOCK : (h + 1) * BLOCK], MASKED)
                new_top = jnp.maximum(top, jnp.max(s, axis=0, keepdims=True))
                p = jnp.exp(s - new_top)
                alpha = jnp.exp(top - new_top)
                total = total * alpha + jnp.sum(p, axis=0, keepdims=True)
                acc = acc * alpha + mm(vt_ref[h * HEAD : (h + 1) * HEAD, keys], p.astype(bf16))
                after.append((new_top, total, acc))
            return tuple(after)

        begin = tuple(
            (
                jnp.full((1, BLOCK), MASKED, f32),
                jnp.zeros((1, BLOCK), f32),
                jnp.zeros((HEAD, BLOCK), f32),
            )
            for _ in range(heads)
        )
        state = lax.fori_loop(low_ref[i], i + 1, step, begin)
        out = jnp.concatenate([acc / total for _, total, acc in state], axis=0)
        outt_ref[:, rows] = out
        mp_ref[rows, :] = out.T.astype(bf16)
        lse = [top + jnp.log(total) for top, total, _ in state]
        lse_ref[:, rows] = jnp.concatenate(lse + [jnp.zeros((8 - heads, BLOCK), f32)], axis=0)

    @pl.loop(0, blocks)
    def _(r):
        rows = pl.ds(pl.multiple_of(r * BLOCK, BLOCK), BLOCK)
        mixed_ref[rows, :] = to_arrival(pcol_ref, r, mp_ref[...]).astype(bf16)


def backward_kernel(
    heads, low_ref, packed_ref, outt_ref, lse_ref, grad_ref, cos_ref, sin_ref, prow_ref, pcol_ref, start_ref,
    qmask_ref, vmask_ref, ktmask_ref,
    qkv_grad_ref, bias_grad_ref, kt_ref, dk_ref, dv_ref, dq_ref, gp_ref,
):
    rows_all, wide = grad_ref.shape
    blocks = rows_all // BLOCK
    split = ROT // 2 * heads

    @pl.loop(0, blocks)
    def _(p):
        rows = pl.ds(pl.multiple_of(p * BLOCK, BLOCK), BLOCK)
        gp_ref[rows, :wide] = to_packed(prow_ref, p, grad_ref[...]).astype(bf16)
        kt_ref[:, rows] = packed_ref[rows, wide : 2 * wide].astype(f32).T.astype(bf16)
        dk_ref[rows, :] = jnp.zeros((BLOCK, wide), f32)
        dv_ref[rows, :] = jnp.zeros((BLOCK, wide), f32)

    @pl.loop(0, blocks)
    def _(i):
        rows = pl.ds(pl.multiple_of(i * BLOCK, BLOCK), BLOCK)
        start = start_ref[0:1, rows]
        q = packed_ref[rows, :wide]
        g = gp_ref[rows, :wide]
        qs = jnp.concatenate([q * qmask_ref[h] for h in range(heads)], axis=0)
        gs = jnp.concatenate([g * vmask_ref[h] for h in range(heads)], axis=0)
        product = g.astype(f32).T * outt_ref[:, rows]
        inner = [
            jnp.sum(product[h * HEAD : (h + 1) * HEAD], axis=0, keepdims=True) for h in range(heads)
        ]
        lse = [lse_ref[h : h + 1, rows] for h in range(heads)]

        def step(j, dqt):
            keys = pl.ds(pl.multiple_of(j * BLOCK, BLOCK), BLOCK)
            k = packed_ref[keys, wide : 2 * wide]
            v = packed_ref[keys, 2 * wide :]
            kt = kt_ref[:, keys]
            keep = kept(i, j, start)
            scores = mm(k, qs, NT)
            slopes = mm(v, gs, NT)
            probs, flows = [], []
            for h in range(heads):
                at = slice(h * BLOCK, (h + 1) * BLOCK)
                p = jnp.exp(jnp.where(keep, scores[:, at], MASKED) - lse[h])
                probs.append(p.astype(bf16))
                flows.append((p * (slopes[:, at] - inner[h])).astype(bf16))
            dv_ref[keys, :] = dv_ref[keys, :] + mm(jnp.concatenate(probs, axis=1), gs)
            dk_ref[keys, :] = dk_ref[keys, :] + mm(jnp.concatenate(flows, axis=1), qs)
            kts = jnp.concatenate([kt * ktmask_ref[h] for h in range(heads)], axis=1)
            return dqt + mm(kts, jnp.concatenate(flows, axis=0))

        dqt = lax.fori_loop(low_ref[i], i + 1, step, jnp.zeros((wide, BLOCK), f32))
        dq_ref[rows, :] = dqt.T * (1.0 / math.sqrt(HEAD))

    bias_grad_ref[...] = jnp.zeros(bias_grad_ref.shape, f32)

    @pl.loop(0, blocks)
    def _(p):
        rows = pl.ds(pl.multiple_of(p * BLOCK, BLOCK), BLOCK)
        cosine, sine = cos_ref[rows, :], -sin_ref[rows, :]
        dq = turned(dq_ref[rows, :], cosine, sine, split)
        dk = turned(dk_ref[rows, :], cosine, sine, split)
        full = jnp.concatenate([dq, dk, dv_ref[rows, :]], axis=1)
        bias_grad_ref[0:1, :] = bias_grad_ref[0:1, :] + jnp.sum(full, axis=0, keepdims=True)
        gp_ref[rows, :] = full.astype(bf16)

    @pl.loop(0, blocks)
    def _(r):
        rows = pl.ds(pl.multiple_of(r * BLOCK, BLOCK), BLOCK)
        qkv_grad_ref[rows, :] = to_arrival(pcol_ref, r, gp_ref[...]).astype(bf16)


def whole(count):
    return [pl.BlockSpec(memory_space=pltpu.VMEM)] * count


COST = 0.05


def blocks_call(kernel, name, z, ins, in_specs, sources, outs, out_specs, scratch, steps, flops, weight_shapes):
    sems = lax.axis_size("fsdp")
    return pl.pallas_call(
        kernel,
        grid_spec=pltpu.PrefetchScalarGridSpec(
            num_scalar_prefetch=1,
            grid=(steps,),
            in_specs=in_specs + [pl.BlockSpec(memory_space=pl.ANY)] * sum(map(len, sources)),
            out_specs=out_specs,
            scratch_shapes=scratch
            + [pltpu.VMEM(shape, bf16) for shape in weight_shapes]
            + [pltpu.SemaphoreType.DMA((sems,))],
        ),
        out_shape=outs,
        compiler_params=pltpu.CompilerParams(vmem_limit_bytes=48 * 2**20),
        cost_estimate=pl.CostEstimate(flops=int(COST * flops), bytes_accessed=2**20, transcendentals=0),
        name=name,
    )(z, *ins, *[x for group in sources for x in group])


def fixed(shape):
    return pl.BlockSpec(shape, lambda *_: (0,) * len(shape))


def by_row(rows, cols):
    return pl.BlockSpec((rows, cols), lambda i, *_: (i, 0))


def prepare_kernel(norm, slots, at_ref, x_ref, gain_ref, shift_ref, out_ref, *rest):
    rows, width = x_ref.shape
    half, step = rows // 2, 64
    feat = width // slots

    @pl.loop(0, half // step)
    def _(b):
        source = pl.ds(pl.multiple_of(at_ref[1] * half + b * step, step), step)
        target = pl.ds(pl.multiple_of(b * step, step), step)
        if norm:
            x = x_ref[source, :].astype(f32)
            mean = jnp.mean(x, axis=-1, keepdims=True)
            centred = x - mean
            rstd = lax.rsqrt(jnp.mean(centred * centred, axis=-1, keepdims=True) + EPSILON)
        for s in range(slots):
            block = lax.rem(at_ref[0] - s + slots, slots)
            columns = pl.ds(pl.multiple_of(block * feat, feat), feat)
            y = x_ref[source, columns]
            if norm:
                y = (y.astype(f32) - mean) * rstd * gain_ref[0:1, columns] + shift_ref[0:1, columns]
            out_ref[target, s * feat : (s + 1) * feat] = y.astype(bf16)

    if not norm:
        sum_ref = rest[0]
        sum_ref[...] = jnp.zeros(sum_ref.shape, f32)

        @pl.loop(0, rows // step)
        def _(b):
            source = pl.ds(pl.multiple_of(b * step, step), step)
            x = x_ref[source, :].astype(f32)
            sum_ref[0:1, :] = sum_ref[0:1, :] + jnp.sum(x, axis=0, keepdims=True)


def prepare(norm, at, x, gain, shift, n):
    rows, width = x.shape
    out = [jax.ShapeDtypeStruct((rows // 2, width), bf16)]
    if not norm:
        out.append(jax.ShapeDtypeStruct((8, width), f32))
    return pl.pallas_call(
        functools.partial(prepare_kernel, norm, n),
        grid_spec=pltpu.PrefetchScalarGridSpec(
            num_scalar_prefetch=1, grid=(), in_specs=whole(3), out_specs=whole(len(out))
        ),
        out_shape=out,
        compiler_params=pltpu.CompilerParams(vmem_limit_bytes=40 * 2**20),
        cost_estimate=pl.CostEstimate(flops=2**20, bytes_accessed=2**20, transcendentals=0),
        name="prepare",
    )(at, x, gain, shift)


def place_kernel(count, at_ref, *refs):
    pieces, outs = refs[:count], refs[count:]
    for j, piece in enumerate(pieces):
        first = 0
        for out_ref in outs:
            cols = out_ref.shape[1] // count
            target = pl.ds(pl.multiple_of((at_ref[0] ^ j) * cols, cols), cols)
            out_ref[:, target] = piece[:, first : first + cols].astype(f32)
            first += cols


def place(c, pieces, widths):
    count, rows = len(pieces), pieces[0].shape[0]
    return pl.pallas_call(
        functools.partial(place_kernel, count),
        grid_spec=pltpu.PrefetchScalarGridSpec(
            num_scalar_prefetch=1, grid=(), in_specs=whole(count), out_specs=whole(len(widths))
        ),
        out_shape=[jax.ShapeDtypeStruct((rows, count * cols), f32) for cols in widths],
        compiler_params=pltpu.CompilerParams(vmem_limit_bytes=40 * 2**20),
        cost_estimate=pl.CostEstimate(flops=2**20, bytes_accessed=2**20, transcendentals=0),
        name="place",
    )(c, *pieces)


def join_kernel(a_ref, b_ref, *outs):
    cols = a_ref.shape[1]
    for s, out_ref in enumerate(outs):

        @pl.when(pl.program_id(0) == s)
        def _():
            out_ref[:, :cols] = a_ref[...]
            out_ref[:, cols:] = b_ref[...]


def join(a, b, n):
    rows, cols = a.shape[0] // n, a.shape[1] + b.shape[1]
    return pl.pallas_call(
        join_kernel,
        grid=(n,),
        in_specs=[
            pl.BlockSpec((rows, a.shape[1]), lambda i: (i, 0)),
            pl.BlockSpec((rows, b.shape[1]), lambda i: (i, 0)),
        ],
        out_specs=[pl.BlockSpec((rows, cols), lambda i: (0, 0))] * n,
        out_shape=[jax.ShapeDtypeStruct((rows, cols), bf16)] * n,
        compiler_params=pltpu.CompilerParams(vmem_limit_bytes=40 * 2**20),
        cost_estimate=pl.CostEstimate(flops=2**20, bytes_accessed=2**20, transcendentals=0),
        name="join",
    )(a, b)


def reorder(order, x, blocks):
    rows, cols = x.shape[0] // blocks, x.shape[1]

    def copy_kernel(order_ref, x_ref, out_ref):
        out_ref[...] = x_ref[...]

    return pl.pallas_call(
        copy_kernel,
        grid_spec=pltpu.PrefetchScalarGridSpec(
            num_scalar_prefetch=1,
            grid=(blocks,),
            in_specs=[pl.BlockSpec((rows, cols), lambda i, order_ref: (order_ref[i], 0))],
            out_specs=pl.BlockSpec((rows, cols), lambda i, order_ref: (i, 0)),
        ),
        out_shape=jax.ShapeDtypeStruct(x.shape, x.dtype),
        compiler_params=pltpu.CompilerParams(vmem_limit_bytes=40 * 2**20),
        cost_estimate=pl.CostEstimate(flops=2**20, bytes_accessed=2**20, transcendentals=0),
        name="reorder",
    )(order, x)


def assemble_kernel(*refs):
    *pieces, out_ref, sems = refs

    def each(do):
        first = 0
        for k, piece in enumerate(pieces):
            count = piece.shape[0]
            do(pltpu.make_async_copy(piece, out_ref.at[pl.ds(first, count), :], sems.at[k]))
            first += count

    each(lambda copy: copy.start())
    each(lambda copy: copy.wait())


def assemble(pieces):
    rows = sum(piece.shape[0] for piece in pieces)
    return pl.pallas_call(
        assemble_kernel,
        in_specs=whole(len(pieces)),
        out_specs=pl.BlockSpec(memory_space=pl.ANY),
        scratch_shapes=[pltpu.SemaphoreType.DMA((len(pieces),))],
        out_shape=jax.ShapeDtypeStruct((rows, pieces[0].shape[1]), bf16),
        compiler_params=pltpu.CompilerParams(vmem_limit_bytes=40 * 2**20),
        cost_estimate=pl.CostEstimate(flops=2**20, bytes_accessed=2**20, transcendentals=0),
        name="assemble",
    )(*pieces)


def pack(heads, z, normed, bias, cosine, sine, prow, sources):
    rows, width = normed.shape
    wide = heads * HEAD
    slab = cosine.shape[1]
    return blocks_call(
        functools.partial(pack_kernel, heads, len(sources)), "pack", z,
        [normed, bias, cosine, sine, prow],
        [by_row(BLOCK, width), fixed(bias.shape), fixed((rows, slab)), fixed((rows, slab)), fixed(prow.shape)],
        [sources],
        [jax.ShapeDtypeStruct((rows, 3 * wide), bf16), jax.ShapeDtypeStruct((wide, rows), bf16)],
        [fixed((rows, 3 * wide)), fixed((wide, rows))],
        [pltpu.VMEM((rows, 3 * wide), bf16)],
        rows // BLOCK, 12 * rows * rows * wide, [(width, 3 * wide)],
    )


def up_forward(z, normed, bias, sources):
    rows, width = normed.shape
    cols = bias.shape[1]
    return blocks_call(
        functools.partial(up_kernel, len(sources)), "up", z,
        [normed, bias], [by_row(512, width), fixed(bias.shape)], [sources],
        [jax.ShapeDtypeStruct((rows, cols), f32), jax.ShapeDtypeStruct((rows, cols), bf16)],
        [by_row(512, cols), by_row(512, cols)], [],
        rows // 512, 2 * rows * width * cols, [(width, cols)],
    )


def up_backward(z, grads, up, sources):
    rows, width = grads.shape
    cols = up.shape[1]
    return blocks_call(
        functools.partial(up_back_kernel, len(sources)), "up_back", z,
        [grads, up], [by_row(512, width), by_row(512, cols)], [sources],
        [jax.ShapeDtypeStruct((rows, cols), bf16), jax.ShapeDtypeStruct((8, cols), f32)],
        [by_row(512, cols), fixed((8, cols))], [],
        rows // 512, 2 * rows * width * cols, [(width, cols)],
    )


def times(z, x, sources, first, cols):
    rows, width = x.shape
    return blocks_call(
        functools.partial(plain_kernel, len(sources), first), "times", z,
        [x], [by_row(512, width)], [sources],
        [jax.ShapeDtypeStruct((rows, cols), bf16)], [by_row(512, cols)], [],
        rows // 512, 2 * rows * width * cols, [(width, cols)],
    )[0]


def to_features(z, a, a_sources, first, b, b_sources, half, width):
    rows = a.shape[0]
    slots, each = rows // (2 * half), 512 // half
    steps = slots // each
    a_cols, b_cols = a.shape[1], b.shape[1]
    out = jax.ShapeDtypeStruct((slots, half, width), bf16)
    block = (each, half, width)
    return blocks_call(
        functools.partial(spread_kernel, (len(a_sources), len(b_sources)), first), "to_features", z,
        [a, b], [by_row(512, a_cols), by_row(512, b_cols)], [a_sources, b_sources],
        [out, out],
        [
            pl.BlockSpec(block, lambda i, *_: (jnp.minimum(i, steps - 1), 0, 0)),
            pl.BlockSpec(block, lambda i, *_: (jnp.maximum(i - steps, 0), 0, 0)),
        ],
        [], 2 * steps, 2 * rows * width * (a_cols + b_cols), [(width, a_cols), (width, b_cols)],
    )


def attend(heads, low, packed, vt, pcol, start, qmask):
    rows, wide = packed.shape[0], heads * HEAD
    pairs = (rows // BLOCK) * 4 * heads * BLOCK * BLOCK
    return pl.pallas_call(
        functools.partial(forward_kernel, heads),
        grid_spec=pltpu.PrefetchScalarGridSpec(
            num_scalar_prefetch=1,
            grid=(),
            in_specs=whole(5),
            out_specs=whole(3),
            scratch_shapes=[pltpu.VMEM((rows, wide), bf16)],
        ),
        out_shape=[
            jax.ShapeDtypeStruct((wide, rows), f32),
            jax.ShapeDtypeStruct((8, rows), f32),
            jax.ShapeDtypeStruct((rows, wide), bf16),
        ],
        compiler_params=pltpu.CompilerParams(vmem_limit_bytes=60 * 2**20),
        cost_estimate=pl.CostEstimate(
            flops=2 * rows * rows * wide + pairs * 4 * wide, bytes_accessed=20 * rows * wide, transcendentals=pairs
        ),
        name="attend_forward",
    )(low, packed, vt, pcol, start, qmask)


def attend_back(heads, low, packed, outt, lse, grad, cosine, sine, prow, pcol, start, qmask, vmask, ktmask):
    rows, wide = grad.shape
    pairs = (rows // BLOCK) * 4 * heads * BLOCK * BLOCK
    return pl.pallas_call(
        functools.partial(backward_kernel, heads),
        grid_spec=pltpu.PrefetchScalarGridSpec(
            num_scalar_prefetch=1,
            grid=(),
            in_specs=whole(12),
            out_specs=whole(2),
            scratch_shapes=[
                pltpu.VMEM((wide, rows), bf16),
                pltpu.VMEM((rows, wide), f32),
                pltpu.VMEM((rows, wide), f32),
                pltpu.VMEM((rows, wide), f32),
                pltpu.VMEM((rows, 3 * wide), bf16),
            ],
        ),
        out_shape=[
            jax.ShapeDtypeStruct((rows, 3 * wide), bf16),
            jax.ShapeDtypeStruct((8, 3 * wide), f32),
        ],
        compiler_params=pltpu.CompilerParams(vmem_limit_bytes=60 * 2**20),
        cost_estimate=pl.CostEstimate(
            flops=8 * rows * rows * wide + pairs * 10 * wide, bytes_accessed=20 * rows * wide, transcendentals=pairs
        ),
        name="attend_backward",
    )(low, packed, outt, lse, grad, cosine, sine, prow, pcol, start, qmask, vmask, ktmask)


def shards(
    hidden_in,
    out_grad,
    ln_gain,
    ln_bias,
    w_qkv,
    b_qkv,
    w_dense,
    b_dense,
    w_fc1,
    b_fc1,
    w_fc2,
    b_fc2,
    lengths,
    assignment,
):
    n = lax.axis_size("fsdp")
    m = lax.axis_size("ctx")
    z = lax.axis_index("fsdp")
    c = lax.axis_index("ctx")
    t = lax.axis_index("tp")
    rows, width = hidden_in.shape[1], hidden_in.shape[2]
    half = rows // 2
    group_rows = rows * m
    feat = width // n
    heads = w_qkv.shape[1] // (3 * HEAD) // m
    wide = heads * HEAD
    by_columns = (((1,), (1,)), ((), ()))
    by_rows = (((0,), (0,)), ((), ()))

    def turn(x):
        return jnp.concatenate(
            [lax.dynamic_slice_in_dim(x, lax.rem(z - s + n, n) * feat, feat, axis=1) for s in range(n)],
            axis=1,
        )

    def by_slots(left, right):
        return [
            lax.dot_general(
                left[:, s * feat : (s + 1) * feat], right, by_rows, preferred_element_type=f32
            ).astype(bf16)
            for s in range(n)
        ]

    def mine(weight):
        share = weight.shape[-1] // m
        return lax.dynamic_slice_in_dim(weight, c * share, share, axis=weight.ndim - 1)

    listed = jnp.array(column_order(heads), jnp.int32)
    place_of = (jnp.arange(3 * wide, dtype=jnp.int32)[:, None] == listed[None, :]).astype(bf16)
    qkv_bias = jnp.dot(mine(b_qkv)[None], place_of, preferred_element_type=f32)
    up_bias = mine(b_fc1).astype(f32)

    order = Order()
    z_ref = jnp.full((1,), z, jnp.int32)
    qkv_own = jnp.dot(mine(w_qkv), place_of, preferred_element_type=f32).astype(bf16)
    first = Gather(jnp.concatenate([qkv_own, mine(w_dense)], axis=1))
    first.start(order)

    at = jnp.stack([z, t]).astype(jnp.int32)
    gain_vec = ln_gain.astype(f32)
    shift_vec = ln_bias.astype(f32)
    gain_row = jnp.broadcast_to(gain_vec[None], (8, width))
    shift_row = jnp.broadcast_to(shift_vec[None], (8, width))
    normed_own = prepare(True, at, after(hidden_in[0], first.ups[0]), gain_row, shift_row, n)[0]
    order.did(normed_own)
    rows_in = Rows(normed_own)
    rows_in.start(order)
    grads_own, out_sum = prepare(False, at, order.then(out_grad[0]), gain_row, shift_row, n)
    order.did(grads_own)
    grads_all = lax.all_gather(grads_own, ("ctx", "tp"), axis=0, tiled=True)
    first.arrive(order)

    first.start(order)
    w_fc1, w_fc2 = order.then((w_fc1, w_fc2))
    second = Gather(mine(w_fc1))
    third_own = mine(w_fc2)
    assignment, lengths = order.then((assignment, lengths))

    block_of = [((c ^ j) * 2 + (t ^ h)) * half for h in range(2) for j in range(m)]
    packed = jnp.concatenate(
        [lax.dynamic_slice_in_dim(assignment[0], at, half) for at in block_of]
    )
    split = ROT // 2 * heads
    slab = 2 * split if 2 * split % 128 == 0 else wide
    lane = jnp.arange(wide)
    lane_head = jnp.where(lane < 2 * split, (lane % split) // (ROT // 2), (lane - 2 * split) // (HEAD - ROT))
    exponent = (lane[:slab] % (ROT // 2)).astype(f32) * 2.0 / ROT
    frequency = jnp.where(lane[:slab] < 2 * split, jnp.power(10000.0, -exponent), 0.0)
    sign = jnp.where(lane[:slab] < split, -1.0, 1.0)

    def tables(place):
        angles = place.astype(f32)[:, None] * frequency[None, :]
        return jnp.cos(angles), jnp.sin(angles) * sign[None, :]

    ordered = jnp.arange(group_rows, dtype=jnp.int32)
    place_packed = positions(ordered, lengths[0])[1]
    start = ordered - place_packed
    low = start[::BLOCK] // BLOCK
    start = start[None]
    cos_arrival, sin_arrival = tables(positions(packed, lengths[0])[1])
    cos_packed, sin_packed = tables(place_packed)
    prow, pcol = packed[None], packed[:, None]
    head_qk = (lane_head[None] == jnp.arange(heads)[:, None]).astype(bf16)
    head_v = ((lane // HEAD)[None] == jnp.arange(heads)[:, None]).astype(bf16)
    qmask = jnp.broadcast_to(head_qk[:, None, :], (heads, BLOCK, wide))
    vmask = jnp.broadcast_to(head_v[:, None, :], (heads, BLOCK, wide))
    ktmask = jnp.broadcast_to(head_qk[:, :, None], (heads, wide, BLOCK))

    order.did(second.ups[0], third_own, cos_arrival, sin_arrival, cos_packed, sin_packed)
    rows_in.arrive(order)
    first.arrive(order)

    first.start(order)
    rows_in.start_far()
    rows_in.arrive_far(order)
    rows_in.halves(order)
    first.arrive(order)
    first.rest(order)

    second.start(order)
    rows_in.start_last(order)
    rows_in.arrive_last(order)
    normed = rows_in.all(order)

    qkv_bias = jnp.broadcast_to(qkv_bias, (8, 3 * wide))
    qkv_packed, vt = pack(
        heads, z_ref, order.then(normed), qkv_bias, cos_arrival, sin_arrival, prow, first.sources()
    )
    order.did(qkv_packed)
    second.arrive(order)

    second.start(order)
    outt, lse, mixed = attend(heads, low, order.then(qkv_packed), vt, pcol, start, qmask)
    order.did(mixed)
    second.arrive(order)

    second.start(order)
    by_block = jnp.stack([at // half for at in block_of]).astype(jnp.int32)
    grads = reorder(by_block, order.then(grads_all), 2 * m)
    order.did(grads)
    mixed_grad = times(z_ref, order.then(grads), first.sources(), 3 * wide, wide)
    order.did(mixed_grad)
    dense_grad = lax.dot_general(grads, order.then(mixed), by_rows, preferred_element_type=f32).astype(bf16)
    order.did(dense_grad)
    second.arrive(order)
    second.rest(order)

    third = lax.all_gather(order.then(third_own), "fsdp", axis=0, tiled=True)
    up_bias = jnp.broadcast_to(up_bias[None], (8, up_bias.shape[0]))
    up, act = up_forward(z_ref, order.then(normed), up_bias, second.sources())
    order.did(act)
    to_slots = jnp.stack([lax.rem(z - f + n, n) for f in range(n)]).astype(jnp.int32)
    down_grad = lax.dot_general(grads, order.then(act), by_rows, preferred_element_type=f32).astype(bf16)
    order.did(down_grad)
    down_grad = reorder(to_slots, down_grad, n)
    order.did(down_grad)
    down_total = lax.psum_scatter(order.then(down_grad), "fsdp", scatter_dimension=0, tiled=True)

    qkv_grad_low, qkv_bias_sum = attend_back(
        heads, low, order.then(qkv_packed), outt, lse, mixed_grad, cos_packed, sin_packed, prow, pcol, start,
        qmask, vmask, ktmask,
    )
    order.did(qkv_grad_low)
    qkv_weight = lax.dot_general(
        normed, order.then(qkv_grad_low), by_rows, preferred_element_type=f32
    ).astype(bf16)
    first_sum = Scatter(join(qkv_weight, dense_grad, n))
    order.did(*first_sum.parts)

    third_sources = [order.arrive(third)]
    first_sum.start(order)
    up_grad_low, up_bias_sum = up_backward(z_ref, grads, order.then(up), third_sources)
    order.did(up_grad_low)
    keep, send = to_features(
        z_ref, order.then(mixed), first.sources(), 3 * wide, act, third_sources, half, width
    )
    order.did(keep)
    first_sum.arrive(order)

    first_sum.start(order)
    other = swap(order.then(send), "tp", 1)
    up_weight = lax.dot_general(
        normed, order.then(up_grad_low), by_rows, preferred_element_type=f32
    ).astype(bf16)
    order.did(up_weight)
    up_weight = reorder(to_slots, order.then(up_weight), n)
    order.did(up_weight)
    up_total = lax.psum_scatter(order.then(up_weight), "fsdp", scatter_dimension=0, tiled=True)
    keep, other = order.arrive((keep, other))

    branch_sum = RowSums(order.arrive(add(keep, other)))
    branch_sum.start(order)
    keep, send = to_features(
        z_ref, order.then(qkv_grad_low), first.sources(), 0, up_grad_low, second.sources(), half, width
    )
    order.did(keep)
    branch_sum.arrive(order)
    first_sum.arrive(order)
    down_total = order.arrive(down_total)

    first_sum.start(order)
    other = swap(order.then(send), "tp", 1)
    branch_sum.start_last(order)
    source = order.then(lax.dynamic_slice_in_dim(hidden_in[0], t * half, half)).astype(f32)
    centred = source - jnp.mean(source, axis=-1, keepdims=True)
    rstd = lax.rsqrt(jnp.mean(centred * centred, axis=-1, keepdims=True) + EPSILON)
    xhat = centred * rstd
    order.did(xhat)
    keep, other = order.arrive((keep, other))
    row_sum = RowSums(order.arrive(add(keep, other)))
    branch_sum.arrive_last(order)
    first_sum.arrive(order)
    first_sum.rest(order)

    row_sum.start(order)
    first_total = order.then(first_sum.total())
    qkv_sum = lax.dot_general(
        first_total[:, : 3 * wide], place_of, by_columns, preferred_element_type=f32
    ).astype(bf16)
    both = jnp.concatenate([qkv_sum, first_total[:, 3 * wide :], down_total], axis=1)
    order.did(both)
    pieces = spread_start(both)
    branch = turn(order.then(branch_sum.total()))
    biases = b_dense.astype(f32) + b_fc2.astype(f32)
    result = (source + branch + biases).astype(bf16)
    order.did(result)
    row_sum.arrive(order)
    pieces = order.arrive(pieces)

    row_sum.start_last(order)
    result_other = swap(order.then(result), "tp", 1)
    c_ref = jnp.full((1,), c, jnp.int32)
    qkv_part, dense_part, down_part = place(
        c_ref, order.then(pieces), [3 * wide, wide, w_fc2.shape[1] // m]
    )
    order.did(qkv_part)
    up_total = order.arrive(up_total)
    row_sum.arrive_last(order)

    up_pieces = spread_start(order.then(up_total))
    normed_grad = turn(row_sum.total())
    d = order.then(normed_grad) * gain_vec
    input_grad = rstd * (
        d - jnp.mean(d, axis=-1, keepdims=True) - xhat * jnp.mean(d * xhat, axis=-1, keepdims=True)
    ) + lax.dynamic_slice_in_dim(out_grad[0], t * half, half).astype(f32)
    norm_sums = jnp.concatenate([jnp.sum(normed_grad * xhat, axis=0), jnp.sum(normed_grad, axis=0)])
    order.did(input_grad, norm_sums)
    input_other = swap(order.then(input_grad), "tp", 1)
    norm_sums = order.then(norm_sums)
    up_part = place(c_ref, order.arrive(up_pieces), [w_fc1.shape[1] // m])[0]

    def in_rows(own_half, other_half):
        return jnp.concatenate(
            [jnp.where(t == 0, own_half, other_half), jnp.where(t == 0, other_half, own_half)], axis=0
        )

    result = in_rows(result, result_other)
    input_grad = in_rows(input_grad, input_other)
    def placed(vector):
        full = jnp.zeros((vector.shape[0] * m,), f32)
        return lax.dynamic_update_slice_in_dim(full, vector, c * vector.shape[0], axis=0)

    qkv_bias_grad = lax.dot_general(
        qkv_bias_sum[:1], place_of.astype(f32), by_columns,
        precision=lax.Precision.HIGHEST, preferred_element_type=f32,
    )[0]
    norm_sums = norm_sums + swap(norm_sums, "tp", 1)
    sums = everywhere(
        jnp.concatenate([norm_sums, out_sum[0], placed(qkv_bias_grad), placed(up_bias_sum[0])]), "fsdp", "ctx"
    )
    gain_grad, shift_grad, out_bias_grad = sums[:width], sums[width : 2 * width], sums[2 * width : 3 * width]
    qkv_bias_grad = sums[3 * width : 3 * width + 3 * wide * m]
    up_bias_grad = sums[3 * width + 3 * wide * m :]
    return (
        result[None],
        input_grad[None],
        gain_grad,
        shift_grad,
        qkv_part,
        qkv_bias_grad,
        dense_part,
        out_bias_grad,
        up_part,
        up_bias_grad,
        down_part,
        out_bias_grad,
    )


def solution(mesh):
    in_specs = (
        P("fsdp", "ctx", None),
        P("fsdp", "ctx", None),
        P(),
        P(),
        P("fsdp", "tp"),
        P("tp"),
        P("fsdp", "tp"),
        P(),
        P("fsdp", "tp"),
        P("tp"),
        P("fsdp", "tp"),
        P(),
        P("fsdp", None),
        P("fsdp", None),
    )
    out_specs = (
        P("fsdp", "ctx", None),
        P("fsdp", "ctx", None),
        P(),
        P(),
        P(("fsdp", "ctx"), "tp"),
        P("tp"),
        P(("fsdp", "ctx"), "tp"),
        P(),
        P(("fsdp", "ctx"), "tp"),
        P("tp"),
        P(("fsdp", "ctx"), "tp"),
        P(),
    )
    return jax.shard_map(shards, mesh=mesh, in_specs=in_specs, out_specs=out_specs, check_vma=False)
```

```python
import functools
import math

import jax
import jax.numpy as jnp
from jax import lax
from jax.experimental import pallas as pl
from jax.experimental.pallas import tpu as pltpu
from jax.sharding import PartitionSpec as P

HEAD = 64
ROT = 32
MASKED = -1e30
EPSILON = 1e-05
f32 = jnp.float32
bf16 = jnp.bfloat16


def positions(packed, lengths):
    seq_ends = jnp.cumsum(lengths)
    starts = seq_ends - lengths
    segment = jnp.sum((packed[:, None] >= seq_ends[None, :]).astype(jnp.int32), axis=1)
    owner_mask = segment[:, None] == jnp.arange(lengths.shape[0], dtype=jnp.int32)[None, :]
    return (segment, packed - jnp.sum(jnp.where(owner_mask, starts[None, :], 0), axis=1))


def gelu_tanh(values):
    return jax.nn.gelu(values, approximate=True)


def swap(x, axis, bit):
    size = lax.axis_size(axis)
    return lax.ppermute(x, axis, [(i, i ^ bit) for i in range(size)])


def everywhere(x, *axes):
    for axis in axes:
        bit = 1
        while bit < lax.axis_size(axis):
            x = x + swap(x, axis, bit)
            bit *= 2
    return x


def after(x, *before):
    before = [item for item in before if item is not None]
    return lax.optimization_barrier((x, *before))[0] if before else x


class Order:
    def __init__(self):
        self.last = ()

    def then(self, x):
        return after(x, *self.last)

    def did(self, *values):
        self.last = values

    def arrive(self, values):
        values = after(values, *self.last)
        self.last = self.last + tuple(jax.tree.leaves(values))
        return values


def line_up(x, first, last):
    return lax.ppermute(x, "fsdp", [(i, i + 1) for i in range(first, last)])


def line_down(x, first, last):
    return lax.ppermute(x, "fsdp", [(i, i - 1) for i in range(first, last)])


class Gather:
    def __init__(self, own):
        self.ups, self.downs = [own], [own]

    def start(self, order):
        n, s = lax.axis_size("fsdp"), len(self.ups)
        if s < n:
            up, down = order.then((self.ups[-1], self.downs[-1]))
            self.ups.append(line_up(up, s - 1, n - 1))
            self.downs.append(line_down(down, 1, n - s + 1))

    def arrive(self, order):
        self.ups[-1], self.downs[-1] = order.arrive((self.ups[-1], self.downs[-1]))

    def rest(self, order):
        for _ in range(len(self.ups), lax.axis_size("fsdp")):
            self.start(order)
            self.arrive(order)

    def sources(self):
        return self.ups + self.downs[1:]


class Scatter:
    def __init__(self, parts):
        self.parts, self.sums, self.step = parts, None, 1

    def start(self, order):
        n, s = lax.axis_size("fsdp"), self.step
        if s < n:
            up, down = order.then((self.parts[s], self.parts[n - s]))
            if self.sums is not None:
                up, down = order.arrive((add(up, self.sums[0]), add(down, self.sums[1])))
            self.sums = line_up(up, 0, min(s, n - 1)), line_down(down, max(n - s, 1), n)
            self.step += 1

    def arrive(self, order):
        self.sums = order.arrive(self.sums)

    def rest(self, order):
        for _ in range(self.step, lax.axis_size("fsdp")):
            self.start(order)
            self.arrive(order)

    def total(self):
        up, down = self.sums
        return (self.parts[0].astype(f32) + up.astype(f32) + down.astype(f32)).astype(bf16)


class Rows:
    def __init__(self, mine):
        self.mine = mine

    def start(self, order):
        mine = order.then(self.mine)
        self.near = [swap(mine, "ctx", 1 << k) for k in range(lax.axis_size("ctx").bit_length() - 1)]

    def arrive(self, order):
        self.near = order.arrive(self.near)

    def start_far(self):
        m, quarter = lax.axis_size("ctx"), self.mine.shape[0] // 2
        if m == 4:
            first, second = self.near
            self.far = [swap(first[:quarter], "ctx", 2), swap(second[quarter:], "ctx", 1)]
        else:
            self.far = [swap(self.mine, "ctx", j) for j in range(1, m) if j & (j - 1)]

    def arrive_far(self, order):
        self.far = order.arrive(self.far)

    def halves(self, order):
        m = lax.axis_size("ctx")
        near, far = list(self.near), list(self.far)
        blocks = [self.mine]
        for j in range(1, m):
            if j & (j - 1) == 0:
                blocks.append(near.pop(0))
            elif m == 4:
                blocks += far
            else:
                blocks.append(far.pop(0))
        self.here = assemble(order.then(blocks))
        order.did(self.here)

    def start_last(self, order):
        self.there = swap(order.then(self.here), "tp", 1)

    def arrive_last(self, order):
        self.there = order.arrive(self.there)

    def all(self, order):
        full = assemble(order.then([self.here, self.there]))
        order.did(full)
        return full


class RowSums:
    def __init__(self, slots):
        self.slots = [slots[j] for j in range(slots.shape[0])]

    def start_direct(self, order):
        slots = order.then(self.slots)
        self.got, self.last = [], [swap(slots[j], "ctx", j) for j in range(1, len(slots))]

    def start(self, order):
        m, slots = len(self.slots), order.then(self.slots)
        quarter = slots[0].shape[0] // 2
        if m == 4:
            self.got = [swap(slots[3][:quarter], "ctx", 2), swap(slots[3][quarter:], "ctx", 1)]
        else:
            self.got = [swap(slots[j], "ctx", j) for j in range(1, m) if j & (j - 1)]

    def arrive(self, order):
        self.got = order.arrive(self.got)

    def start_last(self, order):
        m, slots = len(self.slots), order.then(self.slots)
        quarter = slots[0].shape[0] // 2
        if m == 4:
            first = jnp.concatenate([add(slots[1][:quarter], self.got[0]), slots[1][quarter:]], axis=0)
            second = jnp.concatenate([slots[2][:quarter], add(slots[2][quarter:], self.got[1])], axis=0)
            first, second = order.arrive((first, second))
            self.last, self.got = [swap(first, "ctx", 1), swap(second, "ctx", 2)], []
        else:
            self.last = [swap(slots[j], "ctx", j) for j in range(1, m) if j & (j - 1) == 0]

    def arrive_last(self, order):
        self.last, self.slots[0] = order.arrive((self.last, self.slots[0]))

    def total(self):
        return sum((x.astype(f32) for x in self.got + self.last), self.slots[0].astype(f32))


def add(a, b):
    return (a.astype(f32) + b.astype(f32)).astype(bf16)


def spread_start(block):
    m = lax.axis_size("ctx")
    c = lax.axis_index("ctx")
    rows = block.shape[0] // m
    pieces = []
    for j in range(m):
        piece = lax.dynamic_slice_in_dim(block, (c ^ j) * rows, rows, axis=0)
        pieces.append(piece if j == 0 else swap(piece, "ctx", j))
    return pieces


def column_order(heads):
    order = []
    for part in range(2):
        for start, width in ((0, ROT // 2), (ROT // 2, ROT // 2), (ROT, HEAD - ROT)):
            for head in range(heads):
                base = (head * 3 + part) * HEAD + start
                order += list(range(base, base + width))
    for head in range(heads):
        base = (head * 3 + 2) * HEAD
        order += list(range(base, base + HEAD))
    return order


BLOCK = 256
NT = (((1,), (1,)), ((), ()))


def mm(a, b, dims=(((1,), (0,)), ((), ()))):
    return lax.dot_general(a, b, dims, preferred_element_type=f32)


def turned(x, cosine, sine, split):
    slab = cosine.shape[1]
    front = x[:, :slab]
    if slab == 2 * split:
        partner = pltpu.roll(front, split, 1)
    else:
        lane = lax.broadcasted_iota(jnp.int32, front.shape, 1)
        partner = jnp.where(
            lane < split, pltpu.roll(front, slab - split, 1), pltpu.roll(front, split, 1)
        )
    front = front * cosine + partner * sine
    if slab == x.shape[1]:
        return front
    return jnp.concatenate([front, x[:, slab:]], axis=1)


def to_packed(prow_ref, block, data):
    shape = (BLOCK, prow_ref.shape[1])
    at = lax.broadcasted_iota(jnp.int32, shape, 0) + block * BLOCK
    return mm((at == prow_ref[...]).astype(f32).astype(bf16), data)


def to_arrival(pcol_ref, block, data):
    rows = pl.ds(pl.multiple_of(block * BLOCK, BLOCK), BLOCK)
    shape = (BLOCK, data.shape[0])
    at = lax.broadcasted_iota(jnp.int32, shape, 1)
    return mm((at == pcol_ref[rows, :]).astype(f32).astype(bf16), data)


def kept(i, j, start):
    keys = lax.broadcasted_iota(jnp.int32, (BLOCK, BLOCK), 0) + j * BLOCK
    queries = lax.broadcasted_iota(jnp.int32, (BLOCK, BLOCK), 1) + i * BLOCK
    return (keys >= start) & (keys <= queries)


def fetch(z_ref, sources, weight_ref, sems, first):
    feat, cols = sources[0].shape[0], weight_ref.shape[1]
    if len(sources) == 1:
        feat = weight_ref.shape[0] // sems.shape[0]
    n = weight_ref.shape[0] // feat

    def copy(source, s):
        rows = pl.ds(s * feat, feat)
        return pltpu.make_async_copy(
            source.at[:, pl.ds(first, cols)], weight_ref.at[rows, :], sems.at[s]
        )

    def each(do):
        if len(sources) == 1:
            for s in range(n):
                block = pl.multiple_of(lax.rem(z_ref[0] - s + n, n) * feat, feat)
                do(copy(sources[0].at[pl.ds(block, feat), :], s))
            return
        do(copy(sources[0], 0))
        for s in range(1, n):

            @pl.when(z_ref[0] >= s)
            def _():
                do(copy(sources[s], s))

            @pl.when(z_ref[0] < s)
            def _():
                do(copy(sources[2 * n - 1 - s], s))

    each(lambda c: c.start())
    each(lambda c: c.wait())


def pack_kernel(heads, count, z_ref, x_in_ref, bias_ref, cos_ref, sin_ref, prow_ref, *rest):
    sources, (packed_ref, vt_ref, x_ref, weight_ref, sems) = rest[:count], rest[count:]
    wide = vt_ref.shape[0]
    blocks = x_ref.shape[0] // BLOCK
    split = ROT // 2 * heads
    r = pl.program_id(0)

    @pl.when(r == 0)
    def _():
        fetch(z_ref, sources, weight_ref, sems, 0)

    rows = pl.ds(pl.multiple_of(r * BLOCK, BLOCK), BLOCK)
    cosine, sine = cos_ref[rows, :], sin_ref[rows, :]
    x_in = x_in_ref[...]
    for part in range(3):
        at = slice(part * wide, (part + 1) * wide)
        x = mm(x_in, weight_ref[:, at]) + bias_ref[0:1, at]
        if part < 2:
            x = turned(x, cosine, sine, split)
        if part == 0:
            x = x * (1.0 / math.sqrt(HEAD))
        x_ref[rows, at] = x.astype(bf16)

    @pl.when(r == blocks - 1)
    def _():
        @pl.loop(0, blocks)
        def _(p):
            rows = pl.ds(pl.multiple_of(p * BLOCK, BLOCK), BLOCK)
            y = to_packed(prow_ref, p, x_ref[...])
            packed_ref[rows, :] = y.astype(bf16)
            vt_ref[:, rows] = y[:, 2 * wide :].T.astype(bf16)


def curve(u):
    square = u * u
    return jnp.tanh(math.sqrt(2.0 / math.pi) * (u + 0.044715 * (square * u))), square


def up_kernel(count, z_ref, x_ref, bias_ref, *rest):
    sources, (up_ref, act_ref, weight_ref, sems) = rest[:count], rest[count:]

    @pl.when(pl.program_id(0) == 0)
    def _():
        fetch(z_ref, sources, weight_ref, sems, 0)

    x = x_ref[...]
    step = min(256, up_ref.shape[1])
    for at in range(0, up_ref.shape[1], step):
        at = slice(at, at + step)
        u = mm(x, weight_ref[:, at]) + bias_ref[0:1, at]
        up_ref[:, at] = u
        act_ref[:, at] = (0.5 * u * (1.0 + curve(u)[0])).astype(bf16)


def up_back_kernel(count, z_ref, x_ref, up_ref, *rest):
    sources, (grad_ref, sum_ref, weight_ref, sems) = rest[:count], rest[count:]

    @pl.when(pl.program_id(0) == 0)
    def _():
        fetch(z_ref, sources, weight_ref, sems, 0)
        sum_ref[...] = jnp.zeros(sum_ref.shape, f32)

    x = x_ref[...]
    step = min(256, grad_ref.shape[1])
    for at in range(0, grad_ref.shape[1], step):
        at = slice(at, at + step)
        u = up_ref[:, at]
        bend, square = curve(u)
        slope = 0.5 * (1.0 + bend) + (0.5 * math.sqrt(2.0 / math.pi)) * u * (
            (1.0 - bend * bend) * (1.0 + (3.0 * 0.044715) * square)
        )
        grad = mm(x, weight_ref[:, at]) * slope
        grad_ref[:, at] = grad.astype(bf16)
        sum_ref[0:1, at] = sum_ref[0:1, at] + jnp.sum(grad, axis=0, keepdims=True)


def plain_kernel(count, first, z_ref, x_ref, *rest):
    sources, (out_ref, weight_ref, sems) = rest[:count], rest[count:]

    @pl.when(pl.program_id(0) == 0)
    def _():
        fetch(z_ref, sources, weight_ref, sems, first)

    out_ref[...] = mm(x_ref[...], weight_ref[...]).astype(bf16)


def spread_kernel(count, first, z_ref, a_ref, b_ref, *rest):
    a_sources, b_sources = rest[: count[0]], rest[count[0] : sum(count)]
    keep_ref, send_ref, a_weight_ref, b_weight_ref, sems = rest[sum(count) :]

    @pl.when(pl.program_id(0) == 0)
    def _():
        fetch(z_ref, a_sources, a_weight_ref, sems, first)
        fetch(z_ref, b_sources, b_weight_ref, sems, 0)

    slots, half, width = keep_ref.shape
    steps = pl.num_programs(0) // 2

    def write(out_ref):
        for slot in range(slots):
            rows = slice(slot * half, (slot + 1) * half)
            a, b = a_ref[rows, :], b_ref[rows, :]
            for at in range(0, width, 256):
                at = slice(at, at + 256)
                out = mm(a, a_weight_ref[at, :], NT) + mm(b, b_weight_ref[at, :], NT)
                out_ref[slot, :, at] = out.astype(bf16)

    @pl.when(pl.program_id(0) < steps)
    def _():
        write(keep_ref)

    @pl.when(pl.program_id(0) >= steps)
    def _():
        write(send_ref)


def forward_kernel(
    heads, low_ref, packed_ref, vt_ref, pcol_ref, start_ref, qmask_ref,
    outt_ref, lse_ref, mixed_ref, mp_ref,
):
    rows_all, wide = mixed_ref.shape
    blocks = rows_all // BLOCK

    @pl.loop(0, blocks)
    def _(i):
        rows = pl.ds(pl.multiple_of(i * BLOCK, BLOCK), BLOCK)
        start = start_ref[0:1, rows]
        q = packed_ref[rows, :wide]
        qs = jnp.concatenate([q * qmask_ref[h] for h in range(heads)], axis=0)

        def step(j, carried):
            keys = pl.ds(pl.multiple_of(j * BLOCK, BLOCK), BLOCK)
            k = packed_ref[keys, wide : 2 * wide]
            keep = kept(i, j, start)
            scores = mm(k, qs, NT)
            after = []
            for h in range(heads):
                top, total, acc = carried[h]
                s = jnp.where(keep, scores[:, h * BLOCK : (h + 1) * BLOCK], MASKED)
                new_top = jnp.maximum(top, jnp.max(s, axis=0, keepdims=True))
                p = jnp.exp(s - new_top)
                alpha = jnp.exp(top - new_top)
                total = total * alpha + jnp.sum(p, axis=0, keepdims=True)
                acc = acc * alpha + mm(vt_ref[h * HEAD : (h + 1) * HEAD, keys], p.astype(bf16))
                after.append((new_top, total, acc))
            return tuple(after)

        begin = tuple(
            (
                jnp.full((1, BLOCK), MASKED, f32),
                jnp.zeros((1, BLOCK), f32),
                jnp.zeros((HEAD, BLOCK), f32),
            )
            for _ in range(heads)
        )
        state = lax.fori_loop(low_ref[i], i + 1, step, begin)
        out = jnp.concatenate([acc / total for _, total, acc in state], axis=0)
        outt_ref[:, rows] = out
        mp_ref[rows, :] = out.T.astype(bf16)
        lse = [top + jnp.log(total) for top, total, _ in state]
        lse_ref[:, rows] = jnp.concatenate(lse + [jnp.zeros((8 - heads, BLOCK), f32)], axis=0)

    @pl.loop(0, blocks)
    def _(r):
        rows = pl.ds(pl.multiple_of(r * BLOCK, BLOCK), BLOCK)
        mixed_ref[rows, :] = to_arrival(pcol_ref, r, mp_ref[...]).astype(bf16)


def backward_kernel(
    heads, low_ref, packed_ref, outt_ref, lse_ref, grad_ref, cos_ref, sin_ref, prow_ref, pcol_ref, start_ref,
    qmask_ref, vmask_ref, ktmask_ref,
    qkv_grad_ref, bias_grad_ref, kt_ref, dk_ref, dv_ref, dq_ref, gp_ref,
):
    rows_all, wide = grad_ref.shape
    blocks = rows_all // BLOCK
    split = ROT // 2 * heads

    @pl.loop(0, blocks)
    def _(p):
        rows = pl.ds(pl.multiple_of(p * BLOCK, BLOCK), BLOCK)
        gp_ref[rows, :wide] = to_packed(prow_ref, p, grad_ref[...]).astype(bf16)
        kt_ref[:, rows] = packed_ref[rows, wide : 2 * wide].astype(f32).T.astype(bf16)
        dk_ref[rows, :] = jnp.zeros((BLOCK, wide), f32)
        dv_ref[rows, :] = jnp.zeros((BLOCK, wide), f32)

    @pl.loop(0, blocks)
    def _(i):
        rows = pl.ds(pl.multiple_of(i * BLOCK, BLOCK), BLOCK)
        start = start_ref[0:1, rows]
        q = packed_ref[rows, :wide]
        g = gp_ref[rows, :wide]
        qs = jnp.concatenate([q * qmask_ref[h] for h in range(heads)], axis=0)
        gs = jnp.concatenate([g * vmask_ref[h] for h in range(heads)], axis=0)
        product = g.astype(f32).T * outt_ref[:, rows]
        inner = [
            jnp.sum(product[h * HEAD : (h + 1) * HEAD], axis=0, keepdims=True) for h in range(heads)
        ]
        lse = [lse_ref[h : h + 1, rows] for h in range(heads)]

        def step(j, dqt):
            keys = pl.ds(pl.multiple_of(j * BLOCK, BLOCK), BLOCK)
            k = packed_ref[keys, wide : 2 * wide]
            v = packed_ref[keys, 2 * wide :]
            kt = kt_ref[:, keys]
            keep = kept(i, j, start)
            scores = mm(k, qs, NT)
            slopes = mm(v, gs, NT)
            probs, flows = [], []
            for h in range(heads):
                at = slice(h * BLOCK, (h + 1) * BLOCK)
                p = jnp.exp(jnp.where(keep, scores[:, at], MASKED) - lse[h])
                probs.append(p.astype(bf16))
                flows.append((p * (slopes[:, at] - inner[h])).astype(bf16))
            dv_ref[keys, :] = dv_ref[keys, :] + mm(jnp.concatenate(probs, axis=1), gs)
            dk_ref[keys, :] = dk_ref[keys, :] + mm(jnp.concatenate(flows, axis=1), qs)
            kts = jnp.concatenate([kt * ktmask_ref[h] for h in range(heads)], axis=1)
            return dqt + mm(kts, jnp.concatenate(flows, axis=0))

        dqt = lax.fori_loop(low_ref[i], i + 1, step, jnp.zeros((wide, BLOCK), f32))
        dq_ref[rows, :] = dqt.T * (1.0 / math.sqrt(HEAD))

    bias_grad_ref[...] = jnp.zeros(bias_grad_ref.shape, f32)

    @pl.loop(0, blocks)
    def _(p):
        rows = pl.ds(pl.multiple_of(p * BLOCK, BLOCK), BLOCK)
        cosine, sine = cos_ref[rows, :], -sin_ref[rows, :]
        dq = turned(dq_ref[rows, :], cosine, sine, split)
        dk = turned(dk_ref[rows, :], cosine, sine, split)
        full = jnp.concatenate([dq, dk, dv_ref[rows, :]], axis=1)
        bias_grad_ref[0:1, :] = bias_grad_ref[0:1, :] + jnp.sum(full, axis=0, keepdims=True)
        gp_ref[rows, :] = full.astype(bf16)

    @pl.loop(0, blocks)
    def _(r):
        rows = pl.ds(pl.multiple_of(r * BLOCK, BLOCK), BLOCK)
        qkv_grad_ref[rows, :] = to_arrival(pcol_ref, r, gp_ref[...]).astype(bf16)


def whole(count):
    return [pl.BlockSpec(memory_space=pltpu.VMEM)] * count


COST = 0.05


def blocks_call(kernel, name, z, ins, in_specs, sources, outs, out_specs, scratch, steps, flops, weight_shapes):
    sems = lax.axis_size("fsdp")
    return pl.pallas_call(
        kernel,
        grid_spec=pltpu.PrefetchScalarGridSpec(
            num_scalar_prefetch=1,
            grid=(steps,),
            in_specs=in_specs + [pl.BlockSpec(memory_space=pl.ANY)] * sum(map(len, sources)),
            out_specs=out_specs,
            scratch_shapes=scratch
            + [pltpu.VMEM(shape, bf16) for shape in weight_shapes]
            + [pltpu.SemaphoreType.DMA((sems,))],
        ),
        out_shape=outs,
        compiler_params=pltpu.CompilerParams(vmem_limit_bytes=48 * 2**20),
        cost_estimate=pl.CostEstimate(flops=int(COST * flops), bytes_accessed=2**20, transcendentals=0),
        name=name,
    )(z, *ins, *[x for group in sources for x in group])


def fixed(shape):
    return pl.BlockSpec(shape, lambda *_: (0,) * len(shape))


def by_row(rows, cols):
    return pl.BlockSpec((rows, cols), lambda i, *_: (i, 0))


def prepare_kernel(norm, slots, at_ref, x_ref, gain_ref, shift_ref, out_ref, *rest):
    rows, width = x_ref.shape
    half, step = rows // 2, 64
    feat = width // slots

    @pl.loop(0, half // step)
    def _(b):
        source = pl.ds(pl.multiple_of(at_ref[1] * half + b * step, step), step)
        target = pl.ds(pl.multiple_of(b * step, step), step)
        if norm:
            x = x_ref[source, :].astype(f32)
            mean = jnp.mean(x, axis=-1, keepdims=True)
            centred = x - mean
            rstd = lax.rsqrt(jnp.mean(centred * centred, axis=-1, keepdims=True) + EPSILON)
        for s in range(slots):
            block = lax.rem(at_ref[0] - s + slots, slots)
            columns = pl.ds(pl.multiple_of(block * feat, feat), feat)
            y = x_ref[source, columns]
            if norm:
                y = (y.astype(f32) - mean) * rstd * gain_ref[0:1, columns] + shift_ref[0:1, columns]
            out_ref[target, s * feat : (s + 1) * feat] = y.astype(bf16)

    if not norm:
        sum_ref = rest[0]
        sum_ref[...] = jnp.zeros(sum_ref.shape, f32)

        @pl.loop(0, rows // step)
        def _(b):
            source = pl.ds(pl.multiple_of(b * step, step), step)
            x = x_ref[source, :].astype(f32)
            sum_ref[0:1, :] = sum_ref[0:1, :] + jnp.sum(x, axis=0, keepdims=True)


def prepare(norm, at, x, gain, shift, n):
    rows, width = x.shape
    out = [jax.ShapeDtypeStruct((rows // 2, width), bf16)]
    if not norm:
        out.append(jax.ShapeDtypeStruct((8, width), f32))
    return pl.pallas_call(
        functools.partial(prepare_kernel, norm, n),
        grid_spec=pltpu.PrefetchScalarGridSpec(
            num_scalar_prefetch=1, grid=(), in_specs=whole(3), out_specs=whole(len(out))
        ),
        out_shape=out,
        compiler_params=pltpu.CompilerParams(vmem_limit_bytes=40 * 2**20),
        cost_estimate=pl.CostEstimate(flops=2**20, bytes_accessed=2**20, transcendentals=0),
        name="prepare",
    )(at, x, gain, shift)


def place_kernel(count, at_ref, *refs):
    pieces, outs = refs[:count], refs[count:]
    for j, piece in enumerate(pieces):
        first = 0
        for out_ref in outs:
            cols = out_ref.shape[1] // count
            target = pl.ds(pl.multiple_of((at_ref[0] ^ j) * cols, cols), cols)
            out_ref[:, target] = piece[:, first : first + cols].astype(f32)
            first += cols


def place(c, pieces, widths):
    count, rows = len(pieces), pieces[0].shape[0]
    return pl.pallas_call(
        functools.partial(place_kernel, count),
        grid_spec=pltpu.PrefetchScalarGridSpec(
            num_scalar_prefetch=1, grid=(), in_specs=whole(count), out_specs=whole(len(widths))
        ),
        out_shape=[jax.ShapeDtypeStruct((rows, count * cols), f32) for cols in widths],
        compiler_params=pltpu.CompilerParams(vmem_limit_bytes=40 * 2**20),
        cost_estimate=pl.CostEstimate(flops=2**20, bytes_accessed=2**20, transcendentals=0),
        name="place",
    )(c, *pieces)


def join_kernel(a_ref, b_ref, *outs):
    cols = a_ref.shape[1]
    for s, out_ref in enumerate(outs):

        @pl.when(pl.program_id(0) == s)
        def _():
            out_ref[:, :cols] = a_ref[...]
            out_ref[:, cols:] = b_ref[...]


def join(a, b, n):
    rows, cols = a.shape[0] // n, a.shape[1] + b.shape[1]
    return pl.pallas_call(
        join_kernel,
        grid=(n,),
        in_specs=[
            pl.BlockSpec((rows, a.shape[1]), lambda i: (i, 0)),
            pl.BlockSpec((rows, b.shape[1]), lambda i: (i, 0)),
        ],
        out_specs=[pl.BlockSpec((rows, cols), lambda i: (0, 0))] * n,
        out_shape=[jax.ShapeDtypeStruct((rows, cols), bf16)] * n,
        compiler_params=pltpu.CompilerParams(vmem_limit_bytes=40 * 2**20),
        cost_estimate=pl.CostEstimate(flops=2**20, bytes_accessed=2**20, transcendentals=0),
        name="join",
    )(a, b)


def reorder(order, x, blocks):
    rows, cols = x.shape[0] // blocks, x.shape[1]

    def copy_kernel(order_ref, x_ref, out_ref):
        out_ref[...] = x_ref[...]

    return pl.pallas_call(
        copy_kernel,
        grid_spec=pltpu.PrefetchScalarGridSpec(
            num_scalar_prefetch=1,
            grid=(blocks,),
            in_specs=[pl.BlockSpec((rows, cols), lambda i, order_ref: (order_ref[i], 0))],
            out_specs=pl.BlockSpec((rows, cols), lambda i, order_ref: (i, 0)),
        ),
        out_shape=jax.ShapeDtypeStruct(x.shape, x.dtype),
        compiler_params=pltpu.CompilerParams(vmem_limit_bytes=40 * 2**20),
        cost_estimate=pl.CostEstimate(flops=2**20, bytes_accessed=2**20, transcendentals=0),
        name="reorder",
    )(order, x)


def assemble_kernel(*refs):
    *pieces, out_ref, sems = refs

    def each(do):
        first = 0
        for k, piece in enumerate(pieces):
            count = piece.shape[0]
            do(pltpu.make_async_copy(piece, out_ref.at[pl.ds(first, count), :], sems.at[k]))
            first += count

    each(lambda copy: copy.start())
    each(lambda copy: copy.wait())


def assemble(pieces):
    rows = sum(piece.shape[0] for piece in pieces)
    return pl.pallas_call(
        assemble_kernel,
        in_specs=whole(len(pieces)),
        out_specs=pl.BlockSpec(memory_space=pl.ANY),
        scratch_shapes=[pltpu.SemaphoreType.DMA((len(pieces),))],
        out_shape=jax.ShapeDtypeStruct((rows, pieces[0].shape[1]), bf16),
        compiler_params=pltpu.CompilerParams(vmem_limit_bytes=40 * 2**20),
        cost_estimate=pl.CostEstimate(flops=2**20, bytes_accessed=2**20, transcendentals=0),
        name="assemble",
    )(*pieces)


def pack(heads, z, normed, bias, cosine, sine, prow, sources):
    rows, width = normed.shape
    wide = heads * HEAD
    slab = cosine.shape[1]
    return blocks_call(
        functools.partial(pack_kernel, heads, len(sources)), "pack", z,
        [normed, bias, cosine, sine, prow],
        [by_row(BLOCK, width), fixed(bias.shape), fixed((rows, slab)), fixed((rows, slab)), fixed(prow.shape)],
        [sources],
        [jax.ShapeDtypeStruct((rows, 3 * wide), bf16), jax.ShapeDtypeStruct((wide, rows), bf16)],
        [fixed((rows, 3 * wide)), fixed((wide, rows))],
        [pltpu.VMEM((rows, 3 * wide), bf16)],
        rows // BLOCK, 12 * rows * rows * wide, [(width, 3 * wide)],
    )


def up_forward(z, normed, bias, sources):
    rows, width = normed.shape
    cols = bias.shape[1]
    return blocks_call(
        functools.partial(up_kernel, len(sources)), "up", z,
        [normed, bias], [by_row(512, width), fixed(bias.shape)], [sources],
        [jax.ShapeDtypeStruct((rows, cols), f32), jax.ShapeDtypeStruct((rows, cols), bf16)],
        [by_row(512, cols), by_row(512, cols)], [],
        rows // 512, 2 * rows * width * cols, [(width, cols)],
    )


def up_backward(z, grads, up, sources):
    rows, width = grads.shape
    cols = up.shape[1]
    return blocks_call(
        functools.partial(up_back_kernel, len(sources)), "up_back", z,
        [grads, up], [by_row(512, width), by_row(512, cols)], [sources],
        [jax.ShapeDtypeStruct((rows, cols), bf16), jax.ShapeDtypeStruct((8, cols), f32)],
        [by_row(512, cols), fixed((8, cols))], [],
        rows // 512, 2 * rows * width * cols, [(width, cols)],
    )


def times(z, x, sources, first, cols):
    rows, width = x.shape
    return blocks_call(
        functools.partial(plain_kernel, len(sources), first), "times", z,
        [x], [by_row(512, width)], [sources],
        [jax.ShapeDtypeStruct((rows, cols), bf16)], [by_row(512, cols)], [],
        rows // 512, 2 * rows * width * cols, [(width, cols)],
    )[0]


def to_features(z, a, a_sources, first, b, b_sources, half, width):
    rows = a.shape[0]
    slots, each = rows // (2 * half), 512 // half
    steps = slots // each
    a_cols, b_cols = a.shape[1], b.shape[1]
    out = jax.ShapeDtypeStruct((slots, half, width), bf16)
    block = (each, half, width)
    return blocks_call(
        functools.partial(spread_kernel, (len(a_sources), len(b_sources)), first), "to_features", z,
        [a, b], [by_row(512, a_cols), by_row(512, b_cols)], [a_sources, b_sources],
        [out, out],
        [
            pl.BlockSpec(block, lambda i, *_: (jnp.minimum(i, steps - 1), 0, 0)),
            pl.BlockSpec(block, lambda i, *_: (jnp.maximum(i - steps, 0), 0, 0)),
        ],
        [], 2 * steps, 2 * rows * width * (a_cols + b_cols), [(width, a_cols), (width, b_cols)],
    )


def attend(heads, low, packed, vt, pcol, start, qmask):
    rows, wide = packed.shape[0], heads * HEAD
    pairs = (rows // BLOCK) * 4 * heads * BLOCK * BLOCK
    return pl.pallas_call(
        functools.partial(forward_kernel, heads),
        grid_spec=pltpu.PrefetchScalarGridSpec(
            num_scalar_prefetch=1,
            grid=(),
            in_specs=whole(5),
            out_specs=whole(3),
            scratch_shapes=[pltpu.VMEM((rows, wide), bf16)],
        ),
        out_shape=[
            jax.ShapeDtypeStruct((wide, rows), f32),
            jax.ShapeDtypeStruct((8, rows), f32),
            jax.ShapeDtypeStruct((rows, wide), bf16),
        ],
        compiler_params=pltpu.CompilerParams(vmem_limit_bytes=60 * 2**20),
        cost_estimate=pl.CostEstimate(
            flops=2 * rows * rows * wide + pairs * 4 * wide, bytes_accessed=20 * rows * wide, transcendentals=pairs
        ),
        name="attend_forward",
    )(low, packed, vt, pcol, start, qmask)


def attend_back(heads, low, packed, outt, lse, grad, cosine, sine, prow, pcol, start, qmask, vmask, ktmask):
    rows, wide = grad.shape
    pairs = (rows // BLOCK) * 4 * heads * BLOCK * BLOCK
    return pl.pallas_call(
        functools.partial(backward_kernel, heads),
        grid_spec=pltpu.PrefetchScalarGridSpec(
            num_scalar_prefetch=1,
            grid=(),
            in_specs=whole(12),
            out_specs=whole(2),
            scratch_shapes=[
                pltpu.VMEM((wide, rows), bf16),
                pltpu.VMEM((rows, wide), f32),
                pltpu.VMEM((rows, wide), f32),
                pltpu.VMEM((rows, wide), f32),
                pltpu.VMEM((rows, 3 * wide), bf16),
            ],
        ),
        out_shape=[
            jax.ShapeDtypeStruct((rows, 3 * wide), bf16),
            jax.ShapeDtypeStruct((8, 3 * wide), f32),
        ],
        compiler_params=pltpu.CompilerParams(vmem_limit_bytes=60 * 2**20),
        cost_estimate=pl.CostEstimate(
            flops=8 * rows * rows * wide + pairs * 10 * wide, bytes_accessed=20 * rows * wide, transcendentals=pairs
        ),
        name="attend_backward",
    )(low, packed, outt, lse, grad, cosine, sine, prow, pcol, start, qmask, vmask, ktmask)


def shards(
    hidden_in,
    out_grad,
    ln_gain,
    ln_bias,
    w_qkv,
    b_qkv,
    w_dense,
    b_dense,
    w_fc1,
    b_fc1,
    w_fc2,
    b_fc2,
    lengths,
    assignment,
):
    n = lax.axis_size("fsdp")
    m = lax.axis_size("ctx")
    z = lax.axis_index("fsdp")
    c = lax.axis_index("ctx")
    t = lax.axis_index("tp")
    rows, width = hidden_in.shape[1], hidden_in.shape[2]
    half = rows // 2
    group_rows = rows * m
    feat = width // n
    heads = w_qkv.shape[1] // (3 * HEAD) // m
    wide = heads * HEAD
    by_columns = (((1,), (1,)), ((), ()))
    by_rows = (((0,), (0,)), ((), ()))

    def turn(x):
        return jnp.concatenate(
            [lax.dynamic_slice_in_dim(x, lax.rem(z - s + n, n) * feat, feat, axis=1) for s in range(n)],
            axis=1,
        )

    def by_slots(left, right):
        return [
            lax.dot_general(
                left[:, s * feat : (s + 1) * feat], right, by_rows, preferred_element_type=f32
            ).astype(bf16)
            for s in range(n)
        ]

    def mine(weight):
        share = weight.shape[-1] // m
        return lax.dynamic_slice_in_dim(weight, c * share, share, axis=weight.ndim - 1)

    listed = jnp.array(column_order(heads), jnp.int32)
    place_of = (jnp.arange(3 * wide, dtype=jnp.int32)[:, None] == listed[None, :]).astype(bf16)
    qkv_bias = jnp.dot(mine(b_qkv)[None], place_of, preferred_element_type=f32)
    up_bias = mine(b_fc1).astype(f32)

    order = Order()
    z_ref = jnp.full((1,), z, jnp.int32)
    qkv_own = jnp.dot(mine(w_qkv), place_of, preferred_element_type=f32).astype(bf16)
    first = Gather(jnp.concatenate([qkv_own, mine(w_dense)], axis=1))
    first.start(order)

    at = jnp.stack([z, t]).astype(jnp.int32)
    gain_vec = ln_gain.astype(f32)
    shift_vec = ln_bias.astype(f32)
    gain_row = jnp.broadcast_to(gain_vec[None], (8, width))
    shift_row = jnp.broadcast_to(shift_vec[None], (8, width))
    normed_own = prepare(True, at, after(hidden_in[0], first.ups[0]), gain_row, shift_row, n)[0]
    order.did(normed_own)
    rows_in = Rows(normed_own)
    rows_in.start(order)
    grads_own, out_sum = prepare(False, at, order.then(out_grad[0]), gain_row, shift_row, n)
    order.did(grads_own)
    grads_all = lax.all_gather(grads_own, ("ctx", "tp"), axis=0, tiled=True)
    first.arrive(order)

    first.start(order)
    w_fc1, w_fc2 = order.then((w_fc1, w_fc2))
    second = Gather(mine(w_fc1))
    third_own = mine(w_fc2)
    assignment, lengths = order.then((assignment, lengths))

    block_of = [((c ^ j) * 2 + (t ^ h)) * half for h in range(2) for j in range(m)]
    packed = jnp.concatenate(
        [lax.dynamic_slice_in_dim(assignment[0], at, half) for at in block_of]
    )
    split = ROT // 2 * heads
    slab = 2 * split if 2 * split % 128 == 0 else wide
    lane = jnp.arange(wide)
    lane_head = jnp.where(lane < 2 * split, (lane % split) // (ROT // 2), (lane - 2 * split) // (HEAD - ROT))
    exponent = (lane[:slab] % (ROT // 2)).astype(f32) * 2.0 / ROT
    frequency = jnp.where(lane[:slab] < 2 * split, jnp.power(10000.0, -exponent), 0.0)
    sign = jnp.where(lane[:slab] < split, -1.0, 1.0)

    def tables(place):
        angles = place.astype(f32)[:, None] * frequency[None, :]
        return jnp.cos(angles), jnp.sin(angles) * sign[None, :]

    ordered = jnp.arange(group_rows, dtype=jnp.int32)
    place_packed = positions(ordered, lengths[0])[1]
    start = ordered - place_packed
    low = start[::BLOCK] // BLOCK
    start = start[None]
    cos_arrival, sin_arrival = tables(positions(packed, lengths[0])[1])
    cos_packed, sin_packed = tables(place_packed)
    prow, pcol = packed[None], packed[:, None]
    head_qk = (lane_head[None] == jnp.arange(heads)[:, None]).astype(bf16)
    head_v = ((lane // HEAD)[None] == jnp.arange(heads)[:, None]).astype(bf16)
    qmask = jnp.broadcast_to(head_qk[:, None, :], (heads, BLOCK, wide))
    vmask = jnp.broadcast_to(head_v[:, None, :], (heads, BLOCK, wide))
    ktmask = jnp.broadcast_to(head_qk[:, :, None], (heads, wide, BLOCK))

    order.did(second.ups[0], third_own, cos_arrival, sin_arrival, cos_packed, sin_packed)
    rows_in.arrive(order)
    first.arrive(order)

    first.start(order)
    rows_in.start_far()
    rows_in.arrive_far(order)
    rows_in.halves(order)
    first.arrive(order)
    first.rest(order)

    second.start(order)
    rows_in.start_last(order)
    rows_in.arrive_last(order)
    normed = rows_in.all(order)

    qkv_bias = jnp.broadcast_to(qkv_bias, (8, 3 * wide))
    qkv_packed, vt = pack(
        heads, z_ref, order.then(normed), qkv_bias, cos_arrival, sin_arrival, prow, first.sources()
    )
    order.did(qkv_packed)
    second.arrive(order)

    second.start(order)
    outt, lse, mixed = attend(heads, low, order.then(qkv_packed), vt, pcol, start, qmask)
    order.did(mixed)
    second.arrive(order)

    second.start(order)
    by_block = jnp.stack([at // half for at in block_of]).astype(jnp.int32)
    grads = reorder(by_block, order.then(grads_all), 2 * m)
    order.did(grads)
    mixed_grad = times(z_ref, order.then(grads), first.sources(), 3 * wide, wide)
    order.did(mixed_grad)
    dense_grad = lax.dot_general(grads, order.then(mixed), by_rows, preferred_element_type=f32).astype(bf16)
    order.did(dense_grad)
    second.arrive(order)
    second.rest(order)

    third = lax.all_gather(order.then(third_own), "fsdp", axis=0, tiled=True)
    up_bias = jnp.broadcast_to(up_bias[None], (8, up_bias.shape[0]))
    up, act = up_forward(z_ref, order.then(normed), up_bias, second.sources())
    order.did(act)
    to_slots = jnp.stack([lax.rem(z - f + n, n) for f in range(n)]).astype(jnp.int32)
    down_grad = lax.dot_general(grads, order.then(act), by_rows, preferred_element_type=f32).astype(bf16)
    order.did(down_grad)
    down_grad = reorder(to_slots, down_grad, n)
    order.did(down_grad)
    down_total = lax.psum_scatter(order.then(down_grad), "fsdp", scatter_dimension=0, tiled=True)

    qkv_grad_low, qkv_bias_sum = attend_back(
        heads, low, order.then(qkv_packed), outt, lse, mixed_grad, cos_packed, sin_packed, prow, pcol, start,
        qmask, vmask, ktmask,
    )
    order.did(qkv_grad_low)
    qkv_weight = lax.dot_general(
        normed, order.then(qkv_grad_low), by_rows, preferred_element_type=f32
    ).astype(bf16)
    first_sum = Scatter(join(qkv_weight, dense_grad, n))
    order.did(*first_sum.parts)

    third_sources = [order.arrive(third)]
    first_sum.start(order)
    up_grad_low, up_bias_sum = up_backward(z_ref, grads, order.then(up), third_sources)
    order.did(up_grad_low)
    keep, send = to_features(
        z_ref, order.then(mixed), first.sources(), 3 * wide, act, third_sources, half, width
    )
    order.did(keep)
    first_sum.arrive(order)

    first_sum.start(order)
    other = swap(order.then(send), "tp", 1)
    up_weight = lax.dot_general(
        normed, order.then(up_grad_low), by_rows, preferred_element_type=f32
    ).astype(bf16)
    order.did(up_weight)
    up_weight = reorder(to_slots, order.then(up_weight), n)
    order.did(up_weight)
    up_total = lax.psum_scatter(order.then(up_weight), "fsdp", scatter_dimension=0, tiled=True)
    keep, other = order.arrive((keep, other))

    branch_sum = RowSums(order.arrive(add(keep, other)))
    branch_sum.start_direct(order)
    keep, send = to_features(
        z_ref, order.then(qkv_grad_low), first.sources(), 0, up_grad_low, second.sources(), half, width
    )
    order.did(keep)
    first_sum.arrive(order)
    down_total = order.arrive(down_total)

    first_sum.start(order)
    other = swap(order.then(send), "tp", 1)
    source = order.then(lax.dynamic_slice_in_dim(hidden_in[0], t * half, half)).astype(f32)
    centred = source - jnp.mean(source, axis=-1, keepdims=True)
    rstd = lax.rsqrt(jnp.mean(centred * centred, axis=-1, keepdims=True) + EPSILON)
    xhat = centred * rstd
    order.did(xhat)
    keep, other = order.arrive((keep, other))
    row_sum = RowSums(order.arrive(add(keep, other)))
    branch_sum.arrive_last(order)

    row_sum.start(order)
    branch = turn(order.then(branch_sum.total()))
    biases = b_dense.astype(f32) + b_fc2.astype(f32)
    result = (source + branch + biases).astype(bf16)
    order.did(result)
    row_sum.arrive(order)

    row_sum.start_last(order)
    result_other = swap(order.then(result), "tp", 1)
    first_sum.arrive(order)
    first_sum.rest(order)
    row_sum.arrive_last(order)
    up_total = order.arrive(up_total)
    first_total = order.then(first_sum.total())
    qkv_sum = lax.dot_general(
        first_total[:, : 3 * wide], place_of, by_columns, preferred_element_type=f32
    ).astype(bf16)
    both = jnp.concatenate([qkv_sum, first_total[:, 3 * wide :], down_total], axis=1)
    order.did(both)
    pieces = spread_start(both)
    normed_grad = turn(row_sum.total())
    d = order.then(normed_grad) * gain_vec
    input_grad = rstd * (
        d - jnp.mean(d, axis=-1, keepdims=True) - xhat * jnp.mean(d * xhat, axis=-1, keepdims=True)
    ) + lax.dynamic_slice_in_dim(out_grad[0], t * half, half).astype(f32)
    norm_sums = jnp.concatenate([jnp.sum(normed_grad * xhat, axis=0), jnp.sum(normed_grad, axis=0)])
    order.did(input_grad, norm_sums)
    pieces = order.arrive(pieces)
    up_pieces = spread_start(order.then(up_total))
    input_other = swap(order.then(input_grad), "tp", 1)
    c_ref = jnp.full((1,), c, jnp.int32)
    qkv_part, dense_part, down_part = place(
        c_ref, order.then(pieces), [3 * wide, wide, w_fc2.shape[1] // m]
    )
    order.did(qkv_part)
    norm_sums = order.then(norm_sums)
    up_part = place(c_ref, order.arrive(up_pieces), [w_fc1.shape[1] // m])[0]

    def in_rows(own_half, other_half):
        return jnp.concatenate(
            [jnp.where(t == 0, own_half, other_half), jnp.where(t == 0, other_half, own_half)], axis=0
        )

    result = in_rows(result, result_other)
    input_grad = in_rows(input_grad, input_other)
    def placed(vector):
        full = jnp.zeros((vector.shape[0] * m,), f32)
        return lax.dynamic_update_slice_in_dim(full, vector, c * vector.shape[0], axis=0)

    qkv_bias_grad = lax.dot_general(
        qkv_bias_sum[:1], place_of.astype(f32), by_columns,
        precision=lax.Precision.HIGHEST, preferred_element_type=f32,
    )[0]
    norm_sums = norm_sums + swap(norm_sums, "tp", 1)
    sums = everywhere(
        jnp.concatenate([norm_sums, out_sum[0], placed(qkv_bias_grad), placed(up_bias_sum[0])]), "fsdp", "ctx"
    )
    gain_grad, shift_grad, out_bias_grad = sums[:width], sums[width : 2 * width], sums[2 * width : 3 * width]
    qkv_bias_grad = sums[3 * width : 3 * width + 3 * wide * m]
    up_bias_grad = sums[3 * width + 3 * wide * m :]
    return (
        result[None],
        input_grad[None],
        gain_grad,
        shift_grad,
        qkv_part,
        qkv_bias_grad,
        dense_part,
        out_bias_grad,
        up_part,
        up_bias_grad,
        down_part,
        out_bias_grad,
    )


def solution(mesh):
    in_specs = (
        P("fsdp", "ctx", None),
        P("fsdp", "ctx", None),
        P(),
        P(),
        P("fsdp", "tp"),
        P("tp"),
        P("fsdp", "tp"),
        P(),
        P("fsdp", "tp"),
        P("tp"),
        P("fsdp", "tp"),
        P(),
        P("fsdp", None),
        P("fsdp", None),
    )
    out_specs = (
        P("fsdp", "ctx", None),
        P("fsdp", "ctx", None),
        P(),
        P(),
        P(("fsdp", "ctx"), "tp"),
        P("tp"),
        P(("fsdp", "ctx"), "tp"),
        P(),
        P(("fsdp", "ctx"), "tp"),
        P("tp"),
        P(("fsdp", "ctx"), "tp"),
        P(),
    )
    return jax.shard_map(shards, mesh=mesh, in_specs=in_specs, out_specs=out_specs, check_vma=False)
```

```python
import functools
import math

import jax
import jax.numpy as jnp
from jax import lax
from jax.experimental import pallas as pl
from jax.experimental.pallas import tpu as pltpu
from jax.sharding import PartitionSpec as P

HEAD = 64
ROT = 32
MASKED = -1e30
EPSILON = 1e-05
f32 = jnp.float32
bf16 = jnp.bfloat16


def positions(packed, lengths):
    seq_ends = jnp.cumsum(lengths)
    starts = seq_ends - lengths
    segment = jnp.sum((packed[:, None] >= seq_ends[None, :]).astype(jnp.int32), axis=1)
    owner_mask = segment[:, None] == jnp.arange(lengths.shape[0], dtype=jnp.int32)[None, :]
    return (segment, packed - jnp.sum(jnp.where(owner_mask, starts[None, :], 0), axis=1))


def gelu_tanh(values):
    return jax.nn.gelu(values, approximate=True)


def swap(x, axis, bit):
    size = lax.axis_size(axis)
    return lax.ppermute(x, axis, [(i, i ^ bit) for i in range(size)])


def everywhere(x, *axes):
    for axis in axes:
        bit = 1
        while bit < lax.axis_size(axis):
            x = x + swap(x, axis, bit)
            bit *= 2
    return x


def after(x, *before):
    before = [item for item in before if item is not None]
    return lax.optimization_barrier((x, *before))[0] if before else x


class Order:
    def __init__(self):
        self.last = ()

    def then(self, x):
        return after(x, *self.last)

    def did(self, *values):
        self.last = values

    def arrive(self, values):
        values = after(values, *self.last)
        self.last = self.last + tuple(jax.tree.leaves(values))
        return values


def line_up(x, first, last):
    return lax.ppermute(x, "fsdp", [(i, i + 1) for i in range(first, last)])


def line_down(x, first, last):
    return lax.ppermute(x, "fsdp", [(i, i - 1) for i in range(first, last)])


class Gather:
    def __init__(self, own):
        self.ups, self.downs = [own], [own]

    def start(self, order):
        n, s = lax.axis_size("fsdp"), len(self.ups)
        if s < n:
            up, down = order.then((self.ups[-1], self.downs[-1]))
            self.ups.append(line_up(up, s - 1, n - 1))
            self.downs.append(line_down(down, 1, n - s + 1))

    def arrive(self, order):
        self.ups[-1], self.downs[-1] = order.arrive((self.ups[-1], self.downs[-1]))

    def rest(self, order):
        for _ in range(len(self.ups), lax.axis_size("fsdp")):
            self.start(order)
            self.arrive(order)

    def sources(self):
        return self.ups + self.downs[1:]


class Scatter:
    def __init__(self, parts):
        self.parts, self.sums, self.step = parts, None, 1

    def start(self, order):
        n, s = lax.axis_size("fsdp"), self.step
        if s < n:
            up, down = order.then((self.parts[s], self.parts[n - s]))
            if self.sums is not None:
                up, down = order.arrive((add(up, self.sums[0]), add(down, self.sums[1])))
            self.sums = line_up(up, 0, min(s, n - 1)), line_down(down, max(n - s, 1), n)
            self.step += 1

    def arrive(self, order):
        self.sums = order.arrive(self.sums)

    def rest(self, order):
        for _ in range(self.step, lax.axis_size("fsdp")):
            self.start(order)
            self.arrive(order)

    def total(self):
        up, down = self.sums
        return (self.parts[0].astype(f32) + up.astype(f32) + down.astype(f32)).astype(bf16)


class Rows:
    def __init__(self, mine):
        self.mine = mine

    def start(self, order):
        mine = order.then(self.mine)
        self.near = [swap(mine, "ctx", 1 << k) for k in range(lax.axis_size("ctx").bit_length() - 1)]

    def arrive(self, order):
        self.near = order.arrive(self.near)

    def start_far(self):
        m, quarter = lax.axis_size("ctx"), self.mine.shape[0] // 2
        if m == 4:
            first, second = self.near
            self.far = [swap(first[:quarter], "ctx", 2), swap(second[quarter:], "ctx", 1)]
        else:
            self.far = [swap(self.mine, "ctx", j) for j in range(1, m) if j & (j - 1)]

    def arrive_far(self, order):
        self.far = order.arrive(self.far)

    def halves(self, order):
        m = lax.axis_size("ctx")
        near, far = list(self.near), list(self.far)
        blocks = [self.mine]
        for j in range(1, m):
            if j & (j - 1) == 0:
                blocks.append(near.pop(0))
            elif m == 4:
                blocks += far
            else:
                blocks.append(far.pop(0))
        self.here = assemble(order.then(blocks))
        order.did(self.here)

    def start_last(self, order):
        self.there = swap(order.then(self.here), "tp", 1)

    def arrive_last(self, order):
        self.there = order.arrive(self.there)

    def all(self, order):
        full = assemble(order.then([self.here, self.there]))
        order.did(full)
        return full


class RowSums:
    def __init__(self, slots):
        self.slots = [slots[j] for j in range(slots.shape[0])]

    def start_direct(self, order):
        slots = order.then(self.slots)
        self.got, self.last = [], [swap(slots[j], "ctx", j) for j in range(1, len(slots))]

    def start(self, order):
        m, slots = len(self.slots), order.then(self.slots)
        quarter = slots[0].shape[0] // 2
        if m == 4:
            self.got = [swap(slots[3][:quarter], "ctx", 2), swap(slots[3][quarter:], "ctx", 1)]
        else:
            self.got = [swap(slots[j], "ctx", j) for j in range(1, m) if j & (j - 1)]

    def arrive(self, order):
        self.got = order.arrive(self.got)

    def start_last(self, order):
        m, slots = len(self.slots), order.then(self.slots)
        quarter = slots[0].shape[0] // 2
        if m == 4:
            first = jnp.concatenate([add(slots[1][:quarter], self.got[0]), slots[1][quarter:]], axis=0)
            second = jnp.concatenate([slots[2][:quarter], add(slots[2][quarter:], self.got[1])], axis=0)
            first, second = order.arrive((first, second))
            self.last, self.got = [swap(first, "ctx", 1), swap(second, "ctx", 2)], []
        else:
            self.last = [swap(slots[j], "ctx", j) for j in range(1, m) if j & (j - 1) == 0]

    def arrive_last(self, order):
        self.last, self.slots[0] = order.arrive((self.last, self.slots[0]))

    def total(self):
        return sum((x.astype(f32) for x in self.got + self.last), self.slots[0].astype(f32))


def add(a, b):
    return (a.astype(f32) + b.astype(f32)).astype(bf16)


def spread_start(block):
    m = lax.axis_size("ctx")
    c = lax.axis_index("ctx")
    rows = block.shape[0] // m
    pieces = []
    for j in range(m):
        piece = lax.dynamic_slice_in_dim(block, (c ^ j) * rows, rows, axis=0)
        pieces.append(piece if j == 0 else swap(piece, "ctx", j))
    return pieces


def column_order(heads):
    order = []
    for part in range(2):
        for start, width in ((0, ROT // 2), (ROT // 2, ROT // 2), (ROT, HEAD - ROT)):
            for head in range(heads):
                base = (head * 3 + part) * HEAD + start
                order += list(range(base, base + width))
    for head in range(heads):
        base = (head * 3 + 2) * HEAD
        order += list(range(base, base + HEAD))
    return order


BLOCK = 256
NT = (((1,), (1,)), ((), ()))


def mm(a, b, dims=(((1,), (0,)), ((), ()))):
    return lax.dot_general(a, b, dims, preferred_element_type=f32)


def turned(x, cosine, sine, split):
    slab = cosine.shape[1]
    front = x[:, :slab]
    if slab == 2 * split:
        partner = pltpu.roll(front, split, 1)
    else:
        lane = lax.broadcasted_iota(jnp.int32, front.shape, 1)
        partner = jnp.where(
            lane < split, pltpu.roll(front, slab - split, 1), pltpu.roll(front, split, 1)
        )
    front = front * cosine + partner * sine
    if slab == x.shape[1]:
        return front
    return jnp.concatenate([front, x[:, slab:]], axis=1)


def to_packed(prow_ref, block, data):
    shape = (BLOCK, prow_ref.shape[1])
    at = lax.broadcasted_iota(jnp.int32, shape, 0) + block * BLOCK
    return mm((at == prow_ref[...]).astype(f32).astype(bf16), data)


def to_arrival(pcol_ref, block, data):
    rows = pl.ds(pl.multiple_of(block * BLOCK, BLOCK), BLOCK)
    shape = (BLOCK, data.shape[0])
    at = lax.broadcasted_iota(jnp.int32, shape, 1)
    return mm((at == pcol_ref[rows, :]).astype(f32).astype(bf16), data)


def kept(i, j, start):
    keys = lax.broadcasted_iota(jnp.int32, (BLOCK, BLOCK), 0) + j * BLOCK
    queries = lax.broadcasted_iota(jnp.int32, (BLOCK, BLOCK), 1) + i * BLOCK
    return (keys >= start) & (keys <= queries)


def fetch(z_ref, sources, weight_ref, sems, first):
    feat, cols = sources[0].shape[0], weight_ref.shape[1]
    if len(sources) == 1:
        feat = weight_ref.shape[0] // sems.shape[0]
    n = weight_ref.shape[0] // feat

    def copy(source, s):
        rows = pl.ds(s * feat, feat)
        return pltpu.make_async_copy(
            source.at[:, pl.ds(first, cols)], weight_ref.at[rows, :], sems.at[s]
        )

    def each(do):
        if len(sources) == 1:
            for s in range(n):
                block = pl.multiple_of(lax.rem(z_ref[0] - s + n, n) * feat, feat)
                do(copy(sources[0].at[pl.ds(block, feat), :], s))
            return
        do(copy(sources[0], 0))
        for s in range(1, n):

            @pl.when(z_ref[0] >= s)
            def _():
                do(copy(sources[s], s))

            @pl.when(z_ref[0] < s)
            def _():
                do(copy(sources[2 * n - 1 - s], s))

    each(lambda c: c.start())
    each(lambda c: c.wait())


def pack_kernel(heads, count, z_ref, x_in_ref, bias_ref, cos_ref, sin_ref, prow_ref, *rest):
    sources, (packed_ref, vt_ref, x_ref, weight_ref, sems) = rest[:count], rest[count:]
    wide = vt_ref.shape[0]
    blocks = x_ref.shape[0] // BLOCK
    split = ROT // 2 * heads
    r = pl.program_id(0)

    @pl.when(r == 0)
    def _():
        fetch(z_ref, sources, weight_ref, sems, 0)

    rows = pl.ds(pl.multiple_of(r * BLOCK, BLOCK), BLOCK)
    cosine, sine = cos_ref[rows, :], sin_ref[rows, :]
    x_in = x_in_ref[...]
    for part in range(3):
        at = slice(part * wide, (part + 1) * wide)
        x = mm(x_in, weight_ref[:, at]) + bias_ref[0:1, at]
        if part < 2:
            x = turned(x, cosine, sine, split)
        if part == 0:
            x = x * (1.0 / math.sqrt(HEAD))
        x_ref[rows, at] = x.astype(bf16)

    @pl.when(r == blocks - 1)
    def _():
        @pl.loop(0, blocks)
        def _(p):
            rows = pl.ds(pl.multiple_of(p * BLOCK, BLOCK), BLOCK)
            y = to_packed(prow_ref, p, x_ref[...])
            packed_ref[rows, :] = y.astype(bf16)
            vt_ref[:, rows] = y[:, 2 * wide :].T.astype(bf16)


def curve(u):
    square = u * u
    return jnp.tanh(math.sqrt(2.0 / math.pi) * (u + 0.044715 * (square * u))), square


def up_kernel(count, z_ref, x_ref, bias_ref, *rest):
    sources, (up_ref, act_ref, weight_ref, sems) = rest[:count], rest[count:]

    @pl.when(pl.program_id(0) == 0)
    def _():
        fetch(z_ref, sources, weight_ref, sems, 0)

    x = x_ref[...]
    step = min(256, up_ref.shape[1])
    for at in range(0, up_ref.shape[1], step):
        at = slice(at, at + step)
        u = mm(x, weight_ref[:, at]) + bias_ref[0:1, at]
        up_ref[:, at] = u
        act_ref[:, at] = (0.5 * u * (1.0 + curve(u)[0])).astype(bf16)


def up_back_kernel(count, z_ref, x_ref, up_ref, *rest):
    sources, (grad_ref, sum_ref, weight_ref, sems) = rest[:count], rest[count:]

    @pl.when(pl.program_id(0) == 0)
    def _():
        fetch(z_ref, sources, weight_ref, sems, 0)
        sum_ref[...] = jnp.zeros(sum_ref.shape, f32)

    x = x_ref[...]
    step = min(256, grad_ref.shape[1])
    for at in range(0, grad_ref.shape[1], step):
        at = slice(at, at + step)
        u = up_ref[:, at]
        bend, square = curve(u)
        slope = 0.5 * (1.0 + bend) + (0.5 * math.sqrt(2.0 / math.pi)) * u * (
            (1.0 - bend * bend) * (1.0 + (3.0 * 0.044715) * square)
        )
        grad = mm(x, weight_ref[:, at]) * slope
        grad_ref[:, at] = grad.astype(bf16)
        sum_ref[0:1, at] = sum_ref[0:1, at] + jnp.sum(grad, axis=0, keepdims=True)


def plain_kernel(count, first, z_ref, x_ref, *rest):
    sources, (out_ref, weight_ref, sems) = rest[:count], rest[count:]

    @pl.when(pl.program_id(0) == 0)
    def _():
        fetch(z_ref, sources, weight_ref, sems, first)

    out_ref[...] = mm(x_ref[...], weight_ref[...]).astype(bf16)


def spread_kernel(count, first, z_ref, a_ref, b_ref, *rest):
    a_sources, b_sources = rest[: count[0]], rest[count[0] : sum(count)]
    keep_ref, send_ref, a_weight_ref, b_weight_ref, sems = rest[sum(count) :]

    @pl.when(pl.program_id(0) == 0)
    def _():
        fetch(z_ref, a_sources, a_weight_ref, sems, first)
        fetch(z_ref, b_sources, b_weight_ref, sems, 0)

    slots, half, width = keep_ref.shape
    steps = pl.num_programs(0) // 2

    def write(out_ref):
        for slot in range(slots):
            rows = slice(slot * half, (slot + 1) * half)
            a, b = a_ref[rows, :], b_ref[rows, :]
            for at in range(0, width, 256):
                at = slice(at, at + 256)
                out = mm(a, a_weight_ref[at, :], NT) + mm(b, b_weight_ref[at, :], NT)
                out_ref[slot, :, at] = out.astype(bf16)

    @pl.when(pl.program_id(0) < steps)
    def _():
        write(keep_ref)

    @pl.when(pl.program_id(0) >= steps)
    def _():
        write(send_ref)


def forward_kernel(
    heads, low_ref, packed_ref, vt_ref, pcol_ref, start_ref, qmask_ref,
    outt_ref, lse_ref, mixed_ref, mp_ref,
):
    rows_all, wide = mixed_ref.shape
    blocks = rows_all // BLOCK

    @pl.loop(0, blocks)
    def _(i):
        rows = pl.ds(pl.multiple_of(i * BLOCK, BLOCK), BLOCK)
        start = start_ref[0:1, rows]
        q = packed_ref[rows, :wide]
        qs = jnp.concatenate([q * qmask_ref[h] for h in range(heads)], axis=0)

        def step(j, carried):
            keys = pl.ds(pl.multiple_of(j * BLOCK, BLOCK), BLOCK)
            k = packed_ref[keys, wide : 2 * wide]
            keep = kept(i, j, start)
            scores = mm(k, qs, NT)
            after = []
            for h in range(heads):
                top, total, acc = carried[h]
                s = jnp.where(keep, scores[:, h * BLOCK : (h + 1) * BLOCK], MASKED)
                new_top = jnp.maximum(top, jnp.max(s, axis=0, keepdims=True))
                p = jnp.exp(s - new_top)
                alpha = jnp.exp(top - new_top)
                total = total * alpha + jnp.sum(p, axis=0, keepdims=True)
                acc = acc * alpha + mm(vt_ref[h * HEAD : (h + 1) * HEAD, keys], p.astype(bf16))
                after.append((new_top, total, acc))
            return tuple(after)

        begin = tuple(
            (
                jnp.full((1, BLOCK), MASKED, f32),
                jnp.zeros((1, BLOCK), f32),
                jnp.zeros((HEAD, BLOCK), f32),
            )
            for _ in range(heads)
        )
        state = lax.fori_loop(low_ref[i], i + 1, step, begin)
        out = jnp.concatenate([acc / total for _, total, acc in state], axis=0)
        outt_ref[:, rows] = out
        mp_ref[rows, :] = out.T.astype(bf16)
        lse = [top + jnp.log(total) for top, total, _ in state]
        lse_ref[:, rows] = jnp.concatenate(lse + [jnp.zeros((8 - heads, BLOCK), f32)], axis=0)

    @pl.loop(0, blocks)
    def _(r):
        rows = pl.ds(pl.multiple_of(r * BLOCK, BLOCK), BLOCK)
        mixed_ref[rows, :] = to_arrival(pcol_ref, r, mp_ref[...]).astype(bf16)


def backward_kernel(
    heads, low_ref, packed_ref, outt_ref, lse_ref, grad_ref, cos_ref, sin_ref, prow_ref, pcol_ref, start_ref,
    qmask_ref, vmask_ref, ktmask_ref,
    qkv_grad_ref, bias_grad_ref, kt_ref, dk_ref, dv_ref, dq_ref, gp_ref,
):
    rows_all, wide = grad_ref.shape
    blocks = rows_all // BLOCK
    split = ROT // 2 * heads

    @pl.loop(0, blocks)
    def _(p):
        rows = pl.ds(pl.multiple_of(p * BLOCK, BLOCK), BLOCK)
        gp_ref[rows, :wide] = to_packed(prow_ref, p, grad_ref[...]).astype(bf16)
        kt_ref[:, rows] = packed_ref[rows, wide : 2 * wide].astype(f32).T.astype(bf16)
        dk_ref[rows, :] = jnp.zeros((BLOCK, wide), f32)
        dv_ref[rows, :] = jnp.zeros((BLOCK, wide), f32)

    @pl.loop(0, blocks)
    def _(i):
        rows = pl.ds(pl.multiple_of(i * BLOCK, BLOCK), BLOCK)
        start = start_ref[0:1, rows]
        q = packed_ref[rows, :wide]
        g = gp_ref[rows, :wide]
        qs = jnp.concatenate([q * qmask_ref[h] for h in range(heads)], axis=0)
        gs = jnp.concatenate([g * vmask_ref[h] for h in range(heads)], axis=0)
        product = g.astype(f32).T * outt_ref[:, rows]
        inner = [
            jnp.sum(product[h * HEAD : (h + 1) * HEAD], axis=0, keepdims=True) for h in range(heads)
        ]
        lse = [lse_ref[h : h + 1, rows] for h in range(heads)]

        def step(j, dqt):
            keys = pl.ds(pl.multiple_of(j * BLOCK, BLOCK), BLOCK)
            k = packed_ref[keys, wide : 2 * wide]
            v = packed_ref[keys, 2 * wide :]
            kt = kt_ref[:, keys]
            keep = kept(i, j, start)
            scores = mm(k, qs, NT)
            slopes = mm(v, gs, NT)
            probs, flows = [], []
            for h in range(heads):
                at = slice(h * BLOCK, (h + 1) * BLOCK)
                p = jnp.exp(jnp.where(keep, scores[:, at], MASKED) - lse[h])
                probs.append(p.astype(bf16))
                flows.append((p * (slopes[:, at] - inner[h])).astype(bf16))
            dv_ref[keys, :] = dv_ref[keys, :] + mm(jnp.concatenate(probs, axis=1), gs)
            dk_ref[keys, :] = dk_ref[keys, :] + mm(jnp.concatenate(flows, axis=1), qs)
            kts = jnp.concatenate([kt * ktmask_ref[h] for h in range(heads)], axis=1)
            return dqt + mm(kts, jnp.concatenate(flows, axis=0))

        dqt = lax.fori_loop(low_ref[i], i + 1, step, jnp.zeros((wide, BLOCK), f32))
        dq_ref[rows, :] = dqt.T * (1.0 / math.sqrt(HEAD))

    bias_grad_ref[...] = jnp.zeros(bias_grad_ref.shape, f32)

    @pl.loop(0, blocks)
    def _(p):
        rows = pl.ds(pl.multiple_of(p * BLOCK, BLOCK), BLOCK)
        cosine, sine = cos_ref[rows, :], -sin_ref[rows, :]
        dq = turned(dq_ref[rows, :], cosine, sine, split)
        dk = turned(dk_ref[rows, :], cosine, sine, split)
        full = jnp.concatenate([dq, dk, dv_ref[rows, :]], axis=1)
        bias_grad_ref[0:1, :] = bias_grad_ref[0:1, :] + jnp.sum(full, axis=0, keepdims=True)
        gp_ref[rows, :] = full.astype(bf16)

    @pl.loop(0, blocks)
    def _(r):
        rows = pl.ds(pl.multiple_of(r * BLOCK, BLOCK), BLOCK)
        qkv_grad_ref[rows, :] = to_arrival(pcol_ref, r, gp_ref[...]).astype(bf16)


def whole(count):
    return [pl.BlockSpec(memory_space=pltpu.VMEM)] * count


COST = 0.05


def blocks_call(kernel, name, z, ins, in_specs, sources, outs, out_specs, scratch, steps, flops, weight_shapes):
    sems = lax.axis_size("fsdp")
    return pl.pallas_call(
        kernel,
        grid_spec=pltpu.PrefetchScalarGridSpec(
            num_scalar_prefetch=1,
            grid=(steps,),
            in_specs=in_specs + [pl.BlockSpec(memory_space=pl.ANY)] * sum(map(len, sources)),
            out_specs=out_specs,
            scratch_shapes=scratch
            + [pltpu.VMEM(shape, bf16) for shape in weight_shapes]
            + [pltpu.SemaphoreType.DMA((sems,))],
        ),
        out_shape=outs,
        compiler_params=pltpu.CompilerParams(vmem_limit_bytes=48 * 2**20),
        cost_estimate=pl.CostEstimate(flops=int(COST * flops), bytes_accessed=2**20, transcendentals=0),
        name=name,
    )(z, *ins, *[x for group in sources for x in group])


def fixed(shape):
    return pl.BlockSpec(shape, lambda *_: (0,) * len(shape))


def by_row(rows, cols):
    return pl.BlockSpec((rows, cols), lambda i, *_: (i, 0))


def prepare_kernel(norm, slots, at_ref, x_ref, gain_ref, shift_ref, out_ref, *rest):
    rows, width = x_ref.shape
    half, step = rows // 2, 64
    feat = width // slots

    @pl.loop(0, half // step)
    def _(b):
        source = pl.ds(pl.multiple_of(at_ref[1] * half + b * step, step), step)
        target = pl.ds(pl.multiple_of(b * step, step), step)
        if norm:
            x = x_ref[source, :].astype(f32)
            mean = jnp.mean(x, axis=-1, keepdims=True)
            centred = x - mean
            rstd = lax.rsqrt(jnp.mean(centred * centred, axis=-1, keepdims=True) + EPSILON)
        for s in range(slots):
            block = lax.rem(at_ref[0] - s + slots, slots)
            columns = pl.ds(pl.multiple_of(block * feat, feat), feat)
            y = x_ref[source, columns]
            if norm:
                y = (y.astype(f32) - mean) * rstd * gain_ref[0:1, columns] + shift_ref[0:1, columns]
            out_ref[target, s * feat : (s + 1) * feat] = y.astype(bf16)

    if not norm:
        sum_ref = rest[0]
        sum_ref[...] = jnp.zeros(sum_ref.shape, f32)

        @pl.loop(0, rows // step)
        def _(b):
            source = pl.ds(pl.multiple_of(b * step, step), step)
            x = x_ref[source, :].astype(f32)
            sum_ref[0:1, :] = sum_ref[0:1, :] + jnp.sum(x, axis=0, keepdims=True)


def prepare(norm, at, x, gain, shift, n):
    rows, width = x.shape
    out = [jax.ShapeDtypeStruct((rows // 2, width), bf16)]
    if not norm:
        out.append(jax.ShapeDtypeStruct((8, width), f32))
    return pl.pallas_call(
        functools.partial(prepare_kernel, norm, n),
        grid_spec=pltpu.PrefetchScalarGridSpec(
            num_scalar_prefetch=1, grid=(), in_specs=whole(3), out_specs=whole(len(out))
        ),
        out_shape=out,
        compiler_params=pltpu.CompilerParams(vmem_limit_bytes=40 * 2**20),
        cost_estimate=pl.CostEstimate(flops=2**20, bytes_accessed=2**20, transcendentals=0),
        name="prepare",
    )(at, x, gain, shift)


def place_kernel(count, at_ref, *refs):
    pieces, outs = refs[:count], refs[count:]
    for j, piece in enumerate(pieces):
        first = 0
        for out_ref in outs:
            cols = out_ref.shape[1] // count
            target = pl.ds(pl.multiple_of((at_ref[0] ^ j) * cols, cols), cols)
            out_ref[:, target] = piece[:, first : first + cols].astype(f32)
            first += cols


def place(c, pieces, widths):
    count, rows = len(pieces), pieces[0].shape[0]
    return pl.pallas_call(
        functools.partial(place_kernel, count),
        grid_spec=pltpu.PrefetchScalarGridSpec(
            num_scalar_prefetch=1, grid=(), in_specs=whole(count), out_specs=whole(len(widths))
        ),
        out_shape=[jax.ShapeDtypeStruct((rows, count * cols), f32) for cols in widths],
        compiler_params=pltpu.CompilerParams(vmem_limit_bytes=40 * 2**20),
        cost_estimate=pl.CostEstimate(flops=2**20, bytes_accessed=2**20, transcendentals=0),
        name="place",
    )(c, *pieces)


def join_kernel(a_ref, b_ref, *outs):
    cols = a_ref.shape[1]
    for s, out_ref in enumerate(outs):

        @pl.when(pl.program_id(0) == s)
        def _():
            out_ref[:, :cols] = a_ref[...]
            out_ref[:, cols:] = b_ref[...]


def join(a, b, n):
    rows, cols = a.shape[0] // n, a.shape[1] + b.shape[1]
    return pl.pallas_call(
        join_kernel,
        grid=(n,),
        in_specs=[
            pl.BlockSpec((rows, a.shape[1]), lambda i: (i, 0)),
            pl.BlockSpec((rows, b.shape[1]), lambda i: (i, 0)),
        ],
        out_specs=[pl.BlockSpec((rows, cols), lambda i: (0, 0))] * n,
        out_shape=[jax.ShapeDtypeStruct((rows, cols), bf16)] * n,
        compiler_params=pltpu.CompilerParams(vmem_limit_bytes=40 * 2**20),
        cost_estimate=pl.CostEstimate(flops=2**20, bytes_accessed=2**20, transcendentals=0),
        name="join",
    )(a, b)


def reorder(order, x, blocks):
    rows, cols = x.shape[0] // blocks, x.shape[1]

    def copy_kernel(order_ref, x_ref, out_ref):
        out_ref[...] = x_ref[...]

    return pl.pallas_call(
        copy_kernel,
        grid_spec=pltpu.PrefetchScalarGridSpec(
            num_scalar_prefetch=1,
            grid=(blocks,),
            in_specs=[pl.BlockSpec((rows, cols), lambda i, order_ref: (order_ref[i], 0))],
            out_specs=pl.BlockSpec((rows, cols), lambda i, order_ref: (i, 0)),
        ),
        out_shape=jax.ShapeDtypeStruct(x.shape, x.dtype),
        compiler_params=pltpu.CompilerParams(vmem_limit_bytes=60 * 2**20),
        cost_estimate=pl.CostEstimate(flops=2**20, bytes_accessed=2**20, transcendentals=0),
        name="reorder",
    )(order, x)


def assemble_kernel(*refs):
    *pieces, out_ref, sems = refs

    def each(do):
        first = 0
        for k, piece in enumerate(pieces):
            count = piece.shape[0]
            do(pltpu.make_async_copy(piece, out_ref.at[pl.ds(first, count), :], sems.at[k]))
            first += count

    each(lambda copy: copy.start())
    each(lambda copy: copy.wait())


def assemble(pieces):
    rows = sum(piece.shape[0] for piece in pieces)
    return pl.pallas_call(
        assemble_kernel,
        in_specs=whole(len(pieces)),
        out_specs=pl.BlockSpec(memory_space=pl.ANY),
        scratch_shapes=[pltpu.SemaphoreType.DMA((len(pieces),))],
        out_shape=jax.ShapeDtypeStruct((rows, pieces[0].shape[1]), bf16),
        compiler_params=pltpu.CompilerParams(vmem_limit_bytes=60 * 2**20),
        cost_estimate=pl.CostEstimate(flops=2**20, bytes_accessed=2**20, transcendentals=0),
        name="assemble",
    )(*pieces)


def pack(heads, z, normed, bias, cosine, sine, prow, sources):
    rows, width = normed.shape
    wide = heads * HEAD
    slab = cosine.shape[1]
    return blocks_call(
        functools.partial(pack_kernel, heads, len(sources)), "pack", z,
        [normed, bias, cosine, sine, prow],
        [by_row(BLOCK, width), fixed(bias.shape), fixed((rows, slab)), fixed((rows, slab)), fixed(prow.shape)],
        [sources],
        [jax.ShapeDtypeStruct((rows, 3 * wide), bf16), jax.ShapeDtypeStruct((wide, rows), bf16)],
        [fixed((rows, 3 * wide)), fixed((wide, rows))],
        [pltpu.VMEM((rows, 3 * wide), bf16)],
        rows // BLOCK, 12 * rows * rows * wide, [(width, 3 * wide)],
    )


def up_forward(z, normed, bias, sources):
    rows, width = normed.shape
    cols = bias.shape[1]
    return blocks_call(
        functools.partial(up_kernel, len(sources)), "up", z,
        [normed, bias], [by_row(512, width), fixed(bias.shape)], [sources],
        [jax.ShapeDtypeStruct((rows, cols), f32), jax.ShapeDtypeStruct((rows, cols), bf16)],
        [by_row(512, cols), by_row(512, cols)], [],
        rows // 512, 2 * rows * width * cols, [(width, cols)],
    )


def up_backward(z, grads, up, sources):
    rows, width = grads.shape
    cols = up.shape[1]
    return blocks_call(
        functools.partial(up_back_kernel, len(sources)), "up_back", z,
        [grads, up], [by_row(512, width), by_row(512, cols)], [sources],
        [jax.ShapeDtypeStruct((rows, cols), bf16), jax.ShapeDtypeStruct((8, cols), f32)],
        [by_row(512, cols), fixed((8, cols))], [],
        rows // 512, 2 * rows * width * cols, [(width, cols)],
    )


def times(z, x, sources, first, cols):
    rows, width = x.shape
    return blocks_call(
        functools.partial(plain_kernel, len(sources), first), "times", z,
        [x], [by_row(512, width)], [sources],
        [jax.ShapeDtypeStruct((rows, cols), bf16)], [by_row(512, cols)], [],
        rows // 512, 2 * rows * width * cols, [(width, cols)],
    )[0]


def to_features(z, a, a_sources, first, b, b_sources, half, width):
    rows = a.shape[0]
    slots, each = rows // (2 * half), 512 // half
    steps = slots // each
    a_cols, b_cols = a.shape[1], b.shape[1]
    out = jax.ShapeDtypeStruct((slots, half, width), bf16)
    block = (each, half, width)
    return blocks_call(
        functools.partial(spread_kernel, (len(a_sources), len(b_sources)), first), "to_features", z,
        [a, b], [by_row(512, a_cols), by_row(512, b_cols)], [a_sources, b_sources],
        [out, out],
        [
            pl.BlockSpec(block, lambda i, *_: (jnp.minimum(i, steps - 1), 0, 0)),
            pl.BlockSpec(block, lambda i, *_: (jnp.maximum(i - steps, 0), 0, 0)),
        ],
        [], 2 * steps, 2 * rows * width * (a_cols + b_cols), [(width, a_cols), (width, b_cols)],
    )


def attend(heads, low, packed, vt, pcol, start, qmask):
    rows, wide = packed.shape[0], heads * HEAD
    pairs = (rows // BLOCK) * 4 * heads * BLOCK * BLOCK
    return pl.pallas_call(
        functools.partial(forward_kernel, heads),
        grid_spec=pltpu.PrefetchScalarGridSpec(
            num_scalar_prefetch=1,
            grid=(),
            in_specs=whole(5),
            out_specs=whole(3),
            scratch_shapes=[pltpu.VMEM((rows, wide), bf16)],
        ),
        out_shape=[
            jax.ShapeDtypeStruct((wide, rows), f32),
            jax.ShapeDtypeStruct((8, rows), f32),
            jax.ShapeDtypeStruct((rows, wide), bf16),
        ],
        compiler_params=pltpu.CompilerParams(vmem_limit_bytes=60 * 2**20),
        cost_estimate=pl.CostEstimate(
            flops=2 * rows * rows * wide + pairs * 4 * wide, bytes_accessed=20 * rows * wide, transcendentals=pairs
        ),
        name="attend_forward",
    )(low, packed, vt, pcol, start, qmask)


def attend_back(heads, low, packed, outt, lse, grad, cosine, sine, prow, pcol, start, qmask, vmask, ktmask):
    rows, wide = grad.shape
    pairs = (rows // BLOCK) * 4 * heads * BLOCK * BLOCK
    return pl.pallas_call(
        functools.partial(backward_kernel, heads),
        grid_spec=pltpu.PrefetchScalarGridSpec(
            num_scalar_prefetch=1,
            grid=(),
            in_specs=whole(12),
            out_specs=whole(2),
            scratch_shapes=[
                pltpu.VMEM((wide, rows), bf16),
                pltpu.VMEM((rows, wide), f32),
                pltpu.VMEM((rows, wide), f32),
                pltpu.VMEM((rows, wide), f32),
                pltpu.VMEM((rows, 3 * wide), bf16),
            ],
        ),
        out_shape=[
            jax.ShapeDtypeStruct((rows, 3 * wide), bf16),
            jax.ShapeDtypeStruct((8, 3 * wide), f32),
        ],
        compiler_params=pltpu.CompilerParams(vmem_limit_bytes=60 * 2**20),
        cost_estimate=pl.CostEstimate(
            flops=8 * rows * rows * wide + pairs * 10 * wide, bytes_accessed=20 * rows * wide, transcendentals=pairs
        ),
        name="attend_backward",
    )(low, packed, outt, lse, grad, cosine, sine, prow, pcol, start, qmask, vmask, ktmask)


def shards(
    hidden_in,
    out_grad,
    ln_gain,
    ln_bias,
    w_qkv,
    b_qkv,
    w_dense,
    b_dense,
    w_fc1,
    b_fc1,
    w_fc2,
    b_fc2,
    lengths,
    assignment,
):
    n = lax.axis_size("fsdp")
    m = lax.axis_size("ctx")
    z = lax.axis_index("fsdp")
    c = lax.axis_index("ctx")
    t = lax.axis_index("tp")
    rows, width = hidden_in.shape[1], hidden_in.shape[2]
    half = rows // 2
    group_rows = rows * m
    feat = width // n
    heads = w_qkv.shape[1] // (3 * HEAD) // m
    wide = heads * HEAD
    by_columns = (((1,), (1,)), ((), ()))
    by_rows = (((0,), (0,)), ((), ()))

    def turn(x):
        return jnp.concatenate(
            [lax.dynamic_slice_in_dim(x, lax.rem(z - s + n, n) * feat, feat, axis=1) for s in range(n)],
            axis=1,
        )

    def by_slots(left, right):
        return [
            lax.dot_general(
                left[:, s * feat : (s + 1) * feat], right, by_rows, preferred_element_type=f32
            ).astype(bf16)
            for s in range(n)
        ]

    def mine(weight):
        share = weight.shape[-1] // m
        return lax.dynamic_slice_in_dim(weight, c * share, share, axis=weight.ndim - 1)

    listed = jnp.array(column_order(heads), jnp.int32)
    place_of = (jnp.arange(3 * wide, dtype=jnp.int32)[:, None] == listed[None, :]).astype(bf16)
    qkv_bias = jnp.dot(mine(b_qkv)[None], place_of, preferred_element_type=f32)
    up_bias = mine(b_fc1).astype(f32)

    order = Order()
    z_ref = jnp.full((1,), z, jnp.int32)
    qkv_own = jnp.dot(mine(w_qkv), place_of, preferred_element_type=f32).astype(bf16)
    first = Gather(jnp.concatenate([qkv_own, mine(w_dense)], axis=1))
    first.start(order)

    at = jnp.stack([z, t]).astype(jnp.int32)
    gain_vec = ln_gain.astype(f32)
    shift_vec = ln_bias.astype(f32)
    gain_row = jnp.broadcast_to(gain_vec[None], (8, width))
    shift_row = jnp.broadcast_to(shift_vec[None], (8, width))
    normed_own = prepare(True, at, after(hidden_in[0], first.ups[0]), gain_row, shift_row, n)[0]
    order.did(normed_own)
    rows_in = Rows(normed_own)
    rows_in.start(order)
    grads_own, out_sum = prepare(False, at, order.then(out_grad[0]), gain_row, shift_row, n)
    order.did(grads_own)
    grads_all = lax.all_gather(grads_own, ("ctx", "tp"), axis=0, tiled=True)
    first.arrive(order)

    first.start(order)
    w_fc1, w_fc2 = order.then((w_fc1, w_fc2))
    second = Gather(mine(w_fc1))
    third_own = mine(w_fc2)
    assignment, lengths = order.then((assignment, lengths))

    block_of = [((c ^ j) * 2 + (t ^ h)) * half for h in range(2) for j in range(m)]
    packed = jnp.concatenate(
        [lax.dynamic_slice_in_dim(assignment[0], at, half) for at in block_of]
    )
    split = ROT // 2 * heads
    slab = 2 * split if 2 * split % 128 == 0 else wide
    lane = jnp.arange(wide)
    lane_head = jnp.where(lane < 2 * split, (lane % split) // (ROT // 2), (lane - 2 * split) // (HEAD - ROT))
    exponent = (lane[:slab] % (ROT // 2)).astype(f32) * 2.0 / ROT
    frequency = jnp.where(lane[:slab] < 2 * split, jnp.power(10000.0, -exponent), 0.0)
    sign = jnp.where(lane[:slab] < split, -1.0, 1.0)

    def tables(place):
        angles = place.astype(f32)[:, None] * frequency[None, :]
        return jnp.cos(angles), jnp.sin(angles) * sign[None, :]

    ordered = jnp.arange(group_rows, dtype=jnp.int32)
    place_packed = positions(ordered, lengths[0])[1]
    start = ordered - place_packed
    low = start[::BLOCK] // BLOCK
    start = start[None]
    cos_arrival, sin_arrival = tables(positions(packed, lengths[0])[1])
    cos_packed, sin_packed = tables(place_packed)
    prow, pcol = packed[None], packed[:, None]
    head_qk = (lane_head[None] == jnp.arange(heads)[:, None]).astype(bf16)
    head_v = ((lane // HEAD)[None] == jnp.arange(heads)[:, None]).astype(bf16)
    qmask = jnp.broadcast_to(head_qk[:, None, :], (heads, BLOCK, wide))
    vmask = jnp.broadcast_to(head_v[:, None, :], (heads, BLOCK, wide))
    ktmask = jnp.broadcast_to(head_qk[:, :, None], (heads, wide, BLOCK))

    order.did(second.ups[0], third_own, cos_arrival, sin_arrival, cos_packed, sin_packed)
    rows_in.arrive(order)
    first.arrive(order)

    first.start(order)
    rows_in.start_far()
    rows_in.arrive_far(order)
    rows_in.halves(order)
    first.arrive(order)
    first.rest(order)

    second.start(order)
    rows_in.start_last(order)
    rows_in.arrive_last(order)
    normed = rows_in.all(order)

    qkv_bias = jnp.broadcast_to(qkv_bias, (8, 3 * wide))
    qkv_packed, vt = pack(
        heads, z_ref, order.then(normed), qkv_bias, cos_arrival, sin_arrival, prow, first.sources()
    )
    order.did(qkv_packed)
    second.arrive(order)

    second.start(order)
    outt, lse, mixed = attend(heads, low, order.then(qkv_packed), vt, pcol, start, qmask)
    order.did(mixed)
    second.arrive(order)

    second.start(order)
    by_block = jnp.stack([at // half for at in block_of]).astype(jnp.int32)
    grads = reorder(by_block, order.then(grads_all), 2 * m)
    order.did(grads)
    mixed_grad = times(z_ref, order.then(grads), first.sources(), 3 * wide, wide)
    order.did(mixed_grad)
    dense_grad = lax.dot_general(grads, order.then(mixed), by_rows, preferred_element_type=f32).astype(bf16)
    order.did(dense_grad)
    second.arrive(order)
    second.rest(order)

    third = lax.all_gather(order.then(third_own), "fsdp", axis=0, tiled=True)
    up_bias = jnp.broadcast_to(up_bias[None], (8, up_bias.shape[0]))
    up, act = up_forward(z_ref, order.then(normed), up_bias, second.sources())
    order.did(act)
    to_slots = jnp.stack([lax.rem(z - f + n, n) for f in range(n)]).astype(jnp.int32)
    down_grad = lax.dot_general(grads, order.then(act), by_rows, preferred_element_type=f32).astype(bf16)
    order.did(down_grad)
    down_grad = reorder(to_slots, down_grad, n)
    order.did(down_grad)
    down_total = lax.psum_scatter(order.then(down_grad), "fsdp", scatter_dimension=0, tiled=True)

    qkv_grad_low, qkv_bias_sum = attend_back(
        heads, low, order.then(qkv_packed), outt, lse, mixed_grad, cos_packed, sin_packed, prow, pcol, start,
        qmask, vmask, ktmask,
    )
    order.did(qkv_grad_low)
    qkv_weight = lax.dot_general(
        normed, order.then(qkv_grad_low), by_rows, preferred_element_type=f32
    ).astype(bf16)
    first_sum = Scatter(join(qkv_weight, dense_grad, n))
    order.did(*first_sum.parts)

    third_sources = [order.arrive(third)]
    first_sum.start(order)
    up_grad_low, up_bias_sum = up_backward(z_ref, grads, order.then(up), third_sources)
    order.did(up_grad_low)
    keep, send = to_features(
        z_ref, order.then(mixed), first.sources(), 3 * wide, act, third_sources, half, width
    )
    order.did(keep)
    first_sum.arrive(order)

    first_sum.start(order)
    other = swap(order.then(send), "tp", 1)
    up_weight = lax.dot_general(
        normed, order.then(up_grad_low), by_rows, preferred_element_type=f32
    ).astype(bf16)
    order.did(up_weight)
    up_weight = reorder(to_slots, order.then(up_weight), n)
    order.did(up_weight)
    up_total = lax.psum_scatter(order.then(up_weight), "fsdp", scatter_dimension=0, tiled=True)
    keep, other = order.arrive((keep, other))

    branch_sum = RowSums(order.arrive(add(keep, other)))
    branch_sum.start_direct(order)
    keep, send = to_features(
        z_ref, order.then(qkv_grad_low), first.sources(), 0, up_grad_low, second.sources(), half, width
    )
    order.did(keep)
    first_sum.arrive(order)
    down_total = order.arrive(down_total)

    first_sum.start(order)
    other = swap(order.then(send), "tp", 1)
    source = order.then(lax.dynamic_slice_in_dim(hidden_in[0], t * half, half)).astype(f32)
    centred = source - jnp.mean(source, axis=-1, keepdims=True)
    rstd = lax.rsqrt(jnp.mean(centred * centred, axis=-1, keepdims=True) + EPSILON)
    xhat = centred * rstd
    order.did(xhat)
    keep, other = order.arrive((keep, other))
    row_sum = RowSums(order.arrive(add(keep, other)))
    branch_sum.arrive_last(order)

    row_sum.start(order)
    branch = turn(order.then(branch_sum.total()))
    biases = b_dense.astype(f32) + b_fc2.astype(f32)
    result = (source + branch + biases).astype(bf16)
    order.did(result)
    row_sum.arrive(order)

    row_sum.start_last(order)
    result_other = swap(order.then(result), "tp", 1)
    first_sum.arrive(order)
    first_sum.rest(order)
    row_sum.arrive_last(order)
    up_total = order.arrive(up_total)
    first_total = order.then(first_sum.total())
    qkv_sum = lax.dot_general(
        first_total[:, : 3 * wide], place_of, by_columns, preferred_element_type=f32
    ).astype(bf16)
    both = jnp.concatenate([qkv_sum, first_total[:, 3 * wide :], down_total], axis=1)
    order.did(both)
    pieces = spread_start(both)
    normed_grad = turn(row_sum.total())
    d = order.then(normed_grad) * gain_vec
    input_grad = rstd * (
        d - jnp.mean(d, axis=-1, keepdims=True) - xhat * jnp.mean(d * xhat, axis=-1, keepdims=True)
    ) + lax.dynamic_slice_in_dim(out_grad[0], t * half, half).astype(f32)
    norm_sums = jnp.concatenate([jnp.sum(normed_grad * xhat, axis=0), jnp.sum(normed_grad, axis=0)])
    order.did(input_grad, norm_sums)
    pieces = order.arrive(pieces)
    up_pieces = spread_start(order.then(up_total))
    input_other = swap(order.then(input_grad), "tp", 1)
    c_ref = jnp.full((1,), c, jnp.int32)
    qkv_part, dense_part, down_part = place(
        c_ref, order.then(pieces), [3 * wide, wide, w_fc2.shape[1] // m]
    )
    order.did(qkv_part)
    norm_sums = order.then(norm_sums)
    up_part = place(c_ref, order.arrive(up_pieces), [w_fc1.shape[1] // m])[0]

    def in_rows(own_half, other_half):
        return jnp.concatenate(
            [jnp.where(t == 0, own_half, other_half), jnp.where(t == 0, other_half, own_half)], axis=0
        )

    result = in_rows(result, result_other)
    input_grad = in_rows(input_grad, input_other)
    def placed(vector):
        full = jnp.zeros((vector.shape[0] * m,), f32)
        return lax.dynamic_update_slice_in_dim(full, vector, c * vector.shape[0], axis=0)

    qkv_bias_grad = lax.dot_general(
        qkv_bias_sum[:1], place_of.astype(f32), by_columns,
        precision=lax.Precision.HIGHEST, preferred_element_type=f32,
    )[0]
    norm_sums = norm_sums + swap(norm_sums, "tp", 1)
    sums = everywhere(
        jnp.concatenate([norm_sums, out_sum[0], placed(qkv_bias_grad), placed(up_bias_sum[0])]), "fsdp", "ctx"
    )
    gain_grad, shift_grad, out_bias_grad = sums[:width], sums[width : 2 * width], sums[2 * width : 3 * width]
    qkv_bias_grad = sums[3 * width : 3 * width + 3 * wide * m]
    up_bias_grad = sums[3 * width + 3 * wide * m :]
    return (
        result[None],
        input_grad[None],
        gain_grad,
        shift_grad,
        qkv_part,
        qkv_bias_grad,
        dense_part,
        out_bias_grad,
        up_part,
        up_bias_grad,
        down_part,
        out_bias_grad,
    )


def solution(mesh):
    in_specs = (
        P("fsdp", "ctx", None),
        P("fsdp", "ctx", None),
        P(),
        P(),
        P("fsdp", "tp"),
        P("tp"),
        P("fsdp", "tp"),
        P(),
        P("fsdp", "tp"),
        P("tp"),
        P("fsdp", "tp"),
        P(),
        P("fsdp", None),
        P("fsdp", None),
    )
    out_specs = (
        P("fsdp", "ctx", None),
        P("fsdp", "ctx", None),
        P(),
        P(),
        P(("fsdp", "ctx"), "tp"),
        P("tp"),
        P(("fsdp", "ctx"), "tp"),
        P(),
        P(("fsdp", "ctx"), "tp"),
        P("tp"),
        P(("fsdp", "ctx"), "tp"),
        P(),
    )
    return jax.shard_map(shards, mesh=mesh, in_specs=in_specs, out_specs=out_specs, check_vma=False)
```
